32 devices in a mesh: grp: 4 (over y, x), dom: 8 (over z, core).
Axes of the slice: x: 2, y: 2, z: 4, core: 2. Of those that a mesh axis runs over, the one named last changes fastest.
Arguments:
- node_in: bfloat16 [131072, 128], P(('grp', 'dom')), may hold values from -6 to 6
- edge_in: bfloat16 [1048576, 128], P(('grp', 'dom')), may hold values from -6 to 6
- edge_slot: int32 [1048576], P(('grp', 'dom')), may hold values from 0 to 2047, as said below
- edge_receiver: int32 [1048576], P(('grp', 'dom')), may hold values from 0 to 4095, as said below
- edge_count: int32 [32], P(('grp', 'dom')), may hold values from 10922 to 32768
- request: int32 [32, 8, 256], P(('grp', 'dom')), may hold values from 0 to 4095, as said below
- node_cot: bfloat16 [131072, 128], P(('grp', 'dom')), may hold values from -6 to 6
- edge_cot: bfloat16 [1048576, 128], P(('grp', 'dom')), may hold values from -6 to 6
- edge_entry: float32 [384, 128], replicated, may hold values from -0.3125 to 0.3125
- edge_entry_mean: float32 [384, 128], replicated, may hold values from -0.015625 to 0.015625
- edge_entry_var: float32 [384, 128], replicated, may hold values from 2.2e-06 to 3.6e-05
- edge_entry_ema: float32 [384, 128], replicated, may hold values from -0.3125 to 0.3125
- node_entry: float32 [256, 128], replicated, may hold values from -0.375 to 0.375
- node_entry_mean: float32 [256, 128], replicated, may hold values from -0.015625 to 0.015625
- node_entry_var: float32 [256, 128], replicated, may hold values from 2.2e-06 to 3.6e-05
- node_entry_ema: float32 [256, 128], replicated, may hold values from -0.375 to 0.375
- inner_layers: float32 [4, 128, 128], replicated, may hold values from -0.5 to 0.5
- inner_layers_mean: float32 [4, 128, 128], replicated, may hold values from -0.015625 to 0.015625
- inner_layers_var: float32 [4, 128, 128], replicated, may hold values from 2.2e-06 to 3.6e-05
- inner_layers_ema: float32 [4, 128, 128], replicated, may hold values from -0.5 to 0.5
- vectors: float32 [10, 128], replicated
- vectors_mean: float32 [10, 128], replicated, may hold values from -0.015625 to 0.015625
- vectors_var: float32 [10, 128], replicated, may hold values from 2.2e-06 to 3.6e-05
- vectors_ema: float32 [10, 128], replicated
Outputs:
- node_out: bfloat16 [131072, 128], P(('grp', 'dom'))
- edge_out: bfloat16 [1048576, 128], P(('grp', 'dom'))
- node_grad: float32 [131072, 128], P(('grp', 'dom'))
- edge_grad: float32 [1048576, 128], P(('grp', 'dom'))
- grad_norm: float32 [], replicated
- edge_entry_mean_new: float32 [384, 128], replicated
- edge_entry_var_new: float32 [384, 128], replicated
- edge_entry_new: float32 [384, 128], replicated
- edge_entry_copy: bfloat16 [384, 128], replicated
- edge_entry_ema_new: float32 [384, 128], replicated
- node_entry_mean_new: float32 [256, 128], replicated
- node_entry_var_new: float32 [256, 128], replicated
- node_entry_new: float32 [256, 128], replicated
- node_entry_copy: bfloat16 [256, 128], replicated
- node_entry_ema_new: float32 [256, 128], replicated
- inner_layers_mean_new: float32 [4, 128, 128], replicated
- inner_layers_var_new: float32 [4, 128, 128], replicated
- inner_layers_new: float32 [4, 128, 128], replicated
- inner_layers_copy: bfloat16 [4, 128, 128], replicated
- inner_layers_ema_new: float32 [4, 128, 128], replicated
- vectors_mean_new: float32 [10, 128], replicated
- vectors_var_new: float32 [10, 128], replicated
- vectors_new: float32 [10, 128], replicated
- vectors_copy: bfloat16 [10, 128], replicated
- vectors_ema_new: float32 [10, 128], replicated
The draws below stay inside these ranges and needn't reach their ends.
Inputs may be any that keep to these rules, and one draw needn't show every extreme that they name: `edge_slot`: slot q * 256 + s names request[r, q, s] of the edge's device r; the rows of local edge block k (local rows 128 * k to 128 * k + 127, padding included) read slots k * 8 to (k + 1) * 8 - 1 only. `edge_receiver`: the rows of local edge block k (padding included) receive at local particles k * 16 to (k + 1) * 16 - 1 only. `request`: the 256 particles that a device requests from one device are distinct.
All inputs are finite; a program needn't handle non-finite values.
Results may differ from the reference program's by a relative error of at most 0.011.
Values may be sent and summed in bfloat16 or wider, within the bound.
A program may use at most 320 MiB of HBM per device.

```python
import math
import jax
import jax.numpy as jnp
from jax import lax

L = 128
NVEC = 10
STEP = 10
NODE_DEV = 4096
CAP = 256
E_DEV = 32768
RWIN = 16
SWIN = 8
NODES = 131072
EDGES = 1048576
N_DOM = 8
DEVICES = 32


def draw_edge_count(key, part):
    key = jax.random.fold_in(key, 11)
    position = jnp.arange(DEVICES, dtype=jnp.int32) % N_DOM
    jitter = jax.random.randint(key, (DEVICES,), 0, E_DEV // 8 + 1)
    rising = E_DEV // 3 + 2 * E_DEV // 3 * position // max(N_DOM - 1, 1) + jitter
    return jnp.where(position == N_DOM - 1, E_DEV, jnp.minimum(rising, E_DEV)).astype(jnp.int32)


def windowed_ids(key, width):
    places = jnp.arange(E_DEV, dtype=jnp.int32)
    base = places // 128 * width
    offsets = jax.random.randint(key, (DEVICES, E_DEV), 0, width)
    offsets = jnp.where(places[None, :] == 0, 0, offsets)
    offsets = jnp.where(places[None, :] == E_DEV - 1, width - 1, offsets)
    return (base[None, :] + offsets).reshape(-1).astype(jnp.int32)


def draw_edge_slot(key, part):
    key = jax.random.fold_in(key, 12)
    return windowed_ids(key, SWIN)


def draw_edge_receiver(key, part):
    key = jax.random.fold_in(key, 16)
    return windowed_ids(key, RWIN)


def draw_request(key, part):
    key = jax.random.fold_in(key, 13)
    key_score, key_peer = jax.random.split(key, 2)
    scores = jax.random.randint(key_score, (DEVICES, N_DOM, NODE_DEV), 0, 1 << 16) * NODE_DEV
    scores = scores + jnp.arange(NODE_DEV, dtype=jnp.int32)[None, None, :]
    chosen = jax.random.randint(key_peer, (DEVICES,), 0, N_DOM)
    marked = (jnp.arange(N_DOM, dtype=jnp.int32)[None, :, None] == chosen[:, None, None]) & (jnp.arange(NODE_DEV, dtype=jnp.int32)[None, None, :] == NODE_DEV - 1)
    scores = jnp.where(marked, -1, scores)
    order = jnp.argsort(scores, axis=2, stable=True)
    return order[:, :, :CAP].astype(jnp.int32)


def shaped_vectors(jitter_rows):
    row_ids = jnp.arange(NVEC)[:, None]
    gain_rows = (row_ids == 3) | (row_ids == 8)
    return jnp.where(gain_rows, 1.0 + jitter_rows, jitter_rows).astype(jnp.float32)


def draw_vectors(key, part):
    key = jax.random.fold_in(key, 14)
    jitter_rows = 0.3 * jax.random.normal(key, (NVEC, L), jnp.float32)
    return shaped_vectors(jitter_rows)


def draw_vectors_ema(key, part):
    key = jax.random.fold_in(key, 15)
    jitter_rows = 0.3 * jax.random.normal(key, (NVEC, L), jnp.float32)
    return shaped_vectors(jitter_rows)


def levels(stream_key, extent, cuts, low, top_value):
    gain, own = 1.0, jax.random.fold_in(stream_key, 6)
    for axis_at, blocks in cuts:
        draws = jnp.exp(jax.random.uniform(jax.random.fold_in(own, axis_at), (blocks,), jnp.float32, low / len(cuts), top_value / len(cuts)))
        gain = gain * jnp.repeat(draws, extent[axis_at] // blocks).reshape([-1 if axis == axis_at else 1 for axis in range(len(extent))])
    return gain


def scatter_about(key, shape, deviation, limit, pieces=(), kind=jnp.bfloat16):
    values = deviation * jax.random.normal(key, shape, jnp.float32)
    if pieces:
        values = values * levels(key, shape, pieces, -0.22, 0.18)
    return jnp.clip(values, -limit, limit).astype(kind)


def setup_inputs(seed: int = 0) -> dict:
    key_list = jax.random.split(jax.random.key(seed), 25)
    node_in = scatter_about(key_list[0], (NODES, L), 1.0, 6.0, ((0, 32),))
    edge_in = scatter_about(key_list[1], (EDGES, L), 1.0, 6.0, ((0, 32),))
    edge_slot = draw_edge_slot(jax.random.fold_in(key_list[24], 71), 0)
    edge_receiver = draw_edge_receiver(jax.random.fold_in(key_list[24], 71), 0)
    edge_count = draw_edge_count(jax.random.fold_in(key_list[24], 71), 0)
    request = draw_request(jax.random.fold_in(key_list[24], 71), 0)
    node_cot = scatter_about(key_list[6], (NODES, L), 1.0, 6.0, ((0, 32),))
    edge_cot = scatter_about(key_list[7], (EDGES, L), 1.0, 6.0, ((0, 32),))
    edge_entry = scatter_about(key_list[8], (3 * L, L), (3 * L) ** -0.5, 0.3125, (), jnp.float32)
    edge_entry_mean = scatter_about(key_list[9], (3 * L, L), 0.0026, 0.015625, (), jnp.float32)
    edge_entry_var = jnp.clip(jnp.exp(jax.random.uniform(key_list[10], (3 * L, L), jnp.float32, math.log(2.1999999262334313e-06), math.log(3.600000127335079e-05))), 2.1999999262334313e-06, 3.600000127335079e-05)
    edge_entry_ema = scatter_about(key_list[11], (3 * L, L), (3 * L) ** -0.5, 0.3125, (), jnp.float32)
    node_entry = scatter_about(key_list[12], (2 * L, L), (2 * L) ** -0.5, 0.375, (), jnp.float32)
    node_entry_mean = scatter_about(key_list[13], (2 * L, L), 0.0026, 0.015625, (), jnp.float32)
    node_entry_var = jnp.clip(jnp.exp(jax.random.uniform(key_list[14], (2 * L, L), jnp.float32, math.log(2.1999999262334313e-06), math.log(3.600000127335079e-05))), 2.1999999262334313e-06, 3.600000127335079e-05)
    node_entry_ema = scatter_about(key_list[15], (2 * L, L), (2 * L) ** -0.5, 0.375, (), jnp.float32)
    inner_layers = scatter_about(key_list[16], (4, L, L), L ** -0.5, 0.5, (), jnp.float32)
    inner_layers_mean = scatter_about(key_list[17], (4, L, L), 0.0026, 0.015625, (), jnp.float32)
    inner_layers_var = jnp.clip(jnp.exp(jax.random.uniform(key_list[18], (4, L, L), jnp.float32, math.log(2.1999999262334313e-06), math.log(3.600000127335079e-05))), 2.1999999262334313e-06, 3.600000127335079e-05)
    inner_layers_ema = scatter_about(key_list[19], (4, L, L), L ** -0.5, 0.5, (), jnp.float32)
    vectors = draw_vectors(jax.random.fold_in(key_list[24], 71), 0)
    vectors_mean = scatter_about(key_list[21], (NVEC, L), 0.0026, 0.015625, (), jnp.float32)
    vectors_var = jnp.clip(jnp.exp(jax.random.uniform(key_list[22], (NVEC, L), jnp.float32, math.log(2.1999999262334313e-06), math.log(3.600000127335079e-05))), 2.1999999262334313e-06, 3.600000127335079e-05)
    vectors_ema = draw_vectors_ema(jax.random.fold_in(key_list[24], 71), 0)
    return {"node_in": node_in, "edge_in": edge_in, "edge_slot": edge_slot, "edge_receiver": edge_receiver, "edge_count": edge_count, "request": request, "node_cot": node_cot, "edge_cot": edge_cot, "edge_entry": edge_entry, "edge_entry_mean": edge_entry_mean, "edge_entry_var": edge_entry_var, "edge_entry_ema": edge_entry_ema, "node_entry": node_entry, "node_entry_mean": node_entry_mean, "node_entry_var": node_entry_var, "node_entry_ema": node_entry_ema, "inner_layers": inner_layers, "inner_layers_mean": inner_layers_mean, "inner_layers_var": inner_layers_var, "inner_layers_ema": inner_layers_ema, "vectors": vectors, "vectors_mean": vectors_mean, "vectors_var": vectors_var, "vectors_ema": vectors_ema}


@jax.custom_vjp
def low(v):
    return lax.optimization_barrier(v.astype(jnp.bfloat16)).astype(jnp.float32)

@jax.custom_vjp
def low_back(v):
    return v

def low_keep(v):
    return (low(v), None)

def low_pass(kept, grad):
    return (grad,)

def back_keep(v):
    return (v, None)

def back_low(kept, grad):
    return (low(grad),)
low.defvjp(low_keep, low_pass)
low_back.defvjp(back_keep, back_low)
eps_norm = 1e-05
beta_one = 0.5
beta_two = 0.6
learn_rate = 0.08
decay_rate = 0.01
adam_eps = 1e-08
ema_keep = 0.9
clip_level = 1.0

def high_dot(operand, weights):
    return jnp.dot(operand, weights, precision=lax.Precision.HIGHEST, preferred_element_type=jnp.float32)

def layer_norm(values):
    center = values - lax.optimization_barrier(jnp.mean(values, axis=1, keepdims=True))
    inverse = lax.rsqrt(lax.optimization_barrier(jnp.mean(center * center, axis=1, keepdims=True)) + eps_norm)
    return center * inverse

def adamw_step(master, moment_mean, moment_var, average, gradient, factor):
    clipped = gradient * factor
    mean_new = beta_one * moment_mean + (1.0 - beta_one) * clipped
    var_new = beta_two * moment_var + (1.0 - beta_two) * clipped * clipped
    mean_hat = mean_new / (1.0 - beta_one ** STEP)
    var_hat = var_new / (1.0 - beta_two ** STEP)
    updated = master - learn_rate * (mean_hat / (jnp.sqrt(var_hat) + adam_eps) + decay_rate * master)
    return (mean_new, var_new, updated, updated.astype(jnp.bfloat16), ema_keep * average + (1.0 - ema_keep) * updated)

def reference(node_in, edge_in, edge_slot, edge_receiver, edge_count, request, node_cot, edge_cot, edge_entry, edge_entry_mean, edge_entry_var, edge_entry_ema, node_entry, node_entry_mean, node_entry_var, node_entry_ema, inner_layers, inner_layers_mean, inner_layers_var, inner_layers_ema, vectors, vectors_mean, vectors_var, vectors_ema):
    device_ids = jnp.arange(DEVICES, dtype=jnp.int32)
    group_base = device_ids // N_DOM * N_DOM
    owners = group_base[:, None, None] + jnp.arange(N_DOM, dtype=jnp.int32)[None, :, None]
    sender_table = (owners * NODE_DEV + request).reshape(-1).astype(jnp.int32)
    edge_device = jnp.repeat(device_ids, E_DEV)
    slot_global = (edge_device * (N_DOM * CAP) + edge_slot).astype(jnp.int32)
    receiver_global = (edge_device * NODE_DEV + edge_receiver).astype(jnp.int32)
    local_place = jnp.tile(jnp.arange(E_DEV, dtype=jnp.int32), DEVICES)
    live = (local_place < jnp.take(edge_count, edge_device)).astype(jnp.float32)[:, None]

    def forward(node_f, edge_f, edge_w, node_w, inner_w, vector_w):
        slot_rows = low_back(jnp.take(node_f, sender_table, axis=0))
        sender_rows = jnp.take(slot_rows, slot_global, axis=0)
        receiver_rows = jnp.take(node_f, receiver_global, axis=0)
        edge_low = low(edge_w)
        node_low = low(node_w)
        inner_low = low(inner_w)
        pre_one = low_back(high_dot(edge_f, edge_low[:L]) + high_dot(sender_rows, edge_low[L:2 * L]) + high_dot(receiver_rows, edge_low[2 * L:]) + vector_w[0])
        act_one = low(jax.nn.gelu(pre_one))
        pre_two = low_back(high_dot(act_one, inner_low[0]) + vector_w[1])
        act_two = low(jax.nn.gelu(pre_two))
        pre_three = low_back(high_dot(act_two, inner_low[1]) + vector_w[2])
        message = live * (layer_norm(pre_three) * vector_w[3] + vector_w[4])
        edge_result = edge_f + message
        gathered = low(jax.ops.segment_sum(message, receiver_global, num_segments=DEVICES * NODE_DEV))
        node_one = low_back(high_dot(node_f, node_low[:L]) + high_dot(gathered, node_low[L:]) + vector_w[5])
        node_act_one = low(jax.nn.gelu(node_one))
        node_two = low_back(high_dot(node_act_one, inner_low[2]) + vector_w[6])
        node_act_two = low(jax.nn.gelu(node_two))
        node_three = low_back(high_dot(node_act_two, inner_low[3]) + vector_w[7])
        return (node_f + layer_norm(node_three) * vector_w[8] + vector_w[9], edge_result)
    node_f = node_in.astype(jnp.float32)
    edge_f = edge_in.astype(jnp.float32)
    outputs, pullback = jax.vjp(forward, node_f, edge_f, edge_entry, node_entry, inner_layers, vectors)
    grads = pullback((node_cot.astype(jnp.float32), edge_cot.astype(jnp.float32)))
    weight_grads = grads[2:]
    total = sum((jnp.sum(item * item) for item in weight_grads))
    grad_norm = jnp.sqrt(total)
    factor = clip_level / jnp.maximum(grad_norm, clip_level)
    first_set = adamw_step(edge_entry, edge_entry_mean, edge_entry_var, edge_entry_ema, weight_grads[0], factor)
    second_set = adamw_step(node_entry, node_entry_mean, node_entry_var, node_entry_ema, weight_grads[1], factor)
    third_set = adamw_step(inner_layers, inner_layers_mean, inner_layers_var, inner_layers_ema, weight_grads[2], factor)
    fourth_set = adamw_step(vectors, vectors_mean, vectors_var, vectors_ema, weight_grads[3], factor)
    return (outputs[0].astype(jnp.bfloat16), outputs[1].astype(jnp.bfloat16), grads[0], grads[1], grad_norm, first_set[0], first_set[1], first_set[2], first_set[3], first_set[4], second_set[0], second_set[1], second_set[2], second_set[3], second_set[4], third_set[0], third_set[1], third_set[2], third_set[3], third_set[4], fourth_set[0], fourth_set[1], fourth_set[2], fourth_set[3], fourth_set[4])
```

```python
import functools
import math

import jax
import jax.numpy as jnp
from jax import lax
from jax.experimental import pallas as pl
from jax.experimental.pallas import tpu as pltpu
from jax.sharding import PartitionSpec as P

STEP = 10

eps_norm = 1e-05
beta_one = 0.5
beta_two = 0.6
learn_rate = 0.08
decay_rate = 0.01
adam_eps = 1e-08
ema_keep = 0.9
clip_level = 1.0

gelu_in = math.sqrt(2.0 / math.pi)
gelu_cube = gelu_in * 0.044715

low = jnp.bfloat16
high = jnp.float32

GAP = 4
VMEM = 60 * 1024 * 1024
PAIRS = 8


def dot(operand, weights):
    return jnp.dot(operand, weights, preferred_element_type=high)


def dot_nt(operand, weights):
    return lax.dot_general(
        operand, weights, (((1,), (1,)), ((), ())), preferred_element_type=high
    )


def dot_tn(operand, weights):
    return lax.dot_general(
        operand, weights, (((0,), (0,)), ((), ())), preferred_element_type=high
    )


def gelu_pair(x):
    square = x * x
    u = x * (gelu_in + gelu_cube * square)
    s = 0.5 + 0.5 * jnp.tanh(u)
    value = x * s
    slope = s + (value - value * s) * (2.0 * gelu_in + (6.0 * gelu_cube) * square)
    return value, slope


def fold_rows(values):
    return jnp.sum(values.reshape(values.shape[0] // 8, 8, values.shape[1]), axis=0)


def emit(pairs, per_group, forward, middle, backward, end):
    groups = pairs // per_group
    streams = {"forward": forward, "middle": middle, "backward": backward, "end": end}
    started = dict.fromkeys(streams, 0)
    last = dict.fromkeys(streams, -GAP)
    active, done, now = [], set(), 0

    def ready(name, k):
        if name == "middle":
            return all(("forward", k * per_group + j) in done for j in range(per_group))
        if name == "end":
            return all(("backward", k * per_group + j) in done for j in range(per_group))
        return name == "forward" or ("middle", k // per_group) in done

    while len(done) < 2 * pairs + 2 * groups:
        for name in streams:
            k = started[name]
            count = pairs if name in ("forward", "backward") else groups
            if k < count and now - last[name] >= GAP and ready(name, k):
                active.append(((name, k), streams[name](k)))
                started[name], last[name] = k + 1, now
        for item in list(active):
            try:
                next(item[1])
            except StopIteration:
                active.remove(item)
                done.add(item[0])
        now += 1


class Sizes:
    def __init__(self, edges, nodes, slots, devices):
        self.edges, self.nodes, self.slots = edges, nodes, slots
        blocks = edges // 128
        self.rwin = nodes // blocks
        self.swin = slots // blocks
        self.sub = 4
        while self.sub * (self.rwin + self.swin) > 128:
            self.sub //= 2
        self.chunk = self.sub * 128
        self.chunk_slots = self.sub * self.swin
        self.chunk_nodes = self.sub * self.rwin
        self.pair_nodes, self.pair_slots = 2 * self.chunk_nodes, 2 * self.chunk_slots
        self.per_group = 4
        self.pairs = PAIRS
        self.group_nodes = self.per_group * self.pair_nodes
        self.group_slots = self.per_group * self.pair_slots
        self.tile = self.pairs * 2 * self.chunk
        self.tile_chunks = 2 * self.pairs
        self.tile_nodes = self.pairs * self.pair_nodes
        self.tile_slots = self.pairs * self.pair_slots
        self.steps = edges // self.tile
        self.grad_rows = -(-1162 // (16 * devices)) * 16 * devices


def diagonal(first, second):
    zero_a = jnp.zeros((first.shape[0], second.shape[1]), first.dtype)
    zero_b = jnp.zeros((second.shape[0], first.shape[1]), first.dtype)
    return jnp.concatenate(
        [
            jnp.concatenate([first, zero_a], axis=1),
            jnp.concatenate([zero_b, second], axis=1),
        ],
        axis=0,
    )


def twice(row):
    return jnp.concatenate([row, row], axis=1)


def layer_kernel(
    z,
    count_ref,
    slot_ids_ref,
    recv_ids_ref,
    edge_in_ref,
    edge_cot_ref,
    node_in_ref,
    node_cot_ref,
    slot_ref,
    edge_entry_ref,
    node_entry_ref,
    inner_ref,
    vec_ref,
    node_out_ref,
    edge_out_ref,
    node_grad_ref,
    edge_grad_ref,
    slot_grad_ref,
    grads_ref,
    pick_s,
    pick_t,
    act_one_s,
    act_two_s,
    slope_one_s,
    slope_two_s,
    normed_s,
    inverse_s,
    gathered_s,
    table_s,
    slot_pre_s,
    node_pre_s,
    slot_sum_s,
    recv_sum_s,
    sums_s,
    wide_s,
    below_s,
):
    step = pl.program_id(0)
    chunk, cn, cs = z.chunk, z.chunk_nodes, z.chunk_slots
    pad = 128 - cn - cs
    vec = [vec_ref[pl.ds(k, 1), :] for k in range(10)]

    @pl.when(step == 0)
    def _():
        grads_ref[...] = jnp.zeros_like(grads_ref)
        sums_s[...] = jnp.zeros_like(sums_s)
        first, second = inner_ref[0].astype(low), inner_ref[1].astype(low)
        wide_s[0] = diagonal(first, first)
        middle = second.astype(high)
        middle = (middle - jnp.mean(middle, axis=1, keepdims=True)).astype(low)
        wide_s[1] = diagonal(middle, middle)
        for k, weights in ((2, inner_ref[0]), (3, inner_ref[1]), (4, edge_entry_ref[0:128, :])):
            weights = weights.T.astype(low)
            wide_s[k] = diagonal(weights, weights)
        part = jnp.full((128, 128), 1.0 / 128.0, low)
        wide_s[5] = diagonal(part, part)
        row = lax.broadcasted_iota(jnp.int32, (128, 128), 0)
        column = lax.broadcasted_iota(jnp.int32, (128, 128), 1)
        gain = jnp.broadcast_to(vec[3] * (1.0 / 128.0), (128, 128)).T.astype(low)
        wide_s[6] = diagonal(gain, gain)
        below_s[:, :128] = jnp.where(row == column, 1.0, 0.0).astype(low)
        below_s[:, 128:] = gain

    edge_low = edge_entry_ref[...].astype(low)
    node_low = node_entry_ref[...].astype(low)
    inner_low = [None, None, inner_ref[2].astype(low), inner_ref[3].astype(low)]
    w_edge, w_slot, w_recv = edge_low[:128], edge_low[128:256], edge_low[256:]
    bias_three = vec[2] - jnp.mean(vec[2], axis=1, keepdims=True)
    gain_part = below_s[:, 128:]
    row_ids = lax.broadcasted_iota(jnp.int32, (chunk, 128), 0)
    slot_pre_s[...] = dot(slot_ref[...], w_slot).astype(low)
    node_pre_s[...] = (dot(node_in_ref[...], w_recv) + vec[0]).astype(low)

    def live_rows(index):
        return row_ids < count_ref[0] - (step * z.tile + index * chunk)

    def sides(wide):
        return wide[:, :128], wide[:, 128:]

    def chunk_rows(index):
        return pl.ds(index * chunk, chunk)

    def hot_columns(index):
        columns = []
        for k in range(z.sub):
            block = index * z.sub + k
            number = step * (z.tile // 128) + block
            pieces = []
            for ref, width, count in ((slot_ids_ref, z.swin, cs), (recv_ids_ref, z.rwin, cn)):
                ids = ref[pl.ds(block, 1), :] - number * width
                band = lax.broadcasted_iota(jnp.int32, (width, 128), 0) == ids
                above, below = k * width, count - (k + 1) * width
                if above:
                    pieces.append(jnp.zeros((above, 128), high))
                pieces.append(jnp.where(band, 1.0, 0.0))
                if below:
                    pieces.append(jnp.zeros((below, 128), high))
            if pad:
                pieces.append(jnp.zeros((pad, 128), high))
            columns.append(jnp.concatenate(pieces, axis=0).astype(low))
        return jnp.concatenate(columns, axis=1)

    def edge_forward(pair):
        wide_rows = chunk_rows(pair)
        indices = (2 * pair, 2 * pair + 1)
        pres = []
        for side, index in enumerate(indices):
            hot_t = hot_columns(index)
            hot = hot_t.T
            pick_t[index] = hot_t
            pick_s[chunk_rows(index), :] = hot
            tables = [
                w_edge,
                slot_pre_s[pl.ds(index * cs, cs), :],
                node_pre_s[pl.ds(index * cn, cn), :],
            ]
            if pad:
                tables.append(jnp.zeros((pad, 128), low))
            rows = edge_in_ref[chunk_rows(index), :]
            pres.append(
                dot(jnp.concatenate([rows, hot], axis=1), jnp.concatenate(tables, axis=0)).astype(low)
            )
            yield
        act_one, slope = gelu_pair(jnp.concatenate(pres, axis=1))
        act_one_s[wide_rows, :] = act_one
        slope_one_s[wide_rows, :] = slope
        yield
        pre_two = (dot(act_one, wide_s[0]) + twice(vec[1])).astype(low)
        yield
        act_two, slope = gelu_pair(pre_two)
        act_two_s[wide_rows, :] = act_two
        slope_two_s[wide_rows, :] = slope
        yield
        center = dot(act_two, wide_s[1]) + twice(bias_three)
        square = (center * center).astype(low)
        yield
        inverse = lax.rsqrt(dot(square, wide_s[5]) + eps_norm)
        yield
        messages = []
        for index, center, inverse in zip(indices, sides(center), sides(inverse)):
            live = live_rows(index)
            inverse = jnp.where(live, inverse, 0.0)
            normed = center * inverse
            normed_s[chunk_rows(index), :] = normed
            inverse_s[chunk_rows(index), :] = inverse
            message = jnp.where(live, normed * vec[3] + vec[4], 0.0)
            rows = edge_in_ref[chunk_rows(index), :]
            edge_out_ref[chunk_rows(index), :] = (rows.astype(high) + message).astype(low)
            messages.append(message.astype(low))
        yield
        hots = [pick_t[index, cs : cs + cn, :] for index in indices]
        total = dot(jnp.concatenate(hots, axis=0), jnp.concatenate(messages, axis=1)).astype(low)
        gathered_s[pl.ds(indices[0] * cn, cn), :] = total[:cn, :128]
        gathered_s[pl.ds(indices[1] * cn, cn), :] = total[cn:, 128:]
        yield

    def node_phase(group):
        rows = pl.ds(group * z.group_nodes, z.group_nodes)
        node_rows = node_in_ref[rows, :]
        entry = jnp.concatenate([node_rows, gathered_s[rows, :]], axis=1)
        node_one = (dot(entry, node_low) + vec[5]).astype(low)
        yield
        act_one, slope_one = gelu_pair(node_one)
        yield
        node_two = (dot(act_one, inner_low[2]) + vec[6]).astype(low)
        yield
        act_two, slope_two = gelu_pair(node_two)
        yield
        node_three = dot(act_two, inner_low[3]) + vec[7]
        yield
        center = node_three - jnp.mean(node_three, axis=1, keepdims=True)
        inverse = lax.rsqrt(jnp.mean(center * center, axis=1, keepdims=True) + eps_norm)
        normed = center * inverse
        node_out_ref[rows, :] = (node_rows.astype(high) + normed * vec[8] + vec[9]).astype(low)
        yield
        upstream = node_cot_ref[rows, :].astype(high)
        sums_s[8] += fold_rows(upstream * normed)
        sums_s[9] += fold_rows(upstream)
        upper = upstream * vec[8]
        mean_plain = jnp.mean(upper, axis=1, keepdims=True)
        mean_cross = jnp.mean(upper * normed, axis=1, keepdims=True)
        d_three = inverse * (upper - mean_plain - normed * mean_cross)
        sums_s[7] += fold_rows(d_three)
        d_three = d_three.astype(low)
        yield
        back = dot_nt(d_three, inner_low[3])
        yield
        d_two = back * slope_two.astype(high)
        sums_s[6] += fold_rows(d_two)
        d_two = d_two.astype(low)
        yield
        back = dot_nt(d_two, inner_low[2])
        yield
        d_one = back * slope_one.astype(high)
        sums_s[5] += fold_rows(d_one)
        d_one = d_one.astype(low)
        yield
        back = dot_nt(d_one, node_low)
        node_grad_ref[rows, :] = upstream + back[:, :128]
        arrived = back[:, 128:].astype(low)
        yield
        table_s[rows, :128] = arrived
        table_s[rows, 128:] = dot(arrived, gain_part).astype(low)
        yield
        grads_ref[384:640, :] += dot_tn(entry, d_one)
        grads_ref[896:1024, :] += dot_tn(act_one, d_two)
        grads_ref[1024:1152, :] += dot_tn(act_two, d_three)
        yield

    def edge_backward(pair):
        wide_rows = chunk_rows(pair)
        indices = (2 * pair, 2 * pair + 1)
        upstreams, plains, crosses = [], [], []
        for index in indices:
            tables = [
                jnp.zeros((cs, 256), low),
                table_s[pl.ds(index * cn, cn), :],
            ]
            if pad:
                tables.append(jnp.zeros((pad, 256), low))
            tables.append(below_s[...])
            entry = jnp.concatenate(
                [pick_s[chunk_rows(index), :], edge_cot_ref[chunk_rows(index), :]], axis=1
            )
            upstream, plain = sides(dot(entry, jnp.concatenate(tables, axis=0)))
            upstreams.append(upstream)
            plains.append(plain)
            yield
        for index, upstream in zip(indices, upstreams):
            cross = upstream * normed_s[chunk_rows(index), :]
            sums_s[3] += fold_rows(cross)
            sums_s[4] += fold_rows(jnp.where(live_rows(index), upstream, 0.0))
            crosses.append(cross.astype(low))
        yield
        means = dot(jnp.concatenate(crosses, axis=1), wide_s[6])
        yield
        threes = []
        for index, upstream, plain, cross in zip(indices, upstreams, plains, sides(means)):
            normed = normed_s[chunk_rows(index), :]
            d_three = inverse_s[chunk_rows(index), :] * (
                upstream * vec[3] - plain - normed * cross
            )
            threes.append(d_three.astype(low))
        d_three = jnp.concatenate(threes, axis=1)
        yield
        d_two = dot(d_three, wide_s[3]).astype(low) * slope_two_s[wide_rows, :]
        yield
        d_one = dot(d_two, wide_s[2]).astype(low) * slope_one_s[wide_rows, :]
        yield
        for index, back in zip(indices, sides(dot(d_one, wide_s[4]))):
            edge_grad_ref[chunk_rows(index), :] = (
                edge_cot_ref[chunk_rows(index), :].astype(high) + back
            )
        yield
        ones = jnp.ones((16, chunk), low)
        entry = [edge_in_ref[chunk_rows(index), :].T for index in indices]
        hots = [pick_t[index, : cs + cn, :] for index in indices]
        total = dot(jnp.concatenate(entry + hots, axis=0), d_one)
        grads_ref[0:128, :] += total[:128, :128] + total[128:256, 128:]
        first = total[256 : 256 + cs + cn, :128]
        second = total[256 + cs + cn :, 128:]
        yield
        node_rows = pl.ds(pair * z.pair_nodes, z.pair_nodes)
        slot_rows = pl.ds(pair * z.pair_slots, z.pair_slots)
        slot_sum_s[slot_rows, :] = jnp.concatenate([first[:cs], second[:cs]], axis=0).astype(low)
        recv_sum = jnp.concatenate([first[cs:], second[cs:]], axis=0)
        sums_s[0] += fold_rows(recv_sum)
        recv_sum_s[node_rows, :] = recv_sum.astype(low)
        yield
        for k, act_s, gradient in ((1, act_one_s, d_two), (2, act_two_s, d_three)):
            total = dot(jnp.concatenate([act_s[wide_rows, :].T, ones], axis=0), gradient)
            grads_ref[pl.ds(512 + 128 * k, 128), :] += total[:128, :128] + total[128:256, 128:]
            sums_s[k] += (total[256:264, :128] + total[256:264, 128:]) * 0.125
            yield

    def group_end(group):
        node_rows = pl.ds(group * z.group_nodes, z.group_nodes)
        slot_rows = pl.ds(group * z.group_slots, z.group_slots)
        slot_grad_ref[slot_rows, :] = dot_nt(slot_sum_s[slot_rows, :], w_slot).astype(low)
        node_grad_ref[node_rows, :] += dot_nt(recv_sum_s[node_rows, :], w_recv)
        yield
        grads_ref[128:256, :] += dot_tn(slot_ref[slot_rows, :], slot_sum_s[slot_rows, :])
        grads_ref[256:384, :] += dot_tn(node_in_ref[node_rows, :], recv_sum_s[node_rows, :])
        yield

    emit(z.pairs, z.per_group, edge_forward, node_phase, edge_backward, group_end)

    @pl.when(step == z.steps - 1)
    def _():
        grads_ref[1152:1162, :] = jnp.sum(sums_s[...], axis=1)


def layer_call(z, count, slot_ids, recv_ids, edge_in, edge_cot, node_in, node_cot, slot_rows, weights):
    def rows_spec(rows):
        return pl.BlockSpec((rows, 128), lambda i: (i, 0))

    def whole(array):
        return pl.BlockSpec(array.shape, lambda i: (0,) * array.ndim)

    return pl.pallas_call(
        functools.partial(layer_kernel, z),
        grid=(z.steps,),
        in_specs=[
            pl.BlockSpec(memory_space=pltpu.SMEM),
            rows_spec(z.tile // 128),
            rows_spec(z.tile // 128),
            rows_spec(z.tile),
            rows_spec(z.tile),
            rows_spec(z.tile_nodes),
            rows_spec(z.tile_nodes),
            rows_spec(z.tile_slots),
        ]
        + [whole(w) for w in weights],
        out_specs=[
            rows_spec(z.tile_nodes),
            rows_spec(z.tile),
            rows_spec(z.tile_nodes),
            rows_spec(z.tile),
            rows_spec(z.tile_slots),
            pl.BlockSpec((z.grad_rows, 128), lambda i: (0, 0)),
        ],
        out_shape=[
            jax.ShapeDtypeStruct((z.nodes, 128), low),
            jax.ShapeDtypeStruct((z.edges, 128), low),
            jax.ShapeDtypeStruct((z.nodes, 128), high),
            jax.ShapeDtypeStruct((z.edges, 128), high),
            jax.ShapeDtypeStruct((z.slots, 128), low),
            jax.ShapeDtypeStruct((z.grad_rows, 128), high),
        ],
        scratch_shapes=[
            pltpu.VMEM((z.tile, 128), low),
            pltpu.VMEM((z.tile_chunks, 128, z.chunk), low),
            pltpu.VMEM((z.tile // 2, 256), low),
            pltpu.VMEM((z.tile // 2, 256), low),
            pltpu.VMEM((z.tile // 2, 256), low),
            pltpu.VMEM((z.tile // 2, 256), low),
            pltpu.VMEM((z.tile, 128), high),
            pltpu.VMEM((z.tile, 128), high),
            pltpu.VMEM((z.tile_nodes, 128), low),
            pltpu.VMEM((z.tile_nodes, 256), low),
            pltpu.VMEM((z.tile_slots, 128), low),
            pltpu.VMEM((z.tile_nodes, 128), low),
            pltpu.VMEM((z.tile_slots, 128), low),
            pltpu.VMEM((z.tile_nodes, 128), low),
            pltpu.VMEM((10, 8, 128), high),
            pltpu.VMEM((7, 256, 256), low),
            pltpu.VMEM((128, 256), low),
        ],
        compiler_params=pltpu.CompilerParams(
            dimension_semantics=("arbitrary",), vmem_limit_bytes=VMEM
        ),
        name="layer",
    )(count, slot_ids, recv_ids, edge_in, edge_cot, node_in, node_cot, slot_rows, *weights)


def signal(semaphore, where):
    pl.semaphore_signal(semaphore, inc=1, device_id=where, device_id_type=pl.DeviceIdType.MESH)


def send(source, target, send_sem, recv_sem, where):
    copy = pltpu.make_async_remote_copy(
        src_ref=source,
        dst_ref=target,
        send_sem=send_sem,
        recv_sem=recv_sem,
        device_id=where,
        device_id_type=pl.DeviceIdType.MESH,
    )
    copy.start()
    return copy


def fetch_kernel(
    peers,
    unroll,
    request_ref,
    node_ref,
    rows_ref,
    asked_ref,
    wanted_v,
    asked_v,
    node_v,
    node_s,
    picked_s,
    out_s,
    ask_send,
    ask_recv,
    row_send,
    row_recv,
    load_sem,
):
    me = lax.axis_index("dom")
    slots = picked_s.shape[0]
    barrier = pltpu.get_barrier_semaphore()
    for k in range(1, peers):
        signal(barrier, {"dom": lax.rem(me + k, peers)})
    loads = [
        pltpu.make_async_copy(request_ref, wanted_v, load_sem.at[0]),
        pltpu.make_async_copy(node_ref, node_v, load_sem.at[1]),
    ]
    for load in loads:
        load.start()
    loads[0].wait()
    for k in range(peers):
        asked_v[k] = wanted_v[pl.ds(k, 1), :]
    loads[1].wait()
    node_s[...] = node_v[...].astype(high)
    pl.semaphore_wait(barrier, peers - 1)
    shifts = [peers // 2 + (k // 2) * (1 - 2 * (k % 2)) for k in range(1, peers)]
    asks = [
        send(
            asked_v.at[lax.rem(me + k, peers)],
            asked_v.at[peers + me],
            ask_send.at[k],
            ask_recv.at[k],
            {"dom": lax.rem(me + k, peers)},
        )
        for k in shifts
    ]
    asked_v[peers + me] = asked_v[me]
    for ask in asks:
        ask.wait_recv()
    local = pltpu.make_async_copy(asked_v.at[pl.ds(peers, peers)], asked_ref, load_sem.at[0])
    local.start()
    local.wait()
    sends = []
    for k in shifts + [0]:
        other = lax.rem(me + (peers - k), peers)

        @pl.loop(0, slots // unroll)
        def _(group):
            for place in range(unroll):
                row = group * unroll + place
                index = asked_ref[other, 0, row]
                picked_s[pl.ds(row, 1), :] = node_s[pl.ds(index, 1), :]

        out_s[other] = picked_s[...].astype(low)
        if k:
            sends.append(
                send(
                    out_s.at[other],
                    rows_ref.at[me],
                    row_send.at[k],
                    row_recv.at[k],
                    {"dom": other},
                )
            )
    local = pltpu.make_async_copy(out_s.at[me], rows_ref.at[me], load_sem.at[0])
    local.start()
    for copy in asks:
        copy.wait_send()
    local.wait()
    for copy in sends:
        copy.wait()


def fetch_call(peers, request, node_in):
    slots = request.shape[2]
    dma = pltpu.SemaphoreType.DMA
    hbm = pl.BlockSpec(memory_space=pltpu.HBM)
    return pl.pallas_call(
        functools.partial(fetch_kernel, peers, 32),
        in_specs=[hbm, hbm],
        out_specs=[hbm, pl.BlockSpec(memory_space=pltpu.SMEM)],
        out_shape=[
            jax.ShapeDtypeStruct((peers, slots, 128), low),
            jax.ShapeDtypeStruct((peers, 1, slots), jnp.int32),
        ],
        scratch_shapes=[
            pltpu.VMEM((peers, slots), jnp.int32),
            pltpu.VMEM((2 * peers, 1, slots), jnp.int32),
            pltpu.VMEM(node_in.shape, low),
            pltpu.VMEM(node_in.shape, high),
            pltpu.VMEM((slots, 128), high),
            pltpu.VMEM((peers, slots, 128), low),
            dma((peers,)),
            dma((peers,)),
            dma((peers,)),
            dma((peers,)),
            dma((2,)),
        ],
        compiler_params=pltpu.CompilerParams(
            collective_id=0, has_side_effects=True, vmem_limit_bytes=VMEM
        ),
        name="fetch",
    )(request.reshape(peers, slots), node_in)


def reduce_kernel(
    groups,
    peers,
    grads_ref,
    slot_grad_ref,
    sum_ref,
    back_ref,
    grads_s,
    all_s,
    half_out,
    half_in,
    half_sum,
    quarter_out,
    quarter_in,
    quarter_sum,
    piece_out,
    piece_in,
    back_send,
    back_recv,
    half_send,
    half_recv,
    quarter_send,
    quarter_recv,
    piece_send,
    piece_recv,
    load_sem,
):
    grp, dom = lax.axis_index("grp"), lax.axis_index("dom")
    core, level = lax.rem(dom, 2), lax.div(dom, 2)
    levels = peers // 2
    half, quarter, piece = half_sum.shape[0], quarter_sum.shape[0], piece_out.shape[1]
    barrier = pltpu.get_barrier_semaphore()
    for k in range(1, peers):
        signal(barrier, {"dom": lax.rem(dom + k, peers)})
    for k in range(1, groups):
        signal(barrier, {"grp": lax.rem(grp + k, groups)})
    twin = {"dom": 2 * level + 1 - core}
    loads = [
        pltpu.make_async_copy(
            grads_ref.at[pl.ds(first, half), :], grads_s.at[pl.ds(first, half), :], load_sem.at[k]
        )
        for k, first in enumerate(((1 - core) * half, core * half))
    ]
    loads.append(
        pltpu.make_async_copy(slot_grad_ref.at[dom], back_ref.at[dom], load_sem.at[2])
    )
    for load in loads:
        load.start()
    loads[0].wait()
    half_out[...] = grads_s[pl.ds((1 - core) * half, half), :].astype(low)
    loads[1].wait()
    pl.semaphore_wait(barrier, peers - 1 + groups - 1)

    sends = [send(half_out, half_in, half_send.at[0], half_recv.at[0], twin)]

    def give_back(k):
        other = lax.rem(dom + k, peers)
        return send(
            slot_grad_ref.at[other],
            back_ref.at[dom],
            back_send.at[k],
            back_recv.at[k],
            {"dom": other},
        )

    early = [k for k in range(1, peers) if 2 * k == peers or (2 * k < peers and k % 2)]
    backs = [give_back(k) for k in early]
    sends[0].wait_recv()
    half_sum[...] = grads_s[pl.ds(core * half, half), :] + half_in[...].astype(high)

    copies = []
    for k in range(1, groups):
        other = lax.rem(grp + k, groups)
        quarter_out[k] = half_sum[pl.ds(other * quarter, quarter), :].astype(low)
        copies.append(
            send(
                quarter_out.at[k],
                quarter_in.at[k],
                quarter_send.at[k],
                quarter_recv.at[k],
                {"grp": other},
            )
        )
    total = half_sum[pl.ds(grp * quarter, quarter), :]
    for k in range(1, groups):
        copies[k - 1].wait_recv()
        total = total + quarter_in[k].astype(high)
    quarter_sum[...] = total
    sends += copies

    copies = []
    for k in range(1, levels):
        other = lax.rem(level + k, levels)
        piece_out[k] = quarter_sum[pl.ds(other * piece, piece), :].astype(low)
        copies.append(
            send(
                piece_out.at[k],
                piece_in.at[k],
                piece_send.at[k],
                piece_recv.at[k],
                {"dom": 2 * other + core},
            )
        )
    total = quarter_sum[pl.ds(level * piece, piece), :]
    for k in range(1, levels):
        copies[k - 1].wait_recv()
        total = total + piece_in[k].astype(high)
    sends += copies

    own_half = core * half
    own_quarter = own_half + grp * quarter
    own_piece = own_quarter + level * piece
    all_s[pl.ds(own_piece, piece), :] = total.astype(low)
    copies = []
    for k in range(1, levels):
        place = all_s.at[pl.ds(own_piece, piece), :]
        where = {"dom": 2 * lax.rem(level + k, levels) + core}
        copies.append(
            send(place, place, piece_send.at[levels + k], piece_recv.at[levels + k], where)
        )
    backs += [give_back(k) for k in range(1, peers) if k not in early]
    for copy in copies:
        copy.wait_recv()
    sends += copies
    copies = []
    for k in range(1, groups):
        place = all_s.at[pl.ds(own_quarter, quarter), :]
        where = {"grp": lax.rem(grp + k, groups)}
        copies.append(
            send(place, place, quarter_send.at[groups + k], quarter_recv.at[groups + k], where)
        )
    for copy in copies:
        copy.wait_recv()
    sends += copies
    place = all_s.at[pl.ds(own_half, half), :]
    copy = send(place, place, half_send.at[1], half_recv.at[1], twin)
    copy.wait_recv()
    sends.append(copy)
    loads[2].wait()
    for copy in backs:
        copy.wait()
    for copy in sends:
        copy.wait_send()
    sum_ref[...] = all_s[...]


def reduce_call(groups, peers, grads, slot_grad):
    rows = grads.shape[0]
    levels = peers // 2
    half, quarter, piece = rows // 2, rows // 2 // groups, rows // 2 // groups // levels
    dma = pltpu.SemaphoreType.DMA
    return pl.pallas_call(
        functools.partial(reduce_kernel, groups, peers),
        in_specs=[pl.BlockSpec(memory_space=pltpu.HBM)] * 2,
        out_specs=[
            pl.BlockSpec(memory_space=pltpu.VMEM),
            pl.BlockSpec(memory_space=pltpu.HBM),
        ],
        out_shape=[
            jax.ShapeDtypeStruct((rows, 128), low),
            jax.ShapeDtypeStruct(slot_grad.shape, low),
        ],
        scratch_shapes=[
            pltpu.VMEM((rows, 128), high),
            pltpu.VMEM((rows, 128), low),
            pltpu.VMEM((half, 128), low),
            pltpu.VMEM((half, 128), low),
            pltpu.VMEM((half, 128), high),
            pltpu.VMEM((groups, quarter, 128), low),
            pltpu.VMEM((groups, quarter, 128), low),
            pltpu.VMEM((quarter, 128), high),
            pltpu.VMEM((levels, piece, 128), low),
            pltpu.VMEM((levels, piece, 128), low),
            dma((peers,)),
            dma((peers,)),
            dma((2,)),
            dma((2,)),
            dma((2 * groups,)),
            dma((2 * groups,)),
            dma((2 * levels,)),
            dma((2 * levels,)),
            dma((3,)),
        ],
        compiler_params=pltpu.CompilerParams(
            collective_id=1, has_side_effects=True, vmem_limit_bytes=VMEM
        ),
        name="reduce",
    )(grads, slot_grad)


def adamw_step(master, moment_mean, moment_var, average, gradient, factor):
    clipped = gradient * factor
    mean_new = beta_one * moment_mean + (1.0 - beta_one) * clipped
    var_new = beta_two * moment_var + (1.0 - beta_two) * clipped * clipped
    mean_hat = mean_new / (1.0 - beta_one**STEP)
    var_hat = var_new / (1.0 - beta_two**STEP)
    updated = master - learn_rate * (
        mean_hat / (jnp.sqrt(var_hat) + adam_eps) + decay_rate * master
    )
    return (
        mean_new,
        var_new,
        updated,
        updated.astype(low),
        ema_keep * average + (1.0 - ema_keep) * updated,
    )


FIRST = (0, 384, 640, 1152, 1162)


def finish_kernel(unroll, asked_ref, *refs):
    sources, (norm_ref, *results), refs = refs[:19], refs[19:41], refs[41:]
    loaded, (rows_s, *staged, load_sem, store_sem) = refs[:19], refs[19:]
    summed_s, back_s, node_s = loaded[16:]
    loads = [
        pltpu.make_async_copy(source, place, load_sem.at[k])
        for k, (source, place) in enumerate(zip(sources, loaded))
    ]
    for load in [*loads[17:], loads[16], *loads[:16]]:
        load.start()
    loads[17].wait()
    rows_s[...] = back_s[...].astype(high)
    slots = asked_ref.shape[2]
    loads[18].wait()

    @pl.loop(0, rows_s.shape[0] // unroll)
    def _(group):
        base = group * unroll
        peer, first = lax.div(base, slots), lax.rem(base, slots)
        places = [pl.ds(asked_ref[peer, 0, first + k], 1) for k in range(unroll)]
        values = [
            node_s[place, :] + rows_s[pl.ds(base + k, 1), :] for k, place in enumerate(places)
        ]
        for place, value in zip(places, values):
            node_s[place, :] = value

    stores = [pltpu.make_async_copy(node_s, results[20], store_sem.at[20])]
    stores[0].start()
    for load in loads[:17]:
        load.wait()
    gradient = summed_s[...].astype(high)
    square = jnp.sum(gradient * gradient, axis=0, keepdims=True)
    grad_norm = jnp.sqrt(jnp.sum(square, axis=1, keepdims=True))
    norm_ref[0] = grad_norm[0, 0]
    factor = clip_level / jnp.maximum(grad_norm, clip_level)
    for k in range(4):
        values = [place[...] for place in loaded[4 * k : 4 * k + 4]]
        updates = adamw_step(*values, gradient[FIRST[k] : FIRST[k + 1]], factor)
        for place, value in enumerate(updates):
            place += 5 * k
            staged[place][...] = value
            store = pltpu.make_async_copy(staged[place], results[place], store_sem.at[place])
            store.start()
            stores.append(store)
    for store in stores:
        store.wait()


def finish_call(asked, part, back, summed, tensors):
    smem = pl.BlockSpec(memory_space=pltpu.SMEM)
    hbm = pl.BlockSpec(memory_space=pltpu.HBM)
    sources = [*tensors, summed, back, part]
    shapes = []
    for k in range(4):
        shape = tensors[4 * k].shape
        shapes += [jax.ShapeDtypeStruct(shape, kind) for kind in (high, high, high, low, high)]
    return pl.pallas_call(
        functools.partial(finish_kernel, 32),
        in_specs=[smem] + [hbm] * 19,
        out_specs=[smem] + [hbm] * 21,
        out_shape=[
            jax.ShapeDtypeStruct((1,), high),
            *shapes,
            jax.ShapeDtypeStruct(part.shape, high),
        ],
        scratch_shapes=[
            *[pltpu.VMEM(item.shape, item.dtype) for item in sources],
            pltpu.VMEM(back.shape, high),
            *[pltpu.VMEM(item.shape, item.dtype) for item in shapes],
            pltpu.SemaphoreType.DMA((19,)),
            pltpu.SemaphoreType.DMA((21,)),
        ],
        compiler_params=pltpu.CompilerParams(vmem_limit_bytes=VMEM),
        name="finish",
    )(asked, *sources)


def shards(
    node_in,
    edge_in,
    edge_slot,
    edge_receiver,
    edge_count,
    request,
    node_cot,
    edge_cot,
    *tensors,
):
    groups, peers = lax.axis_size("grp"), lax.axis_size("dom")
    slots = request.shape[2]
    z = Sizes(edge_in.shape[0], node_in.shape[0], peers * slots, groups * peers)
    slot_rows, asked = fetch_call(peers, request, node_in)
    node_out, edge_out, node_part, edge_grad, slot_grad, grads = layer_call(
        z,
        edge_count,
        edge_slot.reshape(-1, 128),
        edge_receiver.reshape(-1, 128),
        edge_in,
        edge_cot,
        node_in,
        node_cot,
        slot_rows.reshape(peers * slots, 128),
        tensors[::4],
    )
    summed, returned = reduce_call(groups, peers, grads, slot_grad.reshape(peers, slots, 128))
    flat = [tensor.reshape(-1, 128) for tensor in tensors]
    grad_norm, *results, node_grad = finish_call(
        asked, node_part, returned.reshape(peers * slots, 128), summed, flat
    )
    results = [value.reshape(tensors[k // 5 * 4].shape) for k, value in enumerate(results)]
    return (node_out, edge_out, node_grad, edge_grad, grad_norm.reshape(()), *results)


def solution(mesh):
    rows = P(("grp", "dom"), None)
    in_specs = (
        rows,
        rows,
        P(("grp", "dom")),
        P(("grp", "dom")),
        P(("grp", "dom")),
        P(("grp", "dom"), None, None),
        rows,
        rows,
    ) + (P(),) * 16
    out_specs = (rows,) * 4 + (P(),) * 21
    return jax.shard_map(shards, mesh=mesh, in_specs=in_specs, out_specs=out_specs, check_vma=False)
```

```python
import functools
import math

import jax
import jax.numpy as jnp
from jax import lax
from jax.experimental import pallas as pl
from jax.experimental.pallas import tpu as pltpu
from jax.sharding import PartitionSpec as P

STEP = 10

eps_norm = 1e-05
beta_one = 0.5
beta_two = 0.6
learn_rate = 0.08
decay_rate = 0.01
adam_eps = 1e-08
ema_keep = 0.9
clip_level = 1.0

gelu_in = math.sqrt(2.0 / math.pi)
gelu_cube = gelu_in * 0.044715

low = jnp.bfloat16
high = jnp.float32

GAP = 4
VMEM = 60 * 1024 * 1024
PAIRS = 8


def dot(operand, weights):
    return jnp.dot(operand, weights, preferred_element_type=high)


def dot_nt(operand, weights):
    return lax.dot_general(
        operand, weights, (((1,), (1,)), ((), ())), preferred_element_type=high
    )


def dot_tn(operand, weights):
    return lax.dot_general(
        operand, weights, (((0,), (0,)), ((), ())), preferred_element_type=high
    )


def gelu_pair(x):
    square = x * x
    u = x * (gelu_in + gelu_cube * square)
    s = 0.5 + 0.5 * jnp.tanh(u)
    value = x * s
    slope = s + (value - value * s) * (2.0 * gelu_in + (6.0 * gelu_cube) * square)
    return value, slope


def fold_rows(values):
    return jnp.sum(values.reshape(values.shape[0] // 8, 8, values.shape[1]), axis=0)


def emit(pairs, per_group, forward, middle, backward, end):
    groups = pairs // per_group
    streams = {"forward": forward, "middle": middle, "backward": backward, "end": end}
    started = dict.fromkeys(streams, 0)
    last = dict.fromkeys(streams, -GAP)
    active, done, now = [], set(), 0

    def ready(name, k):
        if name == "middle":
            return all(("forward", k * per_group + j) in done for j in range(per_group))
        if name == "end":
            return all(("backward", k * per_group + j) in done for j in range(per_group))
        return name == "forward" or ("middle", k // per_group) in done

    while len(done) < 2 * pairs + 2 * groups:
        for name in streams:
            k = started[name]
            count = pairs if name in ("forward", "backward") else groups
            if k < count and now - last[name] >= GAP and ready(name, k):
                active.append(((name, k), streams[name](k)))
                started[name], last[name] = k + 1, now
        for item in list(active):
            try:
                next(item[1])
            except StopIteration:
                active.remove(item)
                done.add(item[0])
        now += 1


class Sizes:
    def __init__(self, edges, nodes, slots, devices):
        self.edges, self.nodes, self.slots = edges, nodes, slots
        blocks = edges // 128
        self.rwin = nodes // blocks
        self.swin = slots // blocks
        self.sub = 4
        while self.sub * (self.rwin + self.swin) > 128:
            self.sub //= 2
        self.chunk = self.sub * 128
        self.chunk_slots = self.sub * self.swin
        self.chunk_nodes = self.sub * self.rwin
        self.pair_nodes, self.pair_slots = 2 * self.chunk_nodes, 2 * self.chunk_slots
        self.per_group = 4
        self.pairs = PAIRS
        self.group_nodes = self.per_group * self.pair_nodes
        self.group_slots = self.per_group * self.pair_slots
        self.tile = self.pairs * 2 * self.chunk
        self.tile_chunks = 2 * self.pairs
        self.tile_nodes = self.pairs * self.pair_nodes
        self.tile_slots = self.pairs * self.pair_slots
        self.steps = edges // self.tile
        self.grad_rows = -(-1162 // (16 * devices)) * 16 * devices


def diagonal(first, second):
    zero_a = jnp.zeros((first.shape[0], second.shape[1]), first.dtype)
    zero_b = jnp.zeros((second.shape[0], first.shape[1]), first.dtype)
    return jnp.concatenate(
        [
            jnp.concatenate([first, zero_a], axis=1),
            jnp.concatenate([zero_b, second], axis=1),
        ],
        axis=0,
    )


def twice(row):
    return jnp.concatenate([row, row], axis=1)


def layer_kernel(
    z,
    count_ref,
    slot_ids_ref,
    recv_ids_ref,
    edge_in_ref,
    edge_cot_ref,
    node_in_ref,
    node_cot_ref,
    slot_ref,
    edge_entry_ref,
    node_entry_ref,
    inner_ref,
    vec_ref,
    node_out_ref,
    edge_out_ref,
    node_grad_ref,
    edge_grad_ref,
    slot_grad_ref,
    grads_ref,
    pick_s,
    pick_t,
    act_one_s,
    act_two_s,
    slope_one_s,
    slope_two_s,
    normed_s,
    inverse_s,
    gathered_s,
    table_s,
    slot_pre_s,
    node_pre_s,
    slot_sum_s,
    recv_sum_s,
    sums_s,
    wide_s,
    below_s,
):
    step = pl.program_id(0)
    chunk, cn, cs = z.chunk, z.chunk_nodes, z.chunk_slots
    pad = 128 - cn - cs
    vec = [vec_ref[pl.ds(k, 1), :] for k in range(10)]

    @pl.when(step == 0)
    def _():
        grads_ref[...] = jnp.zeros_like(grads_ref)
        sums_s[...] = jnp.zeros_like(sums_s)
        first, second = inner_ref[0].astype(low), inner_ref[1].astype(low)
        wide_s[0] = diagonal(first, first)
        middle = second.astype(high)
        middle = (middle - jnp.mean(middle, axis=1, keepdims=True)).astype(low)
        wide_s[1] = diagonal(middle, middle)
        for k, weights in ((2, inner_ref[0]), (3, inner_ref[1]), (4, edge_entry_ref[0:128, :])):
            weights = weights.T.astype(low)
            wide_s[k] = diagonal(weights, weights)
        part = jnp.full((128, 128), 1.0 / 128.0, low)
        wide_s[5] = diagonal(part, part)
        row = lax.broadcasted_iota(jnp.int32, (128, 128), 0)
        column = lax.broadcasted_iota(jnp.int32, (128, 128), 1)
        gain = jnp.broadcast_to(vec[3] * (1.0 / 128.0), (128, 128)).T.astype(low)
        wide_s[6] = diagonal(gain, gain)
        below_s[:, :128] = jnp.where(row == column, 1.0, 0.0).astype(low)
        below_s[:, 128:] = gain

    edge_low = edge_entry_ref[...].astype(low)
    node_low = node_entry_ref[...].astype(low)
    inner_low = [None, None, inner_ref[2].astype(low), inner_ref[3].astype(low)]
    w_edge, w_slot, w_recv = edge_low[:128], edge_low[128:256], edge_low[256:]
    bias_three = vec[2] - jnp.mean(vec[2], axis=1, keepdims=True)
    gain_part = below_s[:, 128:]
    row_ids = lax.broadcasted_iota(jnp.int32, (chunk, 128), 0)
    slot_pre_s[...] = dot(slot_ref[...], w_slot).astype(low)
    node_pre_s[...] = (dot(node_in_ref[...], w_recv) + vec[0]).astype(low)

    def live_rows(index):
        return row_ids < count_ref[0] - (step * z.tile + index * chunk)

    def sides(wide):
        return wide[:, :128], wide[:, 128:]

    def chunk_rows(index):
        return pl.ds(index * chunk, chunk)

    def hot_columns(index):
        columns = []
        for k in range(z.sub):
            block = index * z.sub + k
            number = step * (z.tile // 128) + block
            pieces = []
            for ref, width, count in ((slot_ids_ref, z.swin, cs), (recv_ids_ref, z.rwin, cn)):
                ids = ref[pl.ds(block, 1), :] - number * width
                band = lax.broadcasted_iota(jnp.int32, (width, 128), 0) == ids
                above, below = k * width, count - (k + 1) * width
                if above:
                    pieces.append(jnp.zeros((above, 128), high))
                pieces.append(jnp.where(band, 1.0, 0.0))
                if below:
                    pieces.append(jnp.zeros((below, 128), high))
            if pad:
                pieces.append(jnp.zeros((pad, 128), high))
            columns.append(jnp.concatenate(pieces, axis=0).astype(low))
        return jnp.concatenate(columns, axis=1)

    def edge_forward(pair):
        wide_rows = chunk_rows(pair)
        indices = (2 * pair, 2 * pair + 1)
        pres = []
        for side, index in enumerate(indices):
            hot_t = hot_columns(index)
            hot = hot_t.T
            pick_t[index] = hot_t
            pick_s[chunk_rows(index), :] = hot
            tables = [
                w_edge,
                slot_pre_s[pl.ds(index * cs, cs), :],
                node_pre_s[pl.ds(index * cn, cn), :],
            ]
            if pad:
                tables.append(jnp.zeros((pad, 128), low))
            rows = edge_in_ref[chunk_rows(index), :]
            pres.append(
                dot(jnp.concatenate([rows, hot], axis=1), jnp.concatenate(tables, axis=0)).astype(low)
            )
            yield
        act_one, slope = gelu_pair(jnp.concatenate(pres, axis=1))
        act_one_s[wide_rows, :] = act_one
        slope_one_s[wide_rows, :] = slope
        yield
        pre_two = (dot(act_one, wide_s[0]) + twice(vec[1])).astype(low)
        yield
        act_two, slope = gelu_pair(pre_two)
        act_two_s[wide_rows, :] = act_two
        slope_two_s[wide_rows, :] = slope
        yield
        center = dot(act_two, wide_s[1]) + twice(bias_three)
        yield
        messages = []
        for index, center in zip(indices, sides(center)):
            live = live_rows(index)
            inverse = lax.rsqrt(jnp.mean(center * center, axis=1, keepdims=True) + eps_norm)
            inverse = jnp.where(live, inverse, 0.0)
            normed = center * inverse
            normed_s[chunk_rows(index), :] = normed
            inverse_s[chunk_rows(index), :] = inverse
            message = jnp.where(live, normed * vec[3] + vec[4], 0.0)
            rows = edge_in_ref[chunk_rows(index), :]
            edge_out_ref[chunk_rows(index), :] = (rows.astype(high) + message).astype(low)
            messages.append(message.astype(low))
        yield
        hots = [pick_t[index, cs : cs + cn, :] for index in indices]
        total = dot(jnp.concatenate(hots, axis=0), jnp.concatenate(messages, axis=1)).astype(low)
        gathered_s[pl.ds(indices[0] * cn, cn), :] = total[:cn, :128]
        gathered_s[pl.ds(indices[1] * cn, cn), :] = total[cn:, 128:]
        yield

    def node_phase(group):
        rows = pl.ds(group * z.group_nodes, z.group_nodes)
        node_rows = node_in_ref[rows, :]
        entry = jnp.concatenate([node_rows, gathered_s[rows, :]], axis=1)
        node_one = (dot(entry, node_low) + vec[5]).astype(low)
        yield
        act_one, slope_one = gelu_pair(node_one)
        yield
        node_two = (dot(act_one, inner_low[2]) + vec[6]).astype(low)
        yield
        act_two, slope_two = gelu_pair(node_two)
        yield
        node_three = dot(act_two, inner_low[3]) + vec[7]
        yield
        center = node_three - jnp.mean(node_three, axis=1, keepdims=True)
        inverse = lax.rsqrt(jnp.mean(center * center, axis=1, keepdims=True) + eps_norm)
        normed = center * inverse
        node_out_ref[rows, :] = (node_rows.astype(high) + normed * vec[8] + vec[9]).astype(low)
        yield
        upstream = node_cot_ref[rows, :].astype(high)
        sums_s[8] += fold_rows(upstream * normed)
        sums_s[9] += fold_rows(upstream)
        upper = upstream * vec[8]
        mean_plain = jnp.mean(upper, axis=1, keepdims=True)
        mean_cross = jnp.mean(upper * normed, axis=1, keepdims=True)
        d_three = inverse * (upper - mean_plain - normed * mean_cross)
        sums_s[7] += fold_rows(d_three)
        d_three = d_three.astype(low)
        yield
        back = dot_nt(d_three, inner_low[3])
        yield
        d_two = back * slope_two.astype(high)
        sums_s[6] += fold_rows(d_two)
        d_two = d_two.astype(low)
        yield
        back = dot_nt(d_two, inner_low[2])
        yield
        d_one = back * slope_one.astype(high)
        sums_s[5] += fold_rows(d_one)
        d_one = d_one.astype(low)
        yield
        back = dot_nt(d_one, node_low)
        node_grad_ref[rows, :] = upstream + back[:, :128]
        arrived = back[:, 128:].astype(low)
        yield
        table_s[rows, :128] = arrived
        table_s[rows, 128:] = dot(arrived, gain_part).astype(low)
        yield
        grads_ref[384:640, :] += dot_tn(entry, d_one)
        grads_ref[896:1024, :] += dot_tn(act_one, d_two)
        grads_ref[1024:1152, :] += dot_tn(act_two, d_three)
        yield

    def edge_backward(pair):
        wide_rows = chunk_rows(pair)
        indices = (2 * pair, 2 * pair + 1)
        upstreams, plains = [], []
        for index in indices:
            tables = [
                jnp.zeros((cs, 256), low),
                table_s[pl.ds(index * cn, cn), :],
            ]
            if pad:
                tables.append(jnp.zeros((pad, 256), low))
            tables.append(below_s[...])
            entry = jnp.concatenate(
                [pick_s[chunk_rows(index), :], edge_cot_ref[chunk_rows(index), :]], axis=1
            )
            upstream, plain = sides(dot(entry, jnp.concatenate(tables, axis=0)))
            upstreams.append(upstream)
            plains.append(plain)
            yield
        threes = []
        for index, upstream, plain in zip(indices, upstreams, plains):
            normed = normed_s[chunk_rows(index), :]
            cross = upstream * normed
            sums_s[3] += fold_rows(cross)
            sums_s[4] += fold_rows(jnp.where(live_rows(index), upstream, 0.0))
            cross = jnp.mean(cross * vec[3], axis=1, keepdims=True)
            d_three = inverse_s[chunk_rows(index), :] * (
                upstream * vec[3] - plain - normed * cross
            )
            threes.append(d_three.astype(low))
        d_three = jnp.concatenate(threes, axis=1)
        yield
        d_two = dot(d_three, wide_s[3]).astype(low) * slope_two_s[wide_rows, :]
        yield
        d_one = dot(d_two, wide_s[2]).astype(low) * slope_one_s[wide_rows, :]
        yield
        for index, back in zip(indices, sides(dot(d_one, wide_s[4]))):
            edge_grad_ref[chunk_rows(index), :] = (
                edge_cot_ref[chunk_rows(index), :].astype(high) + back
            )
        yield
        ones = jnp.ones((16, chunk), low)
        entry = [edge_in_ref[chunk_rows(index), :].T for index in indices]
        hots = [pick_t[index, : cs + cn, :] for index in indices]
        total = dot(jnp.concatenate(entry + hots, axis=0), d_one)
        grads_ref[0:128, :] += total[:128, :128] + total[128:256, 128:]
        first = total[256 : 256 + cs + cn, :128]
        second = total[256 + cs + cn :, 128:]
        yield
        node_rows = pl.ds(pair * z.pair_nodes, z.pair_nodes)
        slot_rows = pl.ds(pair * z.pair_slots, z.pair_slots)
        slot_sum_s[slot_rows, :] = jnp.concatenate([first[:cs], second[:cs]], axis=0).astype(low)
        recv_sum = jnp.concatenate([first[cs:], second[cs:]], axis=0)
        sums_s[0] += fold_rows(recv_sum)
        recv_sum_s[node_rows, :] = recv_sum.astype(low)
        yield
        for k, act_s, gradient in ((1, act_one_s, d_two), (2, act_two_s, d_three)):
            total = dot(jnp.concatenate([act_s[wide_rows, :].T, ones], axis=0), gradient)
            grads_ref[pl.ds(512 + 128 * k, 128), :] += total[:128, :128] + total[128:256, 128:]
            sums_s[k] += (total[256:264, :128] + total[256:264, 128:]) * 0.125
            yield

    def group_end(group):
        node_rows = pl.ds(group * z.group_nodes, z.group_nodes)
        slot_rows = pl.ds(group * z.group_slots, z.group_slots)
        slot_grad_ref[slot_rows, :] = dot_nt(slot_sum_s[slot_rows, :], w_slot).astype(low)
        node_grad_ref[node_rows, :] += dot_nt(recv_sum_s[node_rows, :], w_recv)
        yield
        grads_ref[128:256, :] += dot_tn(slot_ref[slot_rows, :], slot_sum_s[slot_rows, :])
        grads_ref[256:384, :] += dot_tn(node_in_ref[node_rows, :], recv_sum_s[node_rows, :])
        yield

    emit(z.pairs, z.per_group, edge_forward, node_phase, edge_backward, group_end)

    @pl.when(step == z.steps - 1)
    def _():
        grads_ref[1152:1162, :] = jnp.sum(sums_s[...], axis=1)


def layer_call(z, count, slot_ids, recv_ids, edge_in, edge_cot, node_in, node_cot, slot_rows, weights):
    def rows_spec(rows):
        return pl.BlockSpec((rows, 128), lambda i: (i, 0))

    def whole(array):
        return pl.BlockSpec(array.shape, lambda i: (0,) * array.ndim)

    return pl.pallas_call(
        functools.partial(layer_kernel, z),
        grid=(z.steps,),
        in_specs=[
            pl.BlockSpec(memory_space=pltpu.SMEM),
            rows_spec(z.tile // 128),
            rows_spec(z.tile // 128),
            rows_spec(z.tile),
            rows_spec(z.tile),
            rows_spec(z.tile_nodes),
            rows_spec(z.tile_nodes),
            rows_spec(z.tile_slots),
        ]
        + [whole(w) for w in weights],
        out_specs=[
            rows_spec(z.tile_nodes),
            rows_spec(z.tile),
            rows_spec(z.tile_nodes),
            rows_spec(z.tile),
            rows_spec(z.tile_slots),
            pl.BlockSpec((z.grad_rows, 128), lambda i: (0, 0)),
        ],
        out_shape=[
            jax.ShapeDtypeStruct((z.nodes, 128), low),
            jax.ShapeDtypeStruct((z.edges, 128), low),
            jax.ShapeDtypeStruct((z.nodes, 128), high),
            jax.ShapeDtypeStruct((z.edges, 128), high),
            jax.ShapeDtypeStruct((z.slots, 128), low),
            jax.ShapeDtypeStruct((z.grad_rows, 128), high),
        ],
        scratch_shapes=[
            pltpu.VMEM((z.tile, 128), low),
            pltpu.VMEM((z.tile_chunks, 128, z.chunk), low),
            pltpu.VMEM((z.tile // 2, 256), low),
            pltpu.VMEM((z.tile // 2, 256), low),
            pltpu.VMEM((z.tile // 2, 256), low),
            pltpu.VMEM((z.tile // 2, 256), low),
            pltpu.VMEM((z.tile, 128), high),
            pltpu.VMEM((z.tile, 128), high),
            pltpu.VMEM((z.tile_nodes, 128), low),
            pltpu.VMEM((z.tile_nodes, 256), low),
            pltpu.VMEM((z.tile_slots, 128), low),
            pltpu.VMEM((z.tile_nodes, 128), low),
            pltpu.VMEM((z.tile_slots, 128), low),
            pltpu.VMEM((z.tile_nodes, 128), low),
            pltpu.VMEM((10, 8, 128), high),
            pltpu.VMEM((7, 256, 256), low),
            pltpu.VMEM((128, 256), low),
        ],
        compiler_params=pltpu.CompilerParams(
            dimension_semantics=("arbitrary",), vmem_limit_bytes=VMEM
        ),
        name="layer",
    )(count, slot_ids, recv_ids, edge_in, edge_cot, node_in, node_cot, slot_rows, *weights)


def signal(semaphore, where):
    pl.semaphore_signal(semaphore, inc=1, device_id=where, device_id_type=pl.DeviceIdType.MESH)


def send(source, target, send_sem, recv_sem, where):
    copy = pltpu.make_async_remote_copy(
        src_ref=source,
        dst_ref=target,
        send_sem=send_sem,
        recv_sem=recv_sem,
        device_id=where,
        device_id_type=pl.DeviceIdType.MESH,
    )
    copy.start()
    return copy


def fetch_kernel(
    peers,
    unroll,
    request_ref,
    node_ref,
    rows_ref,
    asked_ref,
    wanted_v,
    asked_v,
    node_v,
    node_s,
    picked_s,
    out_s,
    ask_send,
    ask_recv,
    row_send,
    row_recv,
    load_sem,
):
    me = lax.axis_index("dom")
    slots = picked_s.shape[0]
    barrier = pltpu.get_barrier_semaphore()
    for k in range(1, peers):
        signal(barrier, {"dom": lax.rem(me + k, peers)})
    loads = [
        pltpu.make_async_copy(request_ref, wanted_v, load_sem.at[0]),
        pltpu.make_async_copy(node_ref, node_v, load_sem.at[1]),
    ]
    for load in loads:
        load.start()
    loads[0].wait()
    for k in range(peers):
        asked_v[k] = wanted_v[pl.ds(k, 1), :]
    loads[1].wait()
    node_s[...] = node_v[...].astype(high)
    pl.semaphore_wait(barrier, peers - 1)
    shifts = [peers // 2 + (k // 2) * (1 - 2 * (k % 2)) for k in range(1, peers)]
    asks = [
        send(
            asked_v.at[lax.rem(me + k, peers)],
            asked_v.at[peers + me],
            ask_send.at[k],
            ask_recv.at[k],
            {"dom": lax.rem(me + k, peers)},
        )
        for k in shifts
    ]
    asked_v[peers + me] = asked_v[me]
    for ask in asks:
        ask.wait_recv()
    local = pltpu.make_async_copy(asked_v.at[pl.ds(peers, peers)], asked_ref, load_sem.at[0])
    local.start()
    local.wait()
    sends = []
    for k in shifts + [0]:
        other = lax.rem(me + (peers - k), peers)

        @pl.loop(0, slots // unroll)
        def _(group):
            for place in range(unroll):
                row = group * unroll + place
                index = asked_ref[other, 0, row]
                picked_s[pl.ds(row, 1), :] = node_s[pl.ds(index, 1), :]

        out_s[other] = picked_s[...].astype(low)
        if k:
            sends.append(
                send(
                    out_s.at[other],
                    rows_ref.at[me],
                    row_send.at[k],
                    row_recv.at[k],
                    {"dom": other},
                )
            )
    local = pltpu.make_async_copy(out_s.at[me], rows_ref.at[me], load_sem.at[0])
    local.start()
    for copy in asks:
        copy.wait_send()
    local.wait()
    for copy in sends:
        copy.wait()


def fetch_call(peers, request, node_in):
    slots = request.shape[2]
    dma = pltpu.SemaphoreType.DMA
    hbm = pl.BlockSpec(memory_space=pltpu.HBM)
    return pl.pallas_call(
        functools.partial(fetch_kernel, peers, 32),
        in_specs=[hbm, hbm],
        out_specs=[hbm, pl.BlockSpec(memory_space=pltpu.SMEM)],
        out_shape=[
            jax.ShapeDtypeStruct((peers, slots, 128), low),
            jax.ShapeDtypeStruct((peers, 1, slots), jnp.int32),
        ],
        scratch_shapes=[
            pltpu.VMEM((peers, slots), jnp.int32),
            pltpu.VMEM((2 * peers, 1, slots), jnp.int32),
            pltpu.VMEM(node_in.shape, low),
            pltpu.VMEM(node_in.shape, high),
            pltpu.VMEM((slots, 128), high),
            pltpu.VMEM((peers, slots, 128), low),
            dma((peers,)),
            dma((peers,)),
            dma((peers,)),
            dma((peers,)),
            dma((2,)),
        ],
        compiler_params=pltpu.CompilerParams(
            collective_id=0, has_side_effects=True, vmem_limit_bytes=VMEM
        ),
        name="fetch",
    )(request.reshape(peers, slots), node_in)


def reduce_kernel(
    groups,
    peers,
    grads_ref,
    slot_grad_ref,
    sum_ref,
    back_ref,
    grads_s,
    all_s,
    half_out,
    half_in,
    half_sum,
    quarter_out,
    quarter_in,
    quarter_sum,
    piece_out,
    piece_in,
    back_send,
    back_recv,
    half_send,
    half_recv,
    quarter_send,
    quarter_recv,
    piece_send,
    piece_recv,
    load_sem,
):
    grp, dom = lax.axis_index("grp"), lax.axis_index("dom")
    core, level = lax.rem(dom, 2), lax.div(dom, 2)
    levels = peers // 2
    half, quarter, piece = half_sum.shape[0], quarter_sum.shape[0], piece_out.shape[1]
    barrier = pltpu.get_barrier_semaphore()
    for k in range(1, peers):
        signal(barrier, {"dom": lax.rem(dom + k, peers)})
    for k in range(1, groups):
        signal(barrier, {"grp": lax.rem(grp + k, groups)})
    twin = {"dom": 2 * level + 1 - core}
    loads = [
        pltpu.make_async_copy(
            grads_ref.at[pl.ds(first, half), :], grads_s.at[pl.ds(first, half), :], load_sem.at[k]
        )
        for k, first in enumerate(((1 - core) * half, core * half))
    ]
    loads.append(
        pltpu.make_async_copy(slot_grad_ref.at[dom], back_ref.at[dom], load_sem.at[2])
    )
    for load in loads:
        load.start()
    loads[0].wait()
    half_out[...] = grads_s[pl.ds((1 - core) * half, half), :].astype(low)
    loads[1].wait()
    pl.semaphore_wait(barrier, peers - 1 + groups - 1)

    sends = [send(half_out, half_in, half_send.at[0], half_recv.at[0], twin)]

    def give_back(k):
        other = lax.rem(dom + k, peers)
        return send(
            slot_grad_ref.at[other],
            back_ref.at[dom],
            back_send.at[k],
            back_recv.at[k],
            {"dom": other},
        )

    early = [k for k in range(1, peers) if 2 * k == peers or (2 * k < peers and k % 2)]
    backs = [give_back(k) for k in early]
    sends[0].wait_recv()
    half_sum[...] = grads_s[pl.ds(core * half, half), :] + half_in[...].astype(high)

    copies = []
    for k in range(1, groups):
        other = lax.rem(grp + k, groups)
        quarter_out[k] = half_sum[pl.ds(other * quarter, quarter), :].astype(low)
        copies.append(
            send(
                quarter_out.at[k],
                quarter_in.at[k],
                quarter_send.at[k],
                quarter_recv.at[k],
                {"grp": other},
            )
        )
    total = half_sum[pl.ds(grp * quarter, quarter), :]
    for k in range(1, groups):
        copies[k - 1].wait_recv()
        total = total + quarter_in[k].astype(high)
    quarter_sum[...] = total
    sends += copies

    copies = []
    for k in range(1, levels):
        other = lax.rem(level + k, levels)
        piece_out[k] = quarter_sum[pl.ds(other * piece, piece), :].astype(low)
        copies.append(
            send(
                piece_out.at[k],
                piece_in.at[k],
                piece_send.at[k],
                piece_recv.at[k],
                {"dom": 2 * other + core},
            )
        )
    total = quarter_sum[pl.ds(level * piece, piece), :]
    for k in range(1, levels):
        copies[k - 1].wait_recv()
        total = total + piece_in[k].astype(high)
    sends += copies

    own_half = core * half
    own_quarter = own_half + grp * quarter
    own_piece = own_quarter + level * piece
    all_s[pl.ds(own_piece, piece), :] = total.astype(low)
    copies = []
    for k in range(1, levels):
        place = all_s.at[pl.ds(own_piece, piece), :]
        where = {"dom": 2 * lax.rem(level + k, levels) + core}
        copies.append(
            send(place, place, piece_send.at[levels + k], piece_recv.at[levels + k], where)
        )
    backs += [give_back(k) for k in range(1, peers) if k not in early]
    for copy in copies:
        copy.wait_recv()
    sends += copies
    copies = []
    for k in range(1, groups):
        place = all_s.at[pl.ds(own_quarter, quarter), :]
        where = {"grp": lax.rem(grp + k, groups)}
        copies.append(
            send(place, place, quarter_send.at[groups + k], quarter_recv.at[groups + k], where)
        )
    for copy in copies:
        copy.wait_recv()
    sends += copies
    place = all_s.at[pl.ds(own_half, half), :]
    copy = send(place, place, half_send.at[1], half_recv.at[1], twin)
    copy.wait_recv()
    sends.append(copy)
    loads[2].wait()
    for copy in backs:
        copy.wait()
    for copy in sends:
        copy.wait_send()
    sum_ref[...] = all_s[...]


def reduce_call(groups, peers, grads, slot_grad):
    rows = grads.shape[0]
    levels = peers // 2
    half, quarter, piece = rows // 2, rows // 2 // groups, rows // 2 // groups // levels
    dma = pltpu.SemaphoreType.DMA
    return pl.pallas_call(
        functools.partial(reduce_kernel, groups, peers),
        in_specs=[pl.BlockSpec(memory_space=pltpu.HBM)] * 2,
        out_specs=[
            pl.BlockSpec(memory_space=pltpu.VMEM),
            pl.BlockSpec(memory_space=pltpu.HBM),
        ],
        out_shape=[
            jax.ShapeDtypeStruct((rows, 128), low),
            jax.ShapeDtypeStruct(slot_grad.shape, low),
        ],
        scratch_shapes=[
            pltpu.VMEM((rows, 128), high),
            pltpu.VMEM((rows, 128), low),
            pltpu.VMEM((half, 128), low),
            pltpu.VMEM((half, 128), low),
            pltpu.VMEM((half, 128), high),
            pltpu.VMEM((groups, quarter, 128), low),
            pltpu.VMEM((groups, quarter, 128), low),
            pltpu.VMEM((quarter, 128), high),
            pltpu.VMEM((levels, piece, 128), low),
            pltpu.VMEM((levels, piece, 128), low),
            dma((peers,)),
            dma((peers,)),
            dma((2,)),
            dma((2,)),
            dma((2 * groups,)),
            dma((2 * groups,)),
            dma((2 * levels,)),
            dma((2 * levels,)),
            dma((3,)),
        ],
        compiler_params=pltpu.CompilerParams(
            collective_id=1, has_side_effects=True, vmem_limit_bytes=VMEM
        ),
        name="reduce",
    )(grads, slot_grad)


def adamw_step(master, moment_mean, moment_var, average, gradient, factor):
    clipped = gradient * factor
    mean_new = beta_one * moment_mean + (1.0 - beta_one) * clipped
    var_new = beta_two * moment_var + (1.0 - beta_two) * clipped * clipped
    mean_hat = mean_new / (1.0 - beta_one**STEP)
    var_hat = var_new / (1.0 - beta_two**STEP)
    updated = master - learn_rate * (
        mean_hat / (jnp.sqrt(var_hat) + adam_eps) + decay_rate * master
    )
    return (
        mean_new,
        var_new,
        updated,
        updated.astype(low),
        ema_keep * average + (1.0 - ema_keep) * updated,
    )


FIRST = (0, 384, 640, 1152, 1162)


def finish_kernel(unroll, asked_ref, *refs):
    sources, (norm_ref, *results), refs = refs[:19], refs[19:41], refs[41:]
    loaded, (rows_s, *staged, load_sem, store_sem) = refs[:19], refs[19:]
    summed_s, back_s, node_s = loaded[16:]
    loads = [
        pltpu.make_async_copy(source, place, load_sem.at[k])
        for k, (source, place) in enumerate(zip(sources, loaded))
    ]
    for load in [*loads[17:], loads[16], *loads[:16]]:
        load.start()
    loads[17].wait()
    rows_s[...] = back_s[...].astype(high)
    slots = asked_ref.shape[2]
    loads[18].wait()

    @pl.loop(0, rows_s.shape[0] // unroll)
    def _(group):
        base = group * unroll
        peer, first = lax.div(base, slots), lax.rem(base, slots)
        places = [pl.ds(asked_ref[peer, 0, first + k], 1) for k in range(unroll)]
        values = [
            node_s[place, :] + rows_s[pl.ds(base + k, 1), :] for k, place in enumerate(places)
        ]
        for place, value in zip(places, values):
            node_s[place, :] = value

    stores = [pltpu.make_async_copy(node_s, results[20], store_sem.at[20])]
    stores[0].start()
    for load in loads[:17]:
        load.wait()
    gradient = summed_s[...].astype(high)
    square = jnp.sum(gradient * gradient, axis=0, keepdims=True)
    grad_norm = jnp.sqrt(jnp.sum(square, axis=1, keepdims=True))
    norm_ref[0] = grad_norm[0, 0]
    factor = clip_level / jnp.maximum(grad_norm, clip_level)
    for k in range(4):
        values = [place[...] for place in loaded[4 * k : 4 * k + 4]]
        updates = adamw_step(*values, gradient[FIRST[k] : FIRST[k + 1]], factor)
        for place, value in enumerate(updates):
            place += 5 * k
            staged[place][...] = value
            store = pltpu.make_async_copy(staged[place], results[place], store_sem.at[place])
            store.start()
            stores.append(store)
    for store in stores:
        store.wait()


def finish_call(asked, part, back, summed, tensors):
    smem = pl.BlockSpec(memory_space=pltpu.SMEM)
    hbm = pl.BlockSpec(memory_space=pltpu.HBM)
    sources = [*tensors, summed, back, part]
    shapes = []
    for k in range(4):
        shape = tensors[4 * k].shape
        shapes += [jax.ShapeDtypeStruct(shape, kind) for kind in (high, high, high, low, high)]
    return pl.pallas_call(
        functools.partial(finish_kernel, 32),
        in_specs=[smem] + [hbm] * 19,
        out_specs=[smem] + [hbm] * 21,
        out_shape=[
            jax.ShapeDtypeStruct((1,), high),
            *shapes,
            jax.ShapeDtypeStruct(part.shape, high),
        ],
        scratch_shapes=[
            *[pltpu.VMEM(item.shape, item.dtype) for item in sources],
            pltpu.VMEM(back.shape, high),
            *[pltpu.VMEM(item.shape, item.dtype) for item in shapes],
            pltpu.SemaphoreType.DMA((19,)),
            pltpu.SemaphoreType.DMA((21,)),
        ],
        compiler_params=pltpu.CompilerParams(vmem_limit_bytes=VMEM),
        name="finish",
    )(asked, *sources)


def shards(
    node_in,
    edge_in,
    edge_slot,
    edge_receiver,
    edge_count,
    request,
    node_cot,
    edge_cot,
    *tensors,
):
    groups, peers = lax.axis_size("grp"), lax.axis_size("dom")
    slots = request.shape[2]
    z = Sizes(edge_in.shape[0], node_in.shape[0], peers * slots, groups * peers)
    slot_rows, asked = fetch_call(peers, request, node_in)
    node_out, edge_out, node_part, edge_grad, slot_grad, grads = layer_call(
        z,
        edge_count,
        edge_slot.reshape(-1, 128),
        edge_receiver.reshape(-1, 128),
        edge_in,
        edge_cot,
        node_in,
        node_cot,
        slot_rows.reshape(peers * slots, 128),
        tensors[::4],
    )
    summed, returned = reduce_call(groups, peers, grads, slot_grad.reshape(peers, slots, 128))
    flat = [tensor.reshape(-1, 128) for tensor in tensors]
    grad_norm, *results, node_grad = finish_call(
        asked, node_part, returned.reshape(peers * slots, 128), summed, flat
    )
    results = [value.reshape(tensors[k // 5 * 4].shape) for k, value in enumerate(results)]
    return (node_out, edge_out, node_grad, edge_grad, grad_norm.reshape(()), *results)


def solution(mesh):
    rows = P(("grp", "dom"), None)
    in_specs = (
        rows,
        rows,
        P(("grp", "dom")),
        P(("grp", "dom")),
        P(("grp", "dom")),
        P(("grp", "dom"), None, None),
        rows,
        rows,
    ) + (P(),) * 16
    out_specs = (rows,) * 4 + (P(),) * 21
    return jax.shard_map(shards, mesh=mesh, in_specs=in_specs, out_specs=out_specs, check_vma=False)
```

```python
import functools
import math

import jax
import jax.numpy as jnp
from jax import lax
from jax.experimental import pallas as pl
from jax.experimental.pallas import tpu as pltpu
from jax.sharding import PartitionSpec as P

STEP = 10

eps_norm = 1e-05
beta_one = 0.5
beta_two = 0.6
learn_rate = 0.08
decay_rate = 0.01
adam_eps = 1e-08
ema_keep = 0.9
clip_level = 1.0

gelu_in = math.sqrt(2.0 / math.pi)
gelu_cube = gelu_in * 0.044715

low = jnp.bfloat16
high = jnp.float32

GAP = 2
PIECE = 64
PIECE_NORM = 32
VMEM = 60 * 1024 * 1024
PAIRS = 2


def dot(operand, weights):
    return jnp.dot(operand, weights, preferred_element_type=high)


def dot_nt(operand, weights):
    return lax.dot_general(
        operand, weights, (((1,), (1,)), ((), ())), preferred_element_type=high
    )


def dot_tn(operand, weights):
    return lax.dot_general(
        operand, weights, (((0,), (0,)), ((), ())), preferred_element_type=high
    )


def gelu_pair(x):
    square = x * x
    u = x * (gelu_in + gelu_cube * square)
    s = 0.5 + 0.5 * jnp.tanh(u)
    value = x * s
    slope = s + (value - value * s) * (2.0 * gelu_in + (6.0 * gelu_cube) * square)
    return value, slope


def fold_rows(values):
    return jnp.sum(values.reshape(values.shape[0] // 8, 8, values.shape[1]), axis=0)


def emit(pairs, per_group, forward, middle, backward, end):
    groups = pairs // per_group
    streams = {"forward": forward, "middle": middle, "backward": backward, "end": end}
    started = dict.fromkeys(streams, 0)
    last = dict.fromkeys(streams, -GAP)
    active, done, now = [], set(), 0

    def ready(name, k):
        if name == "middle":
            return all(("forward", k * per_group + j) in done for j in range(per_group))
        if name == "end":
            return all(("backward", k * per_group + j) in done for j in range(per_group))
        return name == "forward" or ("middle", k // per_group) in done

    while len(done) < 2 * pairs + 2 * groups:
        for name in streams:
            k = started[name]
            count = pairs if name in ("forward", "backward") else groups
            if k < count and now - last[name] >= GAP and ready(name, k):
                active.append(((name, k), streams[name](k)))
                started[name], last[name] = k + 1, now
        for item in list(active):
            try:
                next(item[1])
            except StopIteration:
                active.remove(item)
                done.add(item[0])
        now += 1


class Sizes:
    def __init__(self, edges, nodes, slots, devices):
        self.edges, self.nodes, self.slots = edges, nodes, slots
        blocks = edges // 128
        self.rwin = nodes // blocks
        self.swin = slots // blocks
        self.sub = 4
        while self.sub * (self.rwin + self.swin) > 128:
            self.sub //= 2
        self.chunk = self.sub * 128
        self.chunk_slots = self.sub * self.swin
        self.chunk_nodes = self.sub * self.rwin
        self.pair_nodes, self.pair_slots = 2 * self.chunk_nodes, 2 * self.chunk_slots
        self.per_group = 2
        self.pairs = max(PAIRS, 1024 // (2 * self.chunk))
        self.group_nodes = self.per_group * self.pair_nodes
        self.group_slots = self.per_group * self.pair_slots
        self.tile = self.pairs * 2 * self.chunk
        self.tile_chunks = 2 * self.pairs
        self.tile_nodes = self.pairs * self.pair_nodes
        self.tile_slots = self.pairs * self.pair_slots
        self.steps = edges // self.tile
        self.grad_rows = -(-1162 // (16 * devices)) * 16 * devices


def diagonal(first, second):
    zero_a = jnp.zeros((first.shape[0], second.shape[1]), first.dtype)
    zero_b = jnp.zeros((second.shape[0], first.shape[1]), first.dtype)
    return jnp.concatenate(
        [
            jnp.concatenate([first, zero_a], axis=1),
            jnp.concatenate([zero_b, second], axis=1),
        ],
        axis=0,
    )


def twice(row):
    return jnp.concatenate([row, row], axis=1)


def layer_kernel(
    z,
    count_ref,
    slot_ids_ref,
    recv_ids_ref,
    edge_in_ref,
    edge_cot_ref,
    node_in_ref,
    node_cot_ref,
    slot_ref,
    edge_entry_ref,
    node_entry_ref,
    inner_ref,
    vec_ref,
    node_out_ref,
    edge_out_ref,
    node_grad_ref,
    edge_grad_ref,
    slot_grad_ref,
    grads_ref,
    pick_s,
    pick_t,
    act_one_s,
    act_two_s,
    slope_one_s,
    slope_two_s,
    normed_s,
    inverse_s,
    message_s,
    node_act_s,
    node_slope_s,
    node_back_s,
    gathered_s,
    table_s,
    slot_pre_s,
    node_pre_s,
    slot_sum_s,
    recv_sum_s,
    sums_s,
    wide_s,
    below_s,
):
    step = pl.program_id(0)
    chunk, cn, cs = z.chunk, z.chunk_nodes, z.chunk_slots
    pad = 128 - cn - cs
    vec = [vec_ref[pl.ds(k, 1), :] for k in range(10)]

    @pl.when(step == 0)
    def _():
        grads_ref[...] = jnp.zeros_like(grads_ref)
        sums_s[...] = jnp.zeros_like(sums_s)
        first, second = inner_ref[0].astype(low), inner_ref[1].astype(low)
        wide_s[0] = diagonal(first, first)
        middle = second.astype(high)
        middle = (middle - jnp.mean(middle, axis=1, keepdims=True)).astype(low)
        wide_s[1] = diagonal(middle, middle)
        for k, weights in ((2, inner_ref[0]), (3, inner_ref[1]), (4, edge_entry_ref[0:128, :])):
            weights = weights.T.astype(low)
            wide_s[k] = diagonal(weights, weights)
        part = jnp.full((128, 128), 1.0 / 128.0, low)
        wide_s[5] = diagonal(part, part)
        row = lax.broadcasted_iota(jnp.int32, (128, 128), 0)
        column = lax.broadcasted_iota(jnp.int32, (128, 128), 1)
        gain = jnp.broadcast_to(vec[3] * (1.0 / 128.0), (128, 128)).T.astype(low)
        wide_s[6] = diagonal(gain, gain)
        below_s[:, :128] = jnp.where(row == column, 1.0, 0.0).astype(low)
        below_s[:, 128:] = gain

    edge_low = edge_entry_ref[...].astype(low)
    node_low = node_entry_ref[...].astype(low)
    inner_low = [None, None, inner_ref[2].astype(low), inner_ref[3].astype(low)]
    w_edge, w_slot, w_recv = edge_low[:128], edge_low[128:256], edge_low[256:]
    bias_three = vec[2] - jnp.mean(vec[2], axis=1, keepdims=True)
    gain_part = below_s[:, 128:]
    slot_pre_s[...] = dot(slot_ref[...], w_slot).astype(low)
    node_pre_s[...] = (dot(node_in_ref[...], w_recv) + vec[0]).astype(low)

    def live_rows(index, first, count):
        rows = lax.broadcasted_iota(jnp.int32, (count, 128), 0)
        return rows < count_ref[0] - (step * z.tile + index * chunk + first)

    def sides(wide):
        return wide[:, :128], wide[:, 128:]

    def chunk_rows(index):
        return pl.ds(index * chunk, chunk)

    def hot_block(block, k):
        pieces = []
        number = step * (z.tile // 128) + block
        for ref, width, count in ((slot_ids_ref, z.swin, cs), (recv_ids_ref, z.rwin, cn)):
            ids = ref[pl.ds(block, 1), :] - number * width
            band = lax.broadcasted_iota(jnp.int32, (width, 128), 0) == ids
            above, below = k * width, count - (k + 1) * width
            if above:
                pieces.append(jnp.zeros((above, 128), high))
            pieces.append(jnp.where(band, 1.0, 0.0))
            if below:
                pieces.append(jnp.zeros((below, 128), high))
        if pad:
            pieces.append(jnp.zeros((pad, 128), high))
        return jnp.concatenate(pieces, axis=0).astype(low)

    def row_pieces(count, rows):
        rows = min(count, rows)
        return [(first, first + rows) for first in range(0, count, rows)]

    def gelu_rows(pre, act_s, slope_s, base):
        for first, last in row_pieces(pre.shape[0], PIECE):
            act, slope = gelu_pair(pre[first:last].astype(low))
            act_s[pl.ds(base + first, last - first), :] = act
            slope_s[pl.ds(base + first, last - first), :] = slope

    def edge_forward(pair):
        base = pair * chunk
        wide_rows = chunk_rows(pair)
        indices = (2 * pair, 2 * pair + 1)
        for index in indices:
            for k in range(z.sub):
                block = index * z.sub + k
                hot_t = hot_block(block, k)
                pick_t[index, :, k * 128 : (k + 1) * 128] = hot_t
                pick_s[pl.ds(block * 128, 128), :] = hot_t.T
        yield
        pres = []
        for index in indices:
            tables = [
                w_edge,
                slot_pre_s[pl.ds(index * cs, cs), :],
                node_pre_s[pl.ds(index * cn, cn), :],
            ]
            if pad:
                tables.append(jnp.zeros((pad, 128), low))
            entry = jnp.concatenate(
                [edge_in_ref[chunk_rows(index), :], pick_s[chunk_rows(index), :]], axis=1
            )
            pres.append(dot(entry, jnp.concatenate(tables, axis=0)))
        yield
        gelu_rows(jnp.concatenate(pres, axis=1), act_one_s, slope_one_s, base)
        yield
        pre_two = dot(act_one_s[wide_rows, :], wide_s[0])
        yield
        bias = twice(vec[1])
        for first, last in row_pieces(chunk, PIECE):
            act, slope = gelu_pair((pre_two[first:last] + bias).astype(low))
            act_two_s[pl.ds(base + first, last - first), :] = act
            slope_two_s[pl.ds(base + first, last - first), :] = slope
        yield
        pre_three = dot(act_two_s[wide_rows, :], wide_s[1])
        yield
        for side, index in enumerate(indices):
            half = pre_three[:, side * 128 : (side + 1) * 128]
            for first, last in row_pieces(chunk, PIECE_NORM):
                rows = pl.ds(index * chunk + first, last - first)
                live = live_rows(index, first, last - first)
                center = half[first:last] + bias_three
                inverse = lax.rsqrt(jnp.mean(center * center, axis=1, keepdims=True) + eps_norm)
                inverse = jnp.where(live, inverse, 0.0)
                normed = center * inverse
                normed_s[rows, :] = normed
                inverse_s[rows, :] = inverse
                message = jnp.where(live, normed * vec[3] + vec[4], 0.0)
                edge_out_ref[rows, :] = (edge_in_ref[rows, :].astype(high) + message).astype(low)
                message_s[
                    pl.ds(base + first, last - first), side * 128 : (side + 1) * 128
                ] = message.astype(low)
            yield
        hots = [pick_t[index, cs : cs + cn, :] for index in indices]
        total = dot(jnp.concatenate(hots, axis=0), message_s[wide_rows, :]).astype(low)
        gathered_s[pl.ds(indices[0] * cn, cn), :] = total[:cn, :128]
        gathered_s[pl.ds(indices[1] * cn, cn), :] = total[cn:, 128:]
        yield

    def node_phase(group):
        base = group * z.group_nodes
        rows = pl.ds(base, z.group_nodes)
        parts = row_pieces(z.group_nodes, PIECE)

        def here(first, last):
            return pl.ds(base + first, last - first)

        entry = jnp.concatenate([node_in_ref[rows, :], gathered_s[rows, :]], axis=1)
        pre = dot(entry, node_low)
        yield
        for first, last in parts:
            act, slope = gelu_pair((pre[first:last] + vec[5]).astype(low))
            node_act_s[0, here(first, last), :] = act
            node_slope_s[0, here(first, last), :] = slope
        yield
        pre = dot(node_act_s[0, rows, :], inner_low[2])
        yield
        for first, last in parts:
            act, slope = gelu_pair((pre[first:last] + vec[6]).astype(low))
            node_act_s[1, here(first, last), :] = act
            node_slope_s[1, here(first, last), :] = slope
        yield
        pre = dot(node_act_s[1, rows, :], inner_low[3])
        yield
        for first, last in parts:
            piece = here(first, last)
            value = pre[first:last] + vec[7]
            center = value - jnp.mean(value, axis=1, keepdims=True)
            inverse = lax.rsqrt(jnp.mean(center * center, axis=1, keepdims=True) + eps_norm)
            normed = center * inverse
            node_out_ref[piece, :] = (
                node_in_ref[piece, :].astype(high) + normed * vec[8] + vec[9]
            ).astype(low)
            upstream = node_cot_ref[piece, :].astype(high)
            sums_s[8] += fold_rows(upstream * normed)
            sums_s[9] += fold_rows(upstream)
            upper = upstream * vec[8]
            mean_plain = jnp.mean(upper, axis=1, keepdims=True)
            mean_cross = jnp.mean(upper * normed, axis=1, keepdims=True)
            d_three = inverse * (upper - mean_plain - normed * mean_cross)
            sums_s[7] += fold_rows(d_three)
            node_back_s[2, piece, :] = d_three.astype(low)
        yield
        for k in (1, 0):
            back = dot_nt(node_back_s[k + 1, rows, :], inner_low[2 + k])
            yield
            for first, last in parts:
                piece = here(first, last)
                value = back[first:last] * node_slope_s[k, piece, :].astype(high)
                sums_s[5 + k] += fold_rows(value)
                node_back_s[k, piece, :] = value.astype(low)
            yield
        back = dot_nt(node_back_s[0, rows, :], node_low)
        for first, last in parts:
            piece = here(first, last)
            node_grad_ref[piece, :] = node_cot_ref[piece, :].astype(high) + back[first:last, :128]
            table_s[piece, :128] = back[first:last, 128:].astype(low)
        yield
        table_s[rows, 128:] = dot(table_s[rows, :128], gain_part).astype(low)
        yield
        grads_ref[384:640, :] += dot_tn(entry, node_back_s[0, rows, :])
        grads_ref[896:1024, :] += dot_tn(node_act_s[0, rows, :], node_back_s[1, rows, :])
        grads_ref[1024:1152, :] += dot_tn(node_act_s[1, rows, :], node_back_s[2, rows, :])
        yield

    def edge_backward(pair):
        base = pair * chunk
        wide_rows = chunk_rows(pair)
        indices = (2 * pair, 2 * pair + 1)
        for side, index in enumerate(indices):
            tables = [
                jnp.zeros((cs, 256), low),
                table_s[pl.ds(index * cn, cn), :],
            ]
            if pad:
                tables.append(jnp.zeros((pad, 256), low))
            tables.append(below_s[...])
            entry = jnp.concatenate(
                [pick_s[chunk_rows(index), :], edge_cot_ref[chunk_rows(index), :]], axis=1
            )
            arrived = dot(entry, jnp.concatenate(tables, axis=0))
            yield
            gain_sum = jnp.zeros((8, 128), high)
            shift_sum = jnp.zeros((8, 128), high)
            for first, last in row_pieces(chunk, PIECE_NORM):
                rows = pl.ds(index * chunk + first, last - first)
                upstream, plain = sides(arrived[first:last])
                normed = normed_s[rows, :]
                cross = upstream * normed
                gain_sum = gain_sum + fold_rows(cross)
                live = live_rows(index, first, last - first)
                shift_sum = shift_sum + fold_rows(jnp.where(live, upstream, 0.0))
                cross = jnp.mean(cross * vec[3], axis=1, keepdims=True)
                d_three = inverse_s[rows, :] * (upstream * vec[3] - plain - normed * cross)
                message_s[
                    pl.ds(base + first, last - first), side * 128 : (side + 1) * 128
                ] = d_three.astype(low)
            sums_s[3] += gain_sum
            sums_s[4] += shift_sum
            yield
        for gradient_s, slope_s, weights in ((message_s, slope_two_s, 3), (slope_two_s, slope_one_s, 2)):
            back = dot(gradient_s[wide_rows, :], wide_s[weights])
            yield
            for first, last in row_pieces(chunk, PIECE):
                rows = pl.ds(base + first, last - first)
                slope_s[rows, :] = back[first:last].astype(low) * slope_s[rows, :]
            yield
        back = dot(slope_one_s[wide_rows, :], wide_s[4])
        yield
        for index, half in zip(indices, sides(back)):
            for first, last in row_pieces(chunk, PIECE):
                rows = pl.ds(index * chunk + first, last - first)
                edge_grad_ref[rows, :] = edge_cot_ref[rows, :].astype(high) + half[first:last]
        yield
        ones = jnp.ones((16, chunk), low)
        entry = [edge_in_ref[chunk_rows(index), :].T for index in indices]
        hots = [pick_t[index, : cs + cn, :] for index in indices]
        total = dot(jnp.concatenate(entry + hots, axis=0), slope_one_s[wide_rows, :])
        grads_ref[0:128, :] += total[:128, :128] + total[128:256, 128:]
        first = total[256 : 256 + cs + cn, :128]
        second = total[256 + cs + cn :, 128:]
        node_rows = pl.ds(pair * z.pair_nodes, z.pair_nodes)
        slot_rows = pl.ds(pair * z.pair_slots, z.pair_slots)
        slot_sum_s[slot_rows, :] = jnp.concatenate([first[:cs], second[:cs]], axis=0).astype(low)
        recv_sum = jnp.concatenate([first[cs:], second[cs:]], axis=0)
        sums_s[0] += fold_rows(recv_sum)
        recv_sum_s[node_rows, :] = recv_sum.astype(low)
        yield
        for k, act_s, gradient_s in ((1, act_one_s, slope_two_s), (2, act_two_s, message_s)):
            total = dot(
                jnp.concatenate([act_s[wide_rows, :].T, ones], axis=0), gradient_s[wide_rows, :]
            )
            grads_ref[pl.ds(512 + 128 * k, 128), :] += total[:128, :128] + total[128:256, 128:]
            sums_s[k] += (total[256:264, :128] + total[256:264, 128:]) * 0.125
            yield

    def group_end(group):
        node_rows = pl.ds(group * z.group_nodes, z.group_nodes)
        slot_rows = pl.ds(group * z.group_slots, z.group_slots)
        slot_grad_ref[slot_rows, :] = dot_nt(slot_sum_s[slot_rows, :], w_slot).astype(low)
        node_grad_ref[node_rows, :] += dot_nt(recv_sum_s[node_rows, :], w_recv)
        yield
        grads_ref[128:256, :] += dot_tn(slot_ref[slot_rows, :], slot_sum_s[slot_rows, :])
        grads_ref[256:384, :] += dot_tn(node_in_ref[node_rows, :], recv_sum_s[node_rows, :])
        yield

    emit(z.pairs, z.per_group, edge_forward, node_phase, edge_backward, group_end)

    @pl.when(step == z.steps - 1)
    def _():
        grads_ref[1152:1162, :] = jnp.sum(sums_s[...], axis=1)


def layer_call(z, count, slot_ids, recv_ids, edge_in, edge_cot, node_in, node_cot, slot_rows, weights):
    def rows_spec(rows):
        return pl.BlockSpec((rows, 128), lambda i: (i, 0))

    def whole(array):
        return pl.BlockSpec(array.shape, lambda i: (0,) * array.ndim)

    return pl.pallas_call(
        functools.partial(layer_kernel, z),
        grid=(z.steps,),
        in_specs=[
            pl.BlockSpec(memory_space=pltpu.SMEM),
            rows_spec(z.tile // 128),
            rows_spec(z.tile // 128),
            rows_spec(z.tile),
            rows_spec(z.tile),
            rows_spec(z.tile_nodes),
            rows_spec(z.tile_nodes),
            rows_spec(z.tile_slots),
        ]
        + [whole(w) for w in weights],
        out_specs=[
            rows_spec(z.tile_nodes),
            rows_spec(z.tile),
            rows_spec(z.tile_nodes),
            rows_spec(z.tile),
            rows_spec(z.tile_slots),
            pl.BlockSpec((z.grad_rows, 128), lambda i: (0, 0)),
        ],
        out_shape=[
            jax.ShapeDtypeStruct((z.nodes, 128), low),
            jax.ShapeDtypeStruct((z.edges, 128), low),
            jax.ShapeDtypeStruct((z.nodes, 128), high),
            jax.ShapeDtypeStruct((z.edges, 128), high),
            jax.ShapeDtypeStruct((z.slots, 128), low),
            jax.ShapeDtypeStruct((z.grad_rows, 128), high),
        ],
        scratch_shapes=[
            pltpu.VMEM((z.tile, 128), low),
            pltpu.VMEM((z.tile_chunks, 128, z.chunk), low),
            pltpu.VMEM((z.tile // 2, 256), low),
            pltpu.VMEM((z.tile // 2, 256), low),
            pltpu.VMEM((z.tile // 2, 256), low),
            pltpu.VMEM((z.tile // 2, 256), low),
            pltpu.VMEM((z.tile, 128), high),
            pltpu.VMEM((z.tile, 128), high),
            pltpu.VMEM((z.tile // 2, 256), low),
            pltpu.VMEM((2, z.tile_nodes, 128), low),
            pltpu.VMEM((2, z.tile_nodes, 128), low),
            pltpu.VMEM((3, z.tile_nodes, 128), low),
            pltpu.VMEM((z.tile_nodes, 128), low),
            pltpu.VMEM((z.tile_nodes, 256), low),
            pltpu.VMEM((z.tile_slots, 128), low),
            pltpu.VMEM((z.tile_nodes, 128), low),
            pltpu.VMEM((z.tile_slots, 128), low),
            pltpu.VMEM((z.tile_nodes, 128), low),
            pltpu.VMEM((10, 8, 128), high),
            pltpu.VMEM((7, 256, 256), low),
            pltpu.VMEM((128, 256), low),
        ],
        compiler_params=pltpu.CompilerParams(
            dimension_semantics=("arbitrary",), vmem_limit_bytes=VMEM
        ),
        name="layer",
    )(count, slot_ids, recv_ids, edge_in, edge_cot, node_in, node_cot, slot_rows, *weights)


def signal(semaphore, where):
    pl.semaphore_signal(semaphore, inc=1, device_id=where, device_id_type=pl.DeviceIdType.MESH)


def send(source, target, send_sem, recv_sem, where):
    copy = pltpu.make_async_remote_copy(
        src_ref=source,
        dst_ref=target,
        send_sem=send_sem,
        recv_sem=recv_sem,
        device_id=where,
        device_id_type=pl.DeviceIdType.MESH,
    )
    copy.start()
    return copy


def fetch_kernel(
    peers,
    unroll,
    request_ref,
    node_ref,
    rows_ref,
    asked_ref,
    wanted_v,
    asked_v,
    node_v,
    node_s,
    picked_s,
    out_s,
    ask_send,
    ask_recv,
    row_send,
    row_recv,
    load_sem,
):
    me = lax.axis_index("dom")
    slots = picked_s.shape[0]
    barrier = pltpu.get_barrier_semaphore()
    for k in range(1, peers):
        signal(barrier, {"dom": lax.rem(me + k, peers)})
    loads = [
        pltpu.make_async_copy(request_ref, wanted_v, load_sem.at[0]),
        pltpu.make_async_copy(node_ref, node_v, load_sem.at[1]),
    ]
    for load in loads:
        load.start()
    loads[0].wait()
    for k in range(peers):
        asked_v[k] = wanted_v[pl.ds(k, 1), :]
    loads[1].wait()
    node_s[...] = node_v[...].astype(high)
    pl.semaphore_wait(barrier, peers - 1)
    shifts = [peers // 2 + (k // 2) * (1 - 2 * (k % 2)) for k in range(1, peers)]
    asks = [
        send(
            asked_v.at[lax.rem(me + k, peers)],
            asked_v.at[peers + me],
            ask_send.at[k],
            ask_recv.at[k],
            {"dom": lax.rem(me + k, peers)},
        )
        for k in shifts
    ]
    asked_v[peers + me] = asked_v[me]
    for ask in asks:
        ask.wait_recv()
    local = pltpu.make_async_copy(asked_v.at[pl.ds(peers, peers)], asked_ref, load_sem.at[0])
    local.start()
    local.wait()
    sends = []
    for k in shifts + [0]:
        other = lax.rem(me + (peers - k), peers)

        @pl.loop(0, slots // unroll)
        def _(group):
            for place in range(unroll):
                row = group * unroll + place
                index = asked_ref[other, 0, row]
                picked_s[pl.ds(row, 1), :] = node_s[pl.ds(index, 1), :]

        out_s[other] = picked_s[...].astype(low)
        if k:
            sends.append(
                send(
                    out_s.at[other],
                    rows_ref.at[me],
                    row_send.at[k],
                    row_recv.at[k],
                    {"dom": other},
                )
            )
    local = pltpu.make_async_copy(out_s.at[me], rows_ref.at[me], load_sem.at[0])
    local.start()
    for copy in asks:
        copy.wait_send()
    local.wait()
    for copy in sends:
        copy.wait()


def fetch_call(peers, request, node_in):
    slots = request.shape[2]
    dma = pltpu.SemaphoreType.DMA
    hbm = pl.BlockSpec(memory_space=pltpu.HBM)
    return pl.pallas_call(
        functools.partial(fetch_kernel, peers, 32),
        in_specs=[hbm, hbm],
        out_specs=[hbm, pl.BlockSpec(memory_space=pltpu.SMEM)],
        out_shape=[
            jax.ShapeDtypeStruct((peers, slots, 128), low),
            jax.ShapeDtypeStruct((peers, 1, slots), jnp.int32),
        ],
        scratch_shapes=[
            pltpu.VMEM((peers, slots), jnp.int32),
            pltpu.VMEM((2 * peers, 1, slots), jnp.int32),
            pltpu.VMEM(node_in.shape, low),
            pltpu.VMEM(node_in.shape, high),
            pltpu.VMEM((slots, 128), high),
            pltpu.VMEM((peers, slots, 128), low),
            dma((peers,)),
            dma((peers,)),
            dma((peers,)),
            dma((peers,)),
            dma((2,)),
        ],
        compiler_params=pltpu.CompilerParams(
            collective_id=0, has_side_effects=True, vmem_limit_bytes=VMEM
        ),
        name="fetch",
    )(request.reshape(peers, slots), node_in)


def reduce_kernel(
    groups,
    peers,
    grads_ref,
    slot_grad_ref,
    sum_ref,
    back_ref,
    grads_s,
    all_s,
    half_out,
    half_in,
    half_sum,
    quarter_out,
    quarter_in,
    quarter_sum,
    piece_out,
    piece_in,
    back_send,
    back_recv,
    half_send,
    half_recv,
    quarter_send,
    quarter_recv,
    piece_send,
    piece_recv,
    load_sem,
):
    grp, dom = lax.axis_index("grp"), lax.axis_index("dom")
    core, level = lax.rem(dom, 2), lax.div(dom, 2)
    levels = peers // 2
    half, quarter, piece = half_sum.shape[0], quarter_sum.shape[0], piece_out.shape[1]
    barrier = pltpu.get_barrier_semaphore()
    for k in range(1, peers):
        signal(barrier, {"dom": lax.rem(dom + k, peers)})
    for k in range(1, groups):
        signal(barrier, {"grp": lax.rem(grp + k, groups)})
    twin = {"dom": 2 * level + 1 - core}
    loads = [
        pltpu.make_async_copy(
            grads_ref.at[pl.ds(first, half), :], grads_s.at[pl.ds(first, half), :], load_sem.at[k]
        )
        for k, first in enumerate(((1 - core) * half, core * half))
    ]
    loads.append(
        pltpu.make_async_copy(slot_grad_ref.at[dom], back_ref.at[dom], load_sem.at[2])
    )
    for load in loads:
        load.start()
    loads[0].wait()
    half_out[...] = grads_s[pl.ds((1 - core) * half, half), :].astype(low)
    loads[1].wait()
    pl.semaphore_wait(barrier, peers - 1 + groups - 1)

    sends = [send(half_out, half_in, half_send.at[0], half_recv.at[0], twin)]

    def give_back(k):
        other = lax.rem(dom + k, peers)
        return send(
            slot_grad_ref.at[other],
            back_ref.at[dom],
            back_send.at[k],
            back_recv.at[k],
            {"dom": other},
        )

    early = [k for k in range(1, peers) if 2 * k == peers or (2 * k < peers and k % 2)]
    backs = [give_back(k) for k in early]
    sends[0].wait_recv()
    half_sum[...] = grads_s[pl.ds(core * half, half), :] + half_in[...].astype(high)

    copies = []
    for k in range(1, groups):
        other = lax.rem(grp + k, groups)
        quarter_out[k] = half_sum[pl.ds(other * quarter, quarter), :].astype(low)
        copies.append(
            send(
                quarter_out.at[k],
                quarter_in.at[k],
                quarter_send.at[k],
                quarter_recv.at[k],
                {"grp": other},
            )
        )
    total = half_sum[pl.ds(grp * quarter, quarter), :]
    for k in range(1, groups):
        copies[k - 1].wait_recv()
        total = total + quarter_in[k].astype(high)
    quarter_sum[...] = total
    sends += copies

    copies = []
    for k in range(1, levels):
        other = lax.rem(level + k, levels)
        piece_out[k] = quarter_sum[pl.ds(other * piece, piece), :].astype(low)
        copies.append(
            send(
                piece_out.at[k],
                piece_in.at[k],
                piece_send.at[k],
                piece_recv.at[k],
                {"dom": 2 * other + core},
            )
        )
    total = quarter_sum[pl.ds(level * piece, piece), :]
    for k in range(1, levels):
        copies[k - 1].wait_recv()
        total = total + piece_in[k].astype(high)
    sends += copies

    own_half = core * half
    own_quarter = own_half + grp * quarter
    own_piece = own_quarter + level * piece
    all_s[pl.ds(own_piece, piece), :] = total.astype(low)
    copies = []
    for k in range(1, levels):
        place = all_s.at[pl.ds(own_piece, piece), :]
        where = {"dom": 2 * lax.rem(level + k, levels) + core}
        copies.append(
            send(place, place, piece_send.at[levels + k], piece_recv.at[levels + k], where)
        )
    backs += [give_back(k) for k in range(1, peers) if k not in early]
    for copy in copies:
        copy.wait_recv()
    sends += copies
    copies = []
    for k in range(1, groups):
        place = all_s.at[pl.ds(own_quarter, quarter), :]
        where = {"grp": lax.rem(grp + k, groups)}
        copies.append(
            send(place, place, quarter_send.at[groups + k], quarter_recv.at[groups + k], where)
        )
    for copy in copies:
        copy.wait_recv()
    sends += copies
    place = all_s.at[pl.ds(own_half, half), :]
    copy = send(place, place, half_send.at[1], half_recv.at[1], twin)
    copy.wait_recv()
    sends.append(copy)
    loads[2].wait()
    for copy in backs:
        copy.wait()
    for copy in sends:
        copy.wait_send()
    sum_ref[...] = all_s[...]


def reduce_call(groups, peers, grads, slot_grad):
    rows = grads.shape[0]
    levels = peers // 2
    half, quarter, piece = rows // 2, rows // 2 // groups, rows // 2 // groups // levels
    dma = pltpu.SemaphoreType.DMA
    return pl.pallas_call(
        functools.partial(reduce_kernel, groups, peers),
        in_specs=[pl.BlockSpec(memory_space=pltpu.HBM)] * 2,
        out_specs=[
            pl.BlockSpec(memory_space=pltpu.VMEM),
            pl.BlockSpec(memory_space=pltpu.HBM),
        ],
        out_shape=[
            jax.ShapeDtypeStruct((rows, 128), low),
            jax.ShapeDtypeStruct(slot_grad.shape, low),
        ],
        scratch_shapes=[
            pltpu.VMEM((rows, 128), high),
            pltpu.VMEM((rows, 128), low),
            pltpu.VMEM((half, 128), low),
            pltpu.VMEM((half, 128), low),
            pltpu.VMEM((half, 128), high),
            pltpu.VMEM((groups, quarter, 128), low),
            pltpu.VMEM((groups, quarter, 128), low),
            pltpu.VMEM((quarter, 128), high),
            pltpu.VMEM((levels, piece, 128), low),
            pltpu.VMEM((levels, piece, 128), low),
            dma((peers,)),
            dma((peers,)),
            dma((2,)),
            dma((2,)),
            dma((2 * groups,)),
            dma((2 * groups,)),
            dma((2 * levels,)),
            dma((2 * levels,)),
            dma((3,)),
        ],
        compiler_params=pltpu.CompilerParams(
            collective_id=1, has_side_effects=True, vmem_limit_bytes=VMEM
        ),
        name="reduce",
    )(grads, slot_grad)


def adamw_step(master, moment_mean, moment_var, average, gradient, factor):
    clipped = gradient * factor
    mean_new = beta_one * moment_mean + (1.0 - beta_one) * clipped
    var_new = beta_two * moment_var + (1.0 - beta_two) * clipped * clipped
    mean_hat = mean_new / (1.0 - beta_one**STEP)
    var_hat = var_new / (1.0 - beta_two**STEP)
    updated = master - learn_rate * (
        mean_hat / (jnp.sqrt(var_hat) + adam_eps) + decay_rate * master
    )
    return (
        mean_new,
        var_new,
        updated,
        updated.astype(low),
        ema_keep * average + (1.0 - ema_keep) * updated,
    )


FIRST = (0, 384, 640, 1152, 1162)


def finish_kernel(unroll, asked_ref, *refs):
    sources, (norm_ref, *results), refs = refs[:19], refs[19:41], refs[41:]
    loaded, (rows_s, *staged, load_sem, store_sem) = refs[:19], refs[19:]
    summed_s, back_s, node_s = loaded[16:]
    loads = [
        pltpu.make_async_copy(source, place, load_sem.at[k])
        for k, (source, place) in enumerate(zip(sources, loaded))
    ]
    for load in [*loads[17:], loads[16], *loads[:16]]:
        load.start()
    loads[17].wait()
    rows_s[...] = back_s[...].astype(high)
    slots = asked_ref.shape[2]
    loads[18].wait()

    @pl.loop(0, rows_s.shape[0] // unroll)
    def _(group):
        base = group * unroll
        peer, first = lax.div(base, slots), lax.rem(base, slots)
        places = [pl.ds(asked_ref[peer, 0, first + k], 1) for k in range(unroll)]
        values = [
            node_s[place, :] + rows_s[pl.ds(base + k, 1), :] for k, place in enumerate(places)
        ]
        for place, value in zip(places, values):
            node_s[place, :] = value

    stores = [pltpu.make_async_copy(node_s, results[20], store_sem.at[20])]
    stores[0].start()
    for load in loads[:17]:
        load.wait()
    gradient = summed_s[...].astype(high)
    square = jnp.sum(gradient * gradient, axis=0, keepdims=True)
    grad_norm = jnp.sqrt(jnp.sum(square, axis=1, keepdims=True))
    norm_ref[0] = grad_norm[0, 0]
    factor = clip_level / jnp.maximum(grad_norm, clip_level)
    for k in range(4):
        values = [place[...] for place in loaded[4 * k : 4 * k + 4]]
        updates = adamw_step(*values, gradient[FIRST[k] : FIRST[k + 1]], factor)
        for place, value in enumerate(updates):
            place += 5 * k
            staged[place][...] = value
            store = pltpu.make_async_copy(staged[place], results[place], store_sem.at[place])
            store.start()
            stores.append(store)
    for store in stores:
        store.wait()


def finish_call(asked, part, back, summed, tensors):
    smem = pl.BlockSpec(memory_space=pltpu.SMEM)
    hbm = pl.BlockSpec(memory_space=pltpu.HBM)
    sources = [*tensors, summed, back, part]
    shapes = []
    for k in range(4):
        shape = tensors[4 * k].shape
        shapes += [jax.ShapeDtypeStruct(shape, kind) for kind in (high, high, high, low, high)]
    return pl.pallas_call(
        functools.partial(finish_kernel, 32),
        in_specs=[smem] + [hbm] * 19,
        out_specs=[smem] + [hbm] * 21,
        out_shape=[
            jax.ShapeDtypeStruct((1,), high),
            *shapes,
            jax.ShapeDtypeStruct(part.shape, high),
        ],
        scratch_shapes=[
            *[pltpu.VMEM(item.shape, item.dtype) for item in sources],
            pltpu.VMEM(back.shape, high),
            *[pltpu.VMEM(item.shape, item.dtype) for item in shapes],
            pltpu.SemaphoreType.DMA((19,)),
            pltpu.SemaphoreType.DMA((21,)),
        ],
        compiler_params=pltpu.CompilerParams(vmem_limit_bytes=VMEM),
        name="finish",
    )(asked, *sources)


def shards(
    node_in,
    edge_in,
    edge_slot,
    edge_receiver,
    edge_count,
    request,
    node_cot,
    edge_cot,
    *tensors,
):
    groups, peers = lax.axis_size("grp"), lax.axis_size("dom")
    slots = request.shape[2]
    z = Sizes(edge_in.shape[0], node_in.shape[0], peers * slots, groups * peers)
    slot_rows, asked = fetch_call(peers, request, node_in)
    node_out, edge_out, node_part, edge_grad, slot_grad, grads = layer_call(
        z,
        edge_count,
        edge_slot.reshape(-1, 128),
        edge_receiver.reshape(-1, 128),
        edge_in,
        edge_cot,
        node_in,
        node_cot,
        slot_rows.reshape(peers * slots, 128),
        tensors[::4],
    )
    summed, returned = reduce_call(groups, peers, grads, slot_grad.reshape(peers, slots, 128))
    flat = [tensor.reshape(-1, 128) for tensor in tensors]
    grad_norm, *results, node_grad = finish_call(
        asked, node_part, returned.reshape(peers * slots, 128), summed, flat
    )
    results = [value.reshape(tensors[k // 5 * 4].shape) for k, value in enumerate(results)]
    return (node_out, edge_out, node_grad, edge_grad, grad_norm.reshape(()), *results)


def solution(mesh):
    rows = P(("grp", "dom"), None)
    in_specs = (
        rows,
        rows,
        P(("grp", "dom")),
        P(("grp", "dom")),
        P(("grp", "dom")),
        P(("grp", "dom"), None, None),
        rows,
        rows,
    ) + (P(),) * 16
    out_specs = (rows,) * 4 + (P(),) * 21
    return jax.shard_map(shards, mesh=mesh, in_specs=in_specs, out_specs=out_specs, check_vma=False)
```

```python
import functools
import math

import jax
import jax.numpy as jnp
from jax import lax
from jax.experimental import pallas as pl
from jax.experimental.pallas import tpu as pltpu
from jax.sharding import PartitionSpec as P

STEP = 10

eps_norm = 1e-05
beta_one = 0.5
beta_two = 0.6
learn_rate = 0.08
decay_rate = 0.01
adam_eps = 1e-08
ema_keep = 0.9
clip_level = 1.0

gelu_in = math.sqrt(2.0 / math.pi)
gelu_cube = gelu_in * 0.044715

low = jnp.bfloat16
high = jnp.float32

GAP = 2
PIECE = 64
PIECE_NORM = 32
VMEM = 60 * 1024 * 1024
PAIRS = 8


def dot(operand, weights):
    return jnp.dot(operand, weights, preferred_element_type=high)


def dot_nt(operand, weights):
    return lax.dot_general(
        operand, weights, (((1,), (1,)), ((), ())), preferred_element_type=high
    )


def dot_tn(operand, weights):
    return lax.dot_general(
        operand, weights, (((0,), (0,)), ((), ())), preferred_element_type=high
    )


def gelu_pair(x):
    square = x * x
    u = x * (gelu_in + gelu_cube * square)
    s = 0.5 + 0.5 * jnp.tanh(u)
    value = x * s
    slope = s + (value - value * s) * (2.0 * gelu_in + (6.0 * gelu_cube) * square)
    return value, slope


def fold_rows(values):
    return jnp.sum(values.reshape(values.shape[0] // 8, 8, values.shape[1]), axis=0)


def emit(pairs, per_group, forward, middle, backward, end):
    groups = pairs // per_group
    streams = {"forward": forward, "middle": middle, "backward": backward, "end": end}
    started = dict.fromkeys(streams, 0)
    last = dict.fromkeys(streams, -GAP)
    active, done, now = [], set(), 0

    def ready(name, k):
        if name == "middle":
            return all(("forward", k * per_group + j) in done for j in range(per_group))
        if name == "end":
            return all(("backward", k * per_group + j) in done for j in range(per_group))
        return name == "forward" or ("middle", k // per_group) in done

    while len(done) < 2 * pairs + 2 * groups:
        for name in streams:
            k = started[name]
            count = pairs if name in ("forward", "backward") else groups
            if k < count and now - last[name] >= GAP and ready(name, k):
                active.append(((name, k), streams[name](k)))
                started[name], last[name] = k + 1, now
        for item in list(active):
            try:
                next(item[1])
            except StopIteration:
                active.remove(item)
                done.add(item[0])
        now += 1


class Sizes:
    def __init__(self, edges, nodes, slots, devices):
        self.edges, self.nodes, self.slots = edges, nodes, slots
        blocks = edges // 128
        self.rwin = nodes // blocks
        self.swin = slots // blocks
        self.sub = 4
        while self.sub * (self.rwin + self.swin) > 128:
            self.sub //= 2
        self.chunk = self.sub * 128
        self.chunk_slots = self.sub * self.swin
        self.chunk_nodes = self.sub * self.rwin
        self.pair_nodes, self.pair_slots = 2 * self.chunk_nodes, 2 * self.chunk_slots
        self.per_group = 4
        self.pairs = PAIRS
        self.group_nodes = self.per_group * self.pair_nodes
        self.group_slots = self.per_group * self.pair_slots
        self.tile = self.pairs * 2 * self.chunk
        self.tile_chunks = 2 * self.pairs
        self.tile_nodes = self.pairs * self.pair_nodes
        self.tile_slots = self.pairs * self.pair_slots
        self.tiles = edges // self.tile
        self.grad_rows = -(-1162 // (16 * devices)) * 16 * devices


def diagonal(first, second):
    zero_a = jnp.zeros((first.shape[0], second.shape[1]), first.dtype)
    zero_b = jnp.zeros((second.shape[0], first.shape[1]), first.dtype)
    return jnp.concatenate(
        [
            jnp.concatenate([first, zero_a], axis=1),
            jnp.concatenate([zero_b, second], axis=1),
        ],
        axis=0,
    )


def twice(row):
    return jnp.concatenate([row, row], axis=1)


def prepare(edge_entry_ref, inner_ref, vec_ref, sums_s, wide_s, below_s):
    sums_s[...] = jnp.zeros_like(sums_s)
    first, second = inner_ref[0].astype(low), inner_ref[1].astype(low)
    wide_s[0] = diagonal(first, first)
    middle = second.astype(high)
    middle = (middle - jnp.mean(middle, axis=1, keepdims=True)).astype(low)
    wide_s[1] = diagonal(middle, middle)
    for k, weights in ((2, inner_ref[0]), (3, inner_ref[1]), (4, edge_entry_ref[0:128, :])):
        weights = weights.T.astype(low)
        wide_s[k] = diagonal(weights, weights)
    row = lax.broadcasted_iota(jnp.int32, (128, 128), 0)
    column = lax.broadcasted_iota(jnp.int32, (128, 128), 1)
    gain = jnp.broadcast_to(vec_ref[pl.ds(3, 1), :] * (1.0 / 128.0), (128, 128)).T.astype(low)
    below_s[:, :128] = jnp.where(row == column, 1.0, 0.0).astype(low)
    below_s[:, 128:] = gain


def close_sums(grads_ref, sums_s):
    grads_ref[1152:1162, :] += jnp.sum(sums_s[...], axis=1)


def layer_tile(
    z,
    tile,
    count_ref,
    slot_ids_ref,
    recv_ids_ref,
    edge_in_ref,
    edge_cot_ref,
    node_in_ref,
    node_cot_ref,
    slot_ref,
    edge_entry_ref,
    node_entry_ref,
    inner_ref,
    vec_ref,
    node_out_ref,
    edge_out_ref,
    node_grad_ref,
    edge_grad_ref,
    slot_grad_ref,
    grads_ref,
    sums_s,
    wide_s,
    below_s,
    pick_s,
    pick_t,
    act_one_s,
    act_two_s,
    slope_one_s,
    slope_two_s,
    normed_s,
    inverse_s,
    message_s,
    node_act_s,
    node_slope_s,
    node_back_s,
    gathered_s,
    table_s,
    slot_pre_s,
    node_pre_s,
    slot_sum_s,
    recv_sum_s,
):
    chunk, cn, cs = z.chunk, z.chunk_nodes, z.chunk_slots
    pad = 128 - cn - cs
    vec = [vec_ref[pl.ds(k, 1), :] for k in range(10)]
    edge_low = edge_entry_ref[...].astype(low)
    node_low = node_entry_ref[...].astype(low)
    inner_low = [None, None, inner_ref[2].astype(low), inner_ref[3].astype(low)]
    w_edge, w_slot, w_recv = edge_low[:128], edge_low[128:256], edge_low[256:]
    bias_three = vec[2] - jnp.mean(vec[2], axis=1, keepdims=True)
    gain_part = below_s[:, 128:]
    slot_pre_s[...] = dot(slot_ref[...], w_slot).astype(low)
    node_pre_s[...] = (dot(node_in_ref[...], w_recv) + vec[0]).astype(low)

    def live_rows(index, first, count):
        rows = lax.broadcasted_iota(jnp.int32, (count, 128), 0)
        return rows < count_ref[0] - (tile * z.tile + index * chunk + first)

    def sides(wide):
        return wide[:, :128], wide[:, 128:]

    def chunk_rows(index):
        return pl.ds(index * chunk, chunk)

    def hot_block(block, k):
        pieces = []
        number = tile * (z.tile // 128) + block
        for ref, width, count in ((slot_ids_ref, z.swin, cs), (recv_ids_ref, z.rwin, cn)):
            ids = ref[pl.ds(block, 1), :] - number * width
            band = lax.broadcasted_iota(jnp.int32, (width, 128), 0) == ids
            above, below = k * width, count - (k + 1) * width
            if above:
                pieces.append(jnp.zeros((above, 128), high))
            pieces.append(jnp.where(band, 1.0, 0.0))
            if below:
                pieces.append(jnp.zeros((below, 128), high))
        if pad:
            pieces.append(jnp.zeros((pad, 128), high))
        return jnp.concatenate(pieces, axis=0).astype(low)

    def row_pieces(count, rows):
        rows = min(count, rows)
        return [(first, first + rows) for first in range(0, count, rows)]

    def gelu_rows(pre, act_s, slope_s, base):
        for first, last in row_pieces(pre.shape[0], PIECE):
            act, slope = gelu_pair(pre[first:last].astype(low))
            act_s[pl.ds(base + first, last - first), :] = act
            slope_s[pl.ds(base + first, last - first), :] = slope

    def edge_forward(pair):
        base = pair * chunk
        wide_rows = chunk_rows(pair)
        indices = (2 * pair, 2 * pair + 1)
        for index in indices:
            for k in range(z.sub):
                block = index * z.sub + k
                hot_t = hot_block(block, k)
                pick_t[index, :, k * 128 : (k + 1) * 128] = hot_t
                pick_s[pl.ds(block * 128, 128), :] = hot_t.T
        yield
        pres = []
        for index in indices:
            tables = [
                w_edge,
                slot_pre_s[pl.ds(index * cs, cs), :],
                node_pre_s[pl.ds(index * cn, cn), :],
            ]
            if pad:
                tables.append(jnp.zeros((pad, 128), low))
            entry = jnp.concatenate(
                [edge_in_ref[chunk_rows(index), :], pick_s[chunk_rows(index), :]], axis=1
            )
            pres.append(dot(entry, jnp.concatenate(tables, axis=0)))
        yield
        gelu_rows(jnp.concatenate(pres, axis=1), act_one_s, slope_one_s, base)
        yield
        pre_two = dot(act_one_s[wide_rows, :], wide_s[0])
        yield
        bias = twice(vec[1])
        for first, last in row_pieces(chunk, PIECE):
            act, slope = gelu_pair((pre_two[first:last] + bias).astype(low))
            act_two_s[pl.ds(base + first, last - first), :] = act
            slope_two_s[pl.ds(base + first, last - first), :] = slope
        yield
        pre_three = dot(act_two_s[wide_rows, :], wide_s[1])
        yield
        for side, index in enumerate(indices):
            half = pre_three[:, side * 128 : (side + 1) * 128]
            for first, last in row_pieces(chunk, PIECE_NORM):
                rows = pl.ds(index * chunk + first, last - first)
                live = live_rows(index, first, last - first)
                center = half[first:last] + bias_three
                inverse = lax.rsqrt(jnp.mean(center * center, axis=1, keepdims=True) + eps_norm)
                inverse = jnp.where(live, inverse, 0.0)
                normed = center * inverse
                normed_s[rows, :] = normed
                inverse_s[rows, :] = inverse
                message = jnp.where(live, normed * vec[3] + vec[4], 0.0)
                edge_out_ref[rows, :] = (edge_in_ref[rows, :].astype(high) + message).astype(low)
                message_s[
                    pl.ds(base + first, last - first), side * 128 : (side + 1) * 128
                ] = message.astype(low)
            yield
        hots = [pick_t[index, cs : cs + cn, :] for index in indices]
        total = dot(jnp.concatenate(hots, axis=0), message_s[wide_rows, :]).astype(low)
        gathered_s[pl.ds(indices[0] * cn, cn), :] = total[:cn, :128]
        gathered_s[pl.ds(indices[1] * cn, cn), :] = total[cn:, 128:]
        yield

    def node_phase(group):
        base = group * z.group_nodes
        rows = pl.ds(base, z.group_nodes)
        parts = row_pieces(z.group_nodes, PIECE)

        def here(first, last):
            return pl.ds(base + first, last - first)

        entry = jnp.concatenate([node_in_ref[rows, :], gathered_s[rows, :]], axis=1)
        pre = dot(entry, node_low)
        yield
        for first, last in parts:
            act, slope = gelu_pair((pre[first:last] + vec[5]).astype(low))
            node_act_s[0, here(first, last), :] = act
            node_slope_s[0, here(first, last), :] = slope
        yield
        pre = dot(node_act_s[0, rows, :], inner_low[2])
        yield
        for first, last in parts:
            act, slope = gelu_pair((pre[first:last] + vec[6]).astype(low))
            node_act_s[1, here(first, last), :] = act
            node_slope_s[1, here(first, last), :] = slope
        yield
        pre = dot(node_act_s[1, rows, :], inner_low[3])
        yield
        for first, last in parts:
            piece = here(first, last)
            value = pre[first:last] + vec[7]
            center = value - jnp.mean(value, axis=1, keepdims=True)
            inverse = lax.rsqrt(jnp.mean(center * center, axis=1, keepdims=True) + eps_norm)
            normed = center * inverse
            node_out_ref[piece, :] = (
                node_in_ref[piece, :].astype(high) + normed * vec[8] + vec[9]
            ).astype(low)
            upstream = node_cot_ref[piece, :].astype(high)
            sums_s[8] += fold_rows(upstream * normed)
            sums_s[9] += fold_rows(upstream)
            upper = upstream * vec[8]
            mean_plain = jnp.mean(upper, axis=1, keepdims=True)
            mean_cross = jnp.mean(upper * normed, axis=1, keepdims=True)
            d_three = inverse * (upper - mean_plain - normed * mean_cross)
            sums_s[7] += fold_rows(d_three)
            node_back_s[2, piece, :] = d_three.astype(low)
        yield
        for k in (1, 0):
            back = dot_nt(node_back_s[k + 1, rows, :], inner_low[2 + k])
            yield
            for first, last in parts:
                piece = here(first, last)
                value = back[first:last] * node_slope_s[k, piece, :].astype(high)
                sums_s[5 + k] += fold_rows(value)
                node_back_s[k, piece, :] = value.astype(low)
            yield
        back = dot_nt(node_back_s[0, rows, :], node_low)
        for first, last in parts:
            piece = here(first, last)
            node_grad_ref[piece, :] = node_cot_ref[piece, :].astype(high) + back[first:last, :128]
            table_s[piece, :128] = back[first:last, 128:].astype(low)
        yield
        table_s[rows, 128:] = dot(table_s[rows, :128], gain_part).astype(low)
        yield
        grads_ref[384:640, :] += dot_tn(entry, node_back_s[0, rows, :])
        grads_ref[896:1024, :] += dot_tn(node_act_s[0, rows, :], node_back_s[1, rows, :])
        grads_ref[1024:1152, :] += dot_tn(node_act_s[1, rows, :], node_back_s[2, rows, :])
        yield

    def edge_backward(pair):
        base = pair * chunk
        wide_rows = chunk_rows(pair)
        indices = (2 * pair, 2 * pair + 1)
        for side, index in enumerate(indices):
            tables = [
                jnp.zeros((cs, 256), low),
                table_s[pl.ds(index * cn, cn), :],
            ]
            if pad:
                tables.append(jnp.zeros((pad, 256), low))
            tables.append(below_s[...])
            entry = jnp.concatenate(
                [pick_s[chunk_rows(index), :], edge_cot_ref[chunk_rows(index), :]], axis=1
            )
            arrived = dot(entry, jnp.concatenate(tables, axis=0))
            yield
            gain_sum = jnp.zeros((8, 128), high)
            shift_sum = jnp.zeros((8, 128), high)
            for first, last in row_pieces(chunk, PIECE_NORM):
                rows = pl.ds(index * chunk + first, last - first)
                upstream, plain = sides(arrived[first:last])
                normed = normed_s[rows, :]
                cross = upstream * normed
                gain_sum = gain_sum + fold_rows(cross)
                live = live_rows(index, first, last - first)
                shift_sum = shift_sum + fold_rows(jnp.where(live, upstream, 0.0))
                cross = jnp.mean(cross * vec[3], axis=1, keepdims=True)
                d_three = inverse_s[rows, :] * (upstream * vec[3] - plain - normed * cross)
                message_s[
                    pl.ds(base + first, last - first), side * 128 : (side + 1) * 128
                ] = d_three.astype(low)
            sums_s[3] += gain_sum
            sums_s[4] += shift_sum
            yield
        for gradient_s, slope_s, weights in ((message_s, slope_two_s, 3), (slope_two_s, slope_one_s, 2)):
            back = dot(gradient_s[wide_rows, :], wide_s[weights])
            yield
            for first, last in row_pieces(chunk, PIECE):
                rows = pl.ds(base + first, last - first)
                slope_s[rows, :] = back[first:last].astype(low) * slope_s[rows, :]
            yield
        back = dot(slope_one_s[wide_rows, :], wide_s[4])
        yield
        for index, half in zip(indices, sides(back)):
            for first, last in row_pieces(chunk, PIECE):
                rows = pl.ds(index * chunk + first, last - first)
                edge_grad_ref[rows, :] = edge_cot_ref[rows, :].astype(high) + half[first:last]
        yield
        ones = jnp.ones((16, chunk), low)
        entry = [edge_in_ref[chunk_rows(index), :].T for index in indices]
        hots = [pick_t[index, : cs + cn, :] for index in indices]
        total = dot(jnp.concatenate(entry + hots, axis=0), slope_one_s[wide_rows, :])
        grads_ref[0:128, :] += total[:128, :128] + total[128:256, 128:]
        first = total[256 : 256 + cs + cn, :128]
        second = total[256 + cs + cn :, 128:]
        node_rows = pl.ds(pair * z.pair_nodes, z.pair_nodes)
        slot_rows = pl.ds(pair * z.pair_slots, z.pair_slots)
        slot_sum_s[slot_rows, :] = jnp.concatenate([first[:cs], second[:cs]], axis=0).astype(low)
        recv_sum = jnp.concatenate([first[cs:], second[cs:]], axis=0)
        sums_s[0] += fold_rows(recv_sum)
        recv_sum_s[node_rows, :] = recv_sum.astype(low)
        yield
        for k, act_s, gradient_s in ((1, act_one_s, slope_two_s), (2, act_two_s, message_s)):
            total = dot(
                jnp.concatenate([act_s[wide_rows, :].T, ones], axis=0), gradient_s[wide_rows, :]
            )
            grads_ref[pl.ds(512 + 128 * k, 128), :] += total[:128, :128] + total[128:256, 128:]
            sums_s[k] += (total[256:264, :128] + total[256:264, 128:]) * 0.125
            yield

    def group_end(group):
        node_rows = pl.ds(group * z.group_nodes, z.group_nodes)
        slot_rows = pl.ds(group * z.group_slots, z.group_slots)
        slot_grad_ref[slot_rows, :] = dot_nt(slot_sum_s[slot_rows, :], w_slot).astype(low)
        node_grad_ref[node_rows, :] += dot_nt(recv_sum_s[node_rows, :], w_recv)
        yield
        grads_ref[128:256, :] += dot_tn(slot_ref[slot_rows, :], slot_sum_s[slot_rows, :])
        grads_ref[256:384, :] += dot_tn(node_in_ref[node_rows, :], recv_sum_s[node_rows, :])
        yield

    emit(z.pairs, z.per_group, edge_forward, node_phase, edge_backward, group_end)


def layer_scratch(z):
    return [
        pltpu.VMEM((10, 8, 128), high),
        pltpu.VMEM((5, 256, 256), low),
        pltpu.VMEM((128, 256), low),
        pltpu.VMEM((z.tile, 128), low),
        pltpu.VMEM((z.tile_chunks, 128, z.chunk), low),
        pltpu.VMEM((z.tile // 2, 256), low),
        pltpu.VMEM((z.tile // 2, 256), low),
        pltpu.VMEM((z.tile // 2, 256), low),
        pltpu.VMEM((z.tile // 2, 256), low),
        pltpu.VMEM((z.tile, 128), high),
        pltpu.VMEM((z.tile, 128), high),
        pltpu.VMEM((z.tile // 2, 256), low),
        pltpu.VMEM((2, z.tile_nodes, 128), low),
        pltpu.VMEM((2, z.tile_nodes, 128), low),
        pltpu.VMEM((3, z.tile_nodes, 128), low),
        pltpu.VMEM((z.tile_nodes, 128), low),
        pltpu.VMEM((z.tile_nodes, 256), low),
        pltpu.VMEM((z.tile_slots, 128), low),
        pltpu.VMEM((z.tile_nodes, 128), low),
        pltpu.VMEM((z.tile_slots, 128), low),
        pltpu.VMEM((z.tile_nodes, 128), low),
    ]


def layer_outputs(z, nodes, edges, slots):
    return [
        jax.ShapeDtypeStruct((nodes, 128), low),
        jax.ShapeDtypeStruct((edges, 128), low),
        jax.ShapeDtypeStruct((nodes, 128), high),
        jax.ShapeDtypeStruct((edges, 128), high),
        jax.ShapeDtypeStruct((slots, 128), low),
    ]


def layer_kernel(z, block_ref, *refs):
    inputs, weights, refs = refs[:8], refs[8:12], refs[12:]
    grads_in_ref, own, refs = refs[0], refs[1:6], refs[6:]
    results, grads_ref, staged, refs = refs[:5], refs[5], refs[6:11], refs[11:]
    own_sem, store_sem, *scratch = refs
    step = pl.program_id(0)
    block, steps = block_ref[0], z.tiles - 1
    slot = lax.rem(step, 2)
    counts = [result.shape[0] // z.tiles for result in results]

    def stores(at, tile):
        return [
            pltpu.make_async_copy(
                place.at[at], result.at[pl.ds(tile * count, count), :], store_sem.at[at, k]
            )
            for k, (place, result, count) in enumerate(zip(staged, results, counts))
        ]

    own_copies = [
        pltpu.make_async_copy(
            place, result.at[pl.ds(block * count, count), :], own_sem.at[k]
        )
        for k, (place, result, count) in enumerate(zip(own, results, counts))
    ]

    @pl.when(step == 0)
    def _():
        for copy in own_copies:
            copy.start()
        grads_ref[...] = grads_in_ref[...]
        prepare(weights[0], weights[2], weights[3], *scratch[:3])

    @pl.when(step >= 2)
    def _():
        for copy in stores(slot, 0):
            copy.wait()

    tile = lax.rem(block + 1 + step, z.tiles)
    places = [place.at[slot] for place in staged]
    layer_tile(z, tile, *inputs, *weights, *places, grads_ref, *scratch)
    for copy in stores(slot, tile):
        copy.start()

    @pl.when(step == steps - 1)
    def _():
        close_sums(grads_ref, scratch[0])
        for copy in own_copies:
            copy.wait()
        if steps > 1:
            for copy in stores(1 - slot, 0):
                copy.wait()
        for copy in stores(slot, 0):
            copy.wait()


def layer_call(z, block, inputs, weights, grads, own):
    steps = z.tiles - 1

    def rows_spec(rows):
        return pl.BlockSpec((rows, 128), lambda i, block: (lax.rem(block[0] + 1 + i, z.tiles), 0))

    def whole(array):
        return pl.BlockSpec(array.shape, lambda i, block: (0,) * array.ndim)

    hbm = pl.BlockSpec(memory_space=pltpu.HBM)
    shapes = layer_outputs(z, z.nodes, z.edges, z.slots)
    tile_shapes = layer_outputs(z, z.tile_nodes, z.tile, z.tile_slots)
    return pl.pallas_call(
        functools.partial(layer_kernel, z),
        grid_spec=pltpu.PrefetchScalarGridSpec(
            num_scalar_prefetch=1,
            grid=(steps,),
            in_specs=[
                pl.BlockSpec(memory_space=pltpu.SMEM),
                rows_spec(z.tile // 128),
                rows_spec(z.tile // 128),
                rows_spec(z.tile),
                rows_spec(z.tile),
                rows_spec(z.tile_nodes),
                rows_spec(z.tile_nodes),
                rows_spec(z.tile_slots),
            ]
            + [whole(w) for w in weights]
            + [whole(grads)]
            + [hbm] * 5,
            out_specs=[hbm] * 5 + [whole(grads)],
            scratch_shapes=[pltpu.VMEM((2,) + item.shape, item.dtype) for item in tile_shapes]
            + [pltpu.SemaphoreType.DMA((5,)), pltpu.SemaphoreType.DMA((2, 5))]
            + layer_scratch(z),
        ),
        out_shape=[*shapes, jax.ShapeDtypeStruct(grads.shape, high)],
        compiler_params=pltpu.CompilerParams(
            dimension_semantics=("arbitrary",), vmem_limit_bytes=VMEM
        ),
        name="layer",
    )(block, *inputs, *weights, grads, *own)


def signal(semaphore, where):
    pl.semaphore_signal(semaphore, inc=1, device_id=where, device_id_type=pl.DeviceIdType.MESH)


def send(source, target, send_sem, recv_sem, where):
    copy = pltpu.make_async_remote_copy(
        src_ref=source,
        dst_ref=target,
        send_sem=send_sem,
        recv_sem=recv_sem,
        device_id=where,
        device_id_type=pl.DeviceIdType.MESH,
    )
    copy.start()
    return copy


def fetch_kernel(z, peers, unroll, count_ref, *refs):
    request_ref, sources, weight_refs, refs = refs[0], refs[1:7], refs[7:11], refs[11:]
    rows_ref, asked_ref, block_ref, results, refs = refs[0], refs[1], refs[2], refs[3:9], refs[9:]
    wanted_v, asked_v, node_v, node_s, picked_s, out_s, refs = *refs[:6], refs[6:]
    ask_send, ask_recv, row_send, row_recv, load_sem, store_sem, refs = *refs[:6], refs[6:]
    loaded, weights, slot_v, staged, scratch = refs[:6], refs[6:10], refs[10], refs[11:17], refs[17:]
    me = lax.axis_index("dom")
    slots = picked_s.shape[0]
    mates = z.tile_slots // slots
    blocks = peers // mates
    block, place = lax.div(me, mates), lax.rem(me, mates)

    def peer(across, along, sign):
        return (
            lax.rem(block + (blocks + sign * across), blocks) * mates
            + lax.rem(place + (mates + sign * along), mates)
        )

    order = sorted(range(1, blocks), key=lambda across: (abs(2 * across - blocks), across))
    shifts = [(across, along) for across in order for along in range(mates)]
    shifts[mates:mates] = [(0, along) for along in range(1, mates)]
    barrier = pltpu.get_barrier_semaphore()
    for across, along in shifts:
        signal(barrier, {"dom": peer(across, along, 1)})
    loads = [
        pltpu.make_async_copy(request_ref, wanted_v, load_sem.at[0]),
        pltpu.make_async_copy(sources[4], node_v, load_sem.at[1]),
    ]
    for k, (source, target) in enumerate(zip(sources, loaded)):
        rows = target.shape[0]
        loads.append(
            pltpu.make_async_copy(
                source.at[pl.ds(block * rows, rows), :], target, load_sem.at[2 + k]
            )
        )
    for k, (source, target) in enumerate(zip(weight_refs, weights)):
        loads.append(pltpu.make_async_copy(source, target, load_sem.at[8 + k]))
    for load in loads:
        load.start()
    loads[0].wait()
    for k in range(peers):
        asked_v[k] = wanted_v[pl.ds(k, 1), :]
    loads[1].wait()
    node_s[...] = node_v[...].astype(high)
    block_ref[0] = block
    pl.semaphore_wait(barrier, peers - 1)
    asks = []
    for across, along in shifts:
        other, k = peer(across, along, 1), across * mates + along
        asks.append(
            send(
                asked_v.at[other],
                asked_v.at[peers + me],
                ask_send.at[k],
                ask_recv.at[k],
                {"dom": other},
            )
        )
    asked_v[peers + me] = asked_v[me]
    grads_v = staged[5]
    grads_v[...] = jnp.zeros_like(grads_v)
    for load in loads[8:]:
        load.wait()
    prepare(weights[0], weights[2], weights[3], *scratch[:3])
    for ask in asks:
        ask.wait_recv()
    local = pltpu.make_async_copy(asked_v.at[pl.ds(peers, peers)], asked_ref, load_sem.at[0])
    local.start()
    local.wait()
    sends, arrivals = [], []
    for across, along in shifts + [(0, 0)]:
        other, k = peer(across, along, -1), across * mates + along

        @pl.loop(0, slots // unroll)
        def _(group):
            for place in range(unroll):
                row = group * unroll + place
                index = asked_ref[other, 0, row]
                picked_s[pl.ds(row, 1), :] = node_s[pl.ds(index, 1), :]

        out_s[other] = picked_s[...].astype(low)
        if k:
            copy = send(
                out_s.at[other],
                rows_ref.at[me],
                row_send.at[k],
                row_recv.at[k],
                {"dom": other},
            )
            (sends if across else arrivals).append(copy)
    local = pltpu.make_async_copy(out_s.at[me], rows_ref.at[me], load_sem.at[0])
    local.start()
    local.wait()
    for copy in arrivals:
        copy.wait()
    local = pltpu.make_async_copy(
        rows_ref.at[pl.ds(block * mates, mates)], slot_v, load_sem.at[0]
    )
    local.start()
    for load in loads[2:8]:
        load.wait()
    local.wait()
    slot_rows = slot_v.reshape(mates * slots, 128)
    layer_tile(z, block, count_ref, *loaded, slot_rows, *weights, *staged, *scratch)
    close_sums(grads_v, scratch[0])
    stores = [
        pltpu.make_async_copy(place, result, store_sem.at[k])
        for k, (place, result) in enumerate(zip(staged, results))
    ]
    for store in stores:
        store.start()
    for copy in asks:
        copy.wait_send()
    for copy in sends:
        copy.wait()
    for store in stores:
        store.wait()


def fetch_call(z, peers, count, request, ids, edges, nodes, weights):
    slots = request.shape[2]
    mates = z.tile_slots // slots
    dma = pltpu.SemaphoreType.DMA
    hbm = pl.BlockSpec(memory_space=pltpu.HBM)
    smem = pl.BlockSpec(memory_space=pltpu.SMEM)
    tile_shapes = layer_outputs(z, z.tile_nodes, z.tile, z.tile_slots)
    tile_shapes.append(jax.ShapeDtypeStruct((z.grad_rows, 128), high))
    ids_rows = z.tile // 128
    return pl.pallas_call(
        functools.partial(fetch_kernel, z, peers, 32),
        in_specs=[smem] + [hbm] * 11,
        out_specs=[hbm, smem, smem] + [hbm] * 6,
        out_shape=[
            jax.ShapeDtypeStruct((peers, slots, 128), low),
            jax.ShapeDtypeStruct((peers, 1, slots), jnp.int32),
            jax.ShapeDtypeStruct((1,), jnp.int32),
            *tile_shapes,
        ],
        scratch_shapes=[
            pltpu.VMEM((peers, slots), jnp.int32),
            pltpu.VMEM((2 * peers, 1, slots), jnp.int32),
            pltpu.VMEM((z.nodes, 128), low),
            pltpu.VMEM((z.nodes, 128), high),
            pltpu.VMEM((slots, 128), high),
            pltpu.VMEM((peers, slots, 128), low),
            dma((peers,)),
            dma((peers,)),
            dma((peers,)),
            dma((peers,)),
            dma((12,)),
            dma((6,)),
            pltpu.VMEM((ids_rows, 128), jnp.int32),
            pltpu.VMEM((ids_rows, 128), jnp.int32),
            pltpu.VMEM((z.tile, 128), low),
            pltpu.VMEM((z.tile, 128), low),
            pltpu.VMEM((z.tile_nodes, 128), low),
            pltpu.VMEM((z.tile_nodes, 128), low),
            *[pltpu.VMEM(w.shape, w.dtype) for w in weights],
            pltpu.VMEM((mates, slots, 128), low),
            *[pltpu.VMEM(item.shape, item.dtype) for item in tile_shapes],
            *layer_scratch(z),
        ],
        compiler_params=pltpu.CompilerParams(
            collective_id=0, has_side_effects=True, vmem_limit_bytes=VMEM
        ),
        name="fetch",
    )(count, request.reshape(peers, slots), *ids, *edges, *nodes, *weights)


def reduce_kernel(
    groups,
    peers,
    grads_ref,
    slot_grad_ref,
    sum_ref,
    back_ref,
    grads_s,
    all_s,
    half_out,
    half_in,
    half_sum,
    quarter_out,
    quarter_in,
    quarter_sum,
    piece_out,
    piece_in,
    back_send,
    back_recv,
    half_send,
    half_recv,
    quarter_send,
    quarter_recv,
    piece_send,
    piece_recv,
    load_sem,
):
    grp, dom = lax.axis_index("grp"), lax.axis_index("dom")
    core, level = lax.rem(dom, 2), lax.div(dom, 2)
    levels = peers // 2
    half, quarter, piece = half_sum.shape[0], quarter_sum.shape[0], piece_out.shape[1]
    barrier = pltpu.get_barrier_semaphore()
    for k in range(1, peers):
        signal(barrier, {"dom": lax.rem(dom + k, peers)})
    for k in range(1, groups):
        signal(barrier, {"grp": lax.rem(grp + k, groups)})
    twin = {"dom": 2 * level + 1 - core}
    loads = [
        pltpu.make_async_copy(
            grads_ref.at[pl.ds(first, half), :], grads_s.at[pl.ds(first, half), :], load_sem.at[k]
        )
        for k, first in enumerate(((1 - core) * half, core * half))
    ]
    loads.append(
        pltpu.make_async_copy(slot_grad_ref.at[dom], back_ref.at[dom], load_sem.at[2])
    )
    for load in loads:
        load.start()
    loads[0].wait()
    half_out[...] = grads_s[pl.ds((1 - core) * half, half), :].astype(low)
    loads[1].wait()
    pl.semaphore_wait(barrier, peers - 1 + groups - 1)

    sends = [send(half_out, half_in, half_send.at[0], half_recv.at[0], twin)]

    def give_back(k):
        other = lax.rem(dom + k, peers)
        return send(
            slot_grad_ref.at[other],
            back_ref.at[dom],
            back_send.at[k],
            back_recv.at[k],
            {"dom": other},
        )

    early = [k for k in range(1, peers) if 2 * k == peers or (2 * k < peers and k % 2)]
    backs = [give_back(k) for k in early]
    sends[0].wait_recv()
    half_sum[...] = grads_s[pl.ds(core * half, half), :] + half_in[...].astype(high)

    copies = []
    for k in range(1, groups):
        other = lax.rem(grp + k, groups)
        quarter_out[k] = half_sum[pl.ds(other * quarter, quarter), :].astype(low)
        copies.append(
            send(
                quarter_out.at[k],
                quarter_in.at[k],
                quarter_send.at[k],
                quarter_recv.at[k],
                {"grp": other},
            )
        )
    total = half_sum[pl.ds(grp * quarter, quarter), :]
    for k in range(1, groups):
        copies[k - 1].wait_recv()
        total = total + quarter_in[k].astype(high)
    quarter_sum[...] = total
    sends += copies

    copies = []
    for k in range(1, levels):
        other = lax.rem(level + k, levels)
        piece_out[k] = quarter_sum[pl.ds(other * piece, piece), :].astype(low)
        copies.append(
            send(
                piece_out.at[k],
                piece_in.at[k],
                piece_send.at[k],
                piece_recv.at[k],
                {"dom": 2 * other + core},
            )
        )
    total = quarter_sum[pl.ds(level * piece, piece), :]
    for k in range(1, levels):
        copies[k - 1].wait_recv()
        total = total + piece_in[k].astype(high)
    sends += copies

    own_half = core * half
    own_quarter = own_half + grp * quarter
    own_piece = own_quarter + level * piece
    all_s[pl.ds(own_piece, piece), :] = total.astype(low)
    copies = []
    for k in range(1, levels):
        place = all_s.at[pl.ds(own_piece, piece), :]
        where = {"dom": 2 * lax.rem(level + k, levels) + core}
        copies.append(
            send(place, place, piece_send.at[levels + k], piece_recv.at[levels + k], where)
        )
    backs += [give_back(k) for k in range(1, peers) if k not in early]
    for copy in copies:
        copy.wait_recv()
    sends += copies
    copies = []
    for k in range(1, groups):
        place = all_s.at[pl.ds(own_quarter, quarter), :]
        where = {"grp": lax.rem(grp + k, groups)}
        copies.append(
            send(place, place, quarter_send.at[groups + k], quarter_recv.at[groups + k], where)
        )
    for copy in copies:
        copy.wait_recv()
    sends += copies
    place = all_s.at[pl.ds(own_half, half), :]
    copy = send(place, place, half_send.at[1], half_recv.at[1], twin)
    copy.wait_recv()
    sends.append(copy)
    loads[2].wait()
    for copy in backs:
        copy.wait()
    for copy in sends:
        copy.wait_send()
    sum_ref[...] = all_s[...]


def reduce_call(groups, peers, grads, slot_grad):
    rows = grads.shape[0]
    levels = peers // 2
    half, quarter, piece = rows // 2, rows // 2 // groups, rows // 2 // groups // levels
    dma = pltpu.SemaphoreType.DMA
    return pl.pallas_call(
        functools.partial(reduce_kernel, groups, peers),
        in_specs=[pl.BlockSpec(memory_space=pltpu.HBM)] * 2,
        out_specs=[
            pl.BlockSpec(memory_space=pltpu.VMEM),
            pl.BlockSpec(memory_space=pltpu.HBM),
        ],
        out_shape=[
            jax.ShapeDtypeStruct((rows, 128), low),
            jax.ShapeDtypeStruct(slot_grad.shape, low),
        ],
        scratch_shapes=[
            pltpu.VMEM((rows, 128), high),
            pltpu.VMEM((rows, 128), low),
            pltpu.VMEM((half, 128), low),
            pltpu.VMEM((half, 128), low),
            pltpu.VMEM((half, 128), high),
            pltpu.VMEM((groups, quarter, 128), low),
            pltpu.VMEM((groups, quarter, 128), low),
            pltpu.VMEM((quarter, 128), high),
            pltpu.VMEM((levels, piece, 128), low),
            pltpu.VMEM((levels, piece, 128), low),
            dma((peers,)),
            dma((peers,)),
            dma((2,)),
            dma((2,)),
            dma((2 * groups,)),
            dma((2 * groups,)),
            dma((2 * levels,)),
            dma((2 * levels,)),
            dma((3,)),
        ],
        compiler_params=pltpu.CompilerParams(
            collective_id=1, has_side_effects=True, vmem_limit_bytes=VMEM
        ),
        name="reduce",
    )(grads, slot_grad)


def adamw_step(master, moment_mean, moment_var, average, gradient, factor):
    clipped = gradient * factor
    mean_new = beta_one * moment_mean + (1.0 - beta_one) * clipped
    var_new = beta_two * moment_var + (1.0 - beta_two) * clipped * clipped
    mean_hat = mean_new / (1.0 - beta_one**STEP)
    var_hat = var_new / (1.0 - beta_two**STEP)
    updated = master - learn_rate * (
        mean_hat / (jnp.sqrt(var_hat) + adam_eps) + decay_rate * master
    )
    return (
        mean_new,
        var_new,
        updated,
        updated.astype(low),
        ema_keep * average + (1.0 - ema_keep) * updated,
    )


FIRST = (0, 384, 640, 1152, 1162)


def finish_kernel(unroll, asked_ref, *refs):
    sources, (norm_ref, *results), refs = refs[:19], refs[19:41], refs[41:]
    loaded, (rows_s, *staged, load_sem, store_sem) = refs[:19], refs[19:]
    summed_s, back_s, node_s = loaded[16:]
    loads = [
        pltpu.make_async_copy(source, place, load_sem.at[k])
        for k, (source, place) in enumerate(zip(sources, loaded))
    ]
    for load in [*loads[17:], loads[16], *loads[:16]]:
        load.start()
    loads[17].wait()
    rows_s[...] = back_s[...].astype(high)
    slots = asked_ref.shape[2]
    loads[18].wait()

    @pl.loop(0, rows_s.shape[0] // unroll)
    def _(group):
        base = group * unroll
        peer, first = lax.div(base, slots), lax.rem(base, slots)
        places = [pl.ds(asked_ref[peer, 0, first + k], 1) for k in range(unroll)]
        values = [
            node_s[place, :] + rows_s[pl.ds(base + k, 1), :] for k, place in enumerate(places)
        ]
        for place, value in zip(places, values):
            node_s[place, :] = value

    stores = [pltpu.make_async_copy(node_s, results[20], store_sem.at[20])]
    stores[0].start()
    for load in loads[:17]:
        load.wait()
    gradient = summed_s[...].astype(high)
    square = jnp.sum(gradient * gradient, axis=0, keepdims=True)
    grad_norm = jnp.sqrt(jnp.sum(square, axis=1, keepdims=True))
    norm_ref[0] = grad_norm[0, 0]
    factor = clip_level / jnp.maximum(grad_norm, clip_level)
    for k in range(4):
        values = [place[...] for place in loaded[4 * k : 4 * k + 4]]
        updates = adamw_step(*values, gradient[FIRST[k] : FIRST[k + 1]], factor)
        for place, value in enumerate(updates):
            place += 5 * k
            staged[place][...] = value
            store = pltpu.make_async_copy(staged[place], results[place], store_sem.at[place])
            store.start()
            stores.append(store)
    for store in stores:
        store.wait()


def finish_call(asked, part, back, summed, tensors):
    smem = pl.BlockSpec(memory_space=pltpu.SMEM)
    hbm = pl.BlockSpec(memory_space=pltpu.HBM)
    sources = [*tensors, summed, back, part]
    shapes = []
    for k in range(4):
        shape = tensors[4 * k].shape
        shapes += [jax.ShapeDtypeStruct(shape, kind) for kind in (high, high, high, low, high)]
    return pl.pallas_call(
        functools.partial(finish_kernel, 32),
        in_specs=[smem] + [hbm] * 19,
        out_specs=[smem] + [hbm] * 21,
        out_shape=[
            jax.ShapeDtypeStruct((1,), high),
            *shapes,
            jax.ShapeDtypeStruct(part.shape, high),
        ],
        scratch_shapes=[
            *[pltpu.VMEM(item.shape, item.dtype) for item in sources],
            pltpu.VMEM(back.shape, high),
            *[pltpu.VMEM(item.shape, item.dtype) for item in shapes],
            pltpu.SemaphoreType.DMA((19,)),
            pltpu.SemaphoreType.DMA((21,)),
        ],
        compiler_params=pltpu.CompilerParams(vmem_limit_bytes=VMEM),
        name="finish",
    )(asked, *sources)


def shards(
    node_in,
    edge_in,
    edge_slot,
    edge_receiver,
    edge_count,
    request,
    node_cot,
    edge_cot,
    *tensors,
):
    groups, peers = lax.axis_size("grp"), lax.axis_size("dom")
    slots = request.shape[2]
    z = Sizes(edge_in.shape[0], node_in.shape[0], peers * slots, groups * peers)
    weights = tensors[::4]
    ids = (edge_slot.reshape(-1, 128), edge_receiver.reshape(-1, 128))
    slot_rows, asked, block, *own, grads = fetch_call(
        z,
        peers,
        edge_count,
        request,
        ids,
        (edge_in, edge_cot),
        (node_in, node_cot),
        weights,
    )
    node_out, edge_out, node_part, edge_grad, slot_grad, grads = layer_call(
        z,
        block,
        (
            edge_count,
            *ids,
            edge_in,
            edge_cot,
            node_in,
            node_cot,
            slot_rows.reshape(peers * slots, 128),
        ),
        weights,
        grads,
        own,
    )
    summed, returned = reduce_call(groups, peers, grads, slot_grad.reshape(peers, slots, 128))
    flat = [tensor.reshape(-1, 128) for tensor in tensors]
    grad_norm, *results, node_grad = finish_call(
        asked, node_part, returned.reshape(peers * slots, 128), summed, flat
    )
    results = [value.reshape(tensors[k // 5 * 4].shape) for k, value in enumerate(results)]
    return (node_out, edge_out, node_grad, edge_grad, grad_norm.reshape(()), *results)


def solution(mesh):
    rows = P(("grp", "dom"), None)
    in_specs = (
        rows,
        rows,
        P(("grp", "dom")),
        P(("grp", "dom")),
        P(("grp", "dom")),
        P(("grp", "dom"), None, None),
        rows,
        rows,
    ) + (P(),) * 16
    out_specs = (rows,) * 4 + (P(),) * 21
    return jax.shard_map(shards, mesh=mesh, in_specs=in_specs, out_specs=out_specs, check_vma=False)
```

```python
import functools
import math

import jax
import jax.numpy as jnp
from jax import lax
from jax.experimental import pallas as pl
from jax.experimental.pallas import tpu as pltpu
from jax.sharding import PartitionSpec as P

STEP = 10

eps_norm = 1e-05
beta_one = 0.5
beta_two = 0.6
learn_rate = 0.08
decay_rate = 0.01
adam_eps = 1e-08
ema_keep = 0.9
clip_level = 1.0

gelu_in = math.sqrt(2.0 / math.pi)
gelu_cube = gelu_in * 0.044715

low = jnp.bfloat16
high = jnp.float32

GAP = 2
PIECE = 64
PIECE_NORM = 32
VMEM = 62 * 1024 * 1024
PAIRS = 8


def dot(operand, weights):
    return jnp.dot(operand, weights, preferred_element_type=high)


def dot_nt(operand, weights):
    return lax.dot_general(
        operand, weights, (((1,), (1,)), ((), ())), preferred_element_type=high
    )


def dot_tn(operand, weights):
    return lax.dot_general(
        operand, weights, (((0,), (0,)), ((), ())), preferred_element_type=high
    )


def gelu_pair(x):
    square = x * x
    t = jnp.tanh(x * (gelu_in + gelu_cube * square))
    above = 1.0 + t
    value = (0.5 * x) * above
    slope = 0.5 * above + (value * (1.0 - t)) * (gelu_in + (3.0 * gelu_cube) * square)
    return value.astype(low), slope.astype(low)


def fold_rows(values):
    return jnp.sum(values.reshape(values.shape[0] // 8, 8, values.shape[1]), axis=0)


def emit(pairs, per_group, forward, middle, backward, end):
    groups = pairs // per_group
    streams = {"forward": forward, "middle": middle, "backward": backward, "end": end}
    started = dict.fromkeys(streams, 0)
    last = dict.fromkeys(streams, -GAP)
    active, done, now = [], set(), 0

    def ready(name, k):
        if name == "middle":
            return all(("forward", k * per_group + j) in done for j in range(per_group))
        if name == "end":
            return all(("backward", k * per_group + j) in done for j in range(per_group))
        return name == "forward" or ("middle", k // per_group) in done

    while len(done) < 2 * pairs + 2 * groups:
        for name in streams:
            k = started[name]
            count = pairs if name in ("forward", "backward") else groups
            if k < count and now - last[name] >= GAP and ready(name, k):
                active.append(((name, k), streams[name](k)))
                started[name], last[name] = k + 1, now
        for item in list(active):
            try:
                next(item[1])
            except StopIteration:
                active.remove(item)
                done.add(item[0])
        now += 1


class Sizes:
    def __init__(self, edges, nodes, slots, devices):
        self.edges, self.nodes, self.slots = edges, nodes, slots
        blocks = edges // 128
        self.rwin = nodes // blocks
        self.swin = slots // blocks
        self.sub = 4
        while self.sub * (self.rwin + self.swin) > 128:
            self.sub //= 2
        self.chunk = self.sub * 128
        self.chunk_slots = self.sub * self.swin
        self.chunk_nodes = self.sub * self.rwin
        self.pair_nodes, self.pair_slots = 2 * self.chunk_nodes, 2 * self.chunk_slots
        self.per_group = 4
        self.pairs = PAIRS
        self.group_nodes = self.per_group * self.pair_nodes
        self.group_slots = self.per_group * self.pair_slots
        self.tile = self.pairs * 2 * self.chunk
        self.tile_chunks = 2 * self.pairs
        self.tile_nodes = self.pairs * self.pair_nodes
        self.tile_slots = self.pairs * self.pair_slots
        self.tiles = edges // self.tile
        self.grad_rows = -(-1162 // (16 * devices)) * 16 * devices


def diagonal(first, second):
    zero_a = jnp.zeros((first.shape[0], second.shape[1]), first.dtype)
    zero_b = jnp.zeros((second.shape[0], first.shape[1]), first.dtype)
    return jnp.concatenate(
        [
            jnp.concatenate([first, zero_a], axis=1),
            jnp.concatenate([zero_b, second], axis=1),
        ],
        axis=0,
    )


def twice(row):
    return jnp.concatenate([row, row], axis=1)


def prepare(edge_entry_ref, inner_ref, vec_ref, sums_s, wide_s, below_s):
    sums_s[...] = jnp.zeros_like(sums_s)
    first, second = inner_ref[0].astype(low), inner_ref[1].astype(low)
    wide_s[0] = diagonal(first, first)
    middle = second.astype(high)
    middle = (middle - jnp.mean(middle, axis=1, keepdims=True)).astype(low)
    wide_s[1] = diagonal(middle, middle)
    for k, weights in ((2, inner_ref[0]), (3, inner_ref[1]), (4, edge_entry_ref[0:128, :])):
        weights = weights.T.astype(low)
        wide_s[k] = diagonal(weights, weights)
    row = lax.broadcasted_iota(jnp.int32, (128, 128), 0)
    column = lax.broadcasted_iota(jnp.int32, (128, 128), 1)
    gain = jnp.broadcast_to(vec_ref[pl.ds(3, 1), :] * (1.0 / 128.0), (128, 128)).T.astype(low)
    below_s[:, :128] = jnp.where(row == column, 1.0, 0.0).astype(low)
    below_s[:, 128:] = gain


def close_sums(grads_ref, sums_s):
    grads_ref[1152:1162, :] += jnp.sum(sums_s[...], axis=1)


def layer_tile(
    z,
    tile,
    count_ref,
    slot_ids_ref,
    recv_ids_ref,
    edge_in_ref,
    edge_cot_ref,
    node_in_ref,
    node_cot_ref,
    slot_ref,
    edge_entry_ref,
    node_entry_ref,
    inner_ref,
    vec_ref,
    node_out_ref,
    edge_out_ref,
    node_grad_ref,
    edge_grad_ref,
    slot_grad_ref,
    grads_ref,
    sums_s,
    wide_s,
    below_s,
    pick_s,
    pick_t,
    act_one_s,
    act_two_s,
    slope_one_s,
    slope_two_s,
    normed_s,
    inverse_s,
    message_s,
    node_act_s,
    node_slope_s,
    node_back_s,
    gathered_s,
    table_s,
    slot_pre_s,
    node_pre_s,
):
    chunk, cn, cs = z.chunk, z.chunk_nodes, z.chunk_slots
    pad = 128 - cn - cs
    vec = [vec_ref[pl.ds(k, 1), :] for k in range(10)]
    edge_low = edge_entry_ref[...].astype(low)
    node_low = node_entry_ref[...].astype(low)
    inner_low = [None, None, inner_ref[2].astype(low), inner_ref[3].astype(low)]
    w_edge, w_slot, w_recv = edge_low[:128], edge_low[128:256], edge_low[256:]
    bias_three = vec[2] - jnp.mean(vec[2], axis=1, keepdims=True)
    gain_part = below_s[:, 128:]
    slot_pre_s[...] = dot(slot_ref[...], w_slot).astype(low)
    node_pre_s[...] = (dot(node_in_ref[...], w_recv) + vec[0]).astype(low)

    def live_rows(index, first, count):
        rows = lax.broadcasted_iota(jnp.int32, (count, 128), 0)
        return rows < count_ref[0] - (tile * z.tile + index * chunk + first)

    def sides(wide):
        return wide[:, :128], wide[:, 128:]

    def chunk_rows(index):
        return pl.ds(index * chunk, chunk)

    def hot_block(block, k):
        pieces = []
        number = tile * (z.tile // 128) + block
        for ref, width, count in ((slot_ids_ref, z.swin, cs), (recv_ids_ref, z.rwin, cn)):
            ids = ref[pl.ds(block, 1), :] - number * width
            band = lax.broadcasted_iota(jnp.int32, (width, 128), 0) == ids
            above, below = k * width, count - (k + 1) * width
            if above:
                pieces.append(jnp.zeros((above, 128), high))
            pieces.append(jnp.where(band, 1.0, 0.0))
            if below:
                pieces.append(jnp.zeros((below, 128), high))
        if pad:
            pieces.append(jnp.zeros((pad, 128), high))
        return jnp.concatenate(pieces, axis=0).astype(low)

    def row_pieces(count, rows):
        rows = min(count, rows)
        return [(first, first + rows) for first in range(0, count, rows)]

    def gelu_rows(pre, act_s, slope_s, base):
        for first, last in row_pieces(pre.shape[0], PIECE):
            act, slope = gelu_pair(pre[first:last].astype(low))
            act_s[pl.ds(base + first, last - first), :] = act
            slope_s[pl.ds(base + first, last - first), :] = slope

    def edge_forward(pair):
        base = pair * chunk
        wide_rows = chunk_rows(pair)
        indices = (2 * pair, 2 * pair + 1)
        for index in indices:
            for k in range(z.sub):
                block = index * z.sub + k
                hot_t = hot_block(block, k)
                pick_t[index, :, k * 128 : (k + 1) * 128] = hot_t[: cs + cn]
                pick_s[pl.ds(block * 128, 128), :] = hot_t.T
        yield
        pres = []
        for index in indices:
            tables = [
                w_edge,
                slot_pre_s[pl.ds(index * cs, cs), :],
                node_pre_s[pl.ds(index * cn, cn), :],
            ]
            if pad:
                tables.append(jnp.zeros((pad, 128), low))
            entry = jnp.concatenate(
                [edge_in_ref[chunk_rows(index), :], pick_s[chunk_rows(index), :]], axis=1
            )
            pres.append(dot(entry, jnp.concatenate(tables, axis=0)))
        yield
        gelu_rows(jnp.concatenate(pres, axis=1), act_one_s, slope_one_s, base)
        yield
        pre_two = dot(act_one_s[wide_rows, :], wide_s[0])
        yield
        bias = twice(vec[1])
        for first, last in row_pieces(chunk, PIECE):
            act, slope = gelu_pair((pre_two[first:last] + bias).astype(low))
            act_two_s[pl.ds(base + first, last - first), :] = act
            slope_two_s[pl.ds(base + first, last - first), :] = slope
        yield
        pre_three = dot(act_two_s[wide_rows, :], wide_s[1])
        yield
        for side, index in enumerate(indices):
            half = pre_three[:, side * 128 : (side + 1) * 128]
            for first, last in row_pieces(chunk, PIECE_NORM):
                rows = pl.ds(index * chunk + first, last - first)
                live = live_rows(index, first, last - first)
                center = half[first:last] + bias_three
                inverse = lax.rsqrt(jnp.mean(center * center, axis=1, keepdims=True) + eps_norm)
                inverse = jnp.where(live, inverse, 0.0)
                normed = center * inverse
                normed_s[rows, :] = normed
                inverse_s[rows, :] = inverse.astype(low)
                message = jnp.where(live, normed * vec[3] + vec[4], 0.0)
                edge_out_ref[rows, :] = (edge_in_ref[rows, :].astype(high) + message).astype(low)
                message_s[
                    pl.ds(base + first, last - first), side * 128 : (side + 1) * 128
                ] = message.astype(low)
            yield
        hots = [pick_t[index, cs : cs + cn, :] for index in indices]
        total = dot(jnp.concatenate(hots, axis=0), message_s[wide_rows, :]).astype(low)
        gathered_s[pl.ds(indices[0] * cn, cn), :] = total[:cn, :128]
        gathered_s[pl.ds(indices[1] * cn, cn), :] = total[cn:, 128:]
        yield

    def node_phase(group):
        base = group * z.group_nodes
        rows = pl.ds(base, z.group_nodes)
        parts = row_pieces(z.group_nodes, PIECE)

        def here(first, last):
            return pl.ds(base + first, last - first)

        entry = jnp.concatenate([node_in_ref[rows, :], gathered_s[rows, :]], axis=1)
        pre = dot(entry, node_low)
        yield
        for first, last in parts:
            act, slope = gelu_pair(pre[first:last] + vec[5])
            node_act_s[0, here(first, last), :] = act
            node_slope_s[0, here(first, last), :] = slope
        yield
        pre = dot(node_act_s[0, rows, :], inner_low[2])
        yield
        for first, last in parts:
            act, slope = gelu_pair(pre[first:last] + vec[6])
            node_act_s[1, here(first, last), :] = act
            node_slope_s[1, here(first, last), :] = slope
        yield
        pre = dot(node_act_s[1, rows, :], inner_low[3])
        yield
        for first, last in parts:
            piece = here(first, last)
            value = pre[first:last] + vec[7]
            center = value - jnp.mean(value, axis=1, keepdims=True)
            inverse = lax.rsqrt(jnp.mean(center * center, axis=1, keepdims=True) + eps_norm)
            normed = center * inverse
            node_out_ref[piece, :] = (
                node_in_ref[piece, :].astype(high) + normed * vec[8] + vec[9]
            ).astype(low)
            upstream = node_cot_ref[piece, :].astype(high)
            sums_s[8] += fold_rows(upstream * normed)
            sums_s[9] += fold_rows(upstream)
            upper = upstream * vec[8]
            mean_plain = jnp.mean(upper, axis=1, keepdims=True)
            mean_cross = jnp.mean(upper * normed, axis=1, keepdims=True)
            d_three = inverse * (upper - mean_plain - normed * mean_cross)
            sums_s[7] += fold_rows(d_three)
            node_back_s[piece, :] = d_three.astype(low)
        yield
        for k in (1, 0):
            upper = node_back_s[rows, :] if k else node_slope_s[1, rows, :]
            back = dot_nt(upper, inner_low[2 + k])
            yield
            for first, last in parts:
                piece = here(first, last)
                value = back[first:last] * node_slope_s[k, piece, :].astype(high)
                sums_s[5 + k] += fold_rows(value)
                node_slope_s[k, piece, :] = value.astype(low)
            yield
        back = dot_nt(node_slope_s[0, rows, :], node_low)
        for first, last in parts:
            piece = here(first, last)
            node_grad_ref[piece, :] = node_cot_ref[piece, :].astype(high) + back[first:last, :128]
            table_s[piece, :128] = back[first:last, 128:].astype(low)
        yield
        table_s[rows, 128:] = dot(table_s[rows, :128], gain_part).astype(low)
        yield
        grads_ref[384:640, :] += dot_tn(entry, node_slope_s[0, rows, :])
        grads_ref[896:1024, :] += dot_tn(node_act_s[0, rows, :], node_slope_s[1, rows, :])
        grads_ref[1024:1152, :] += dot_tn(node_act_s[1, rows, :], node_back_s[rows, :])
        yield

    def edge_backward(pair):
        base = pair * chunk
        wide_rows = chunk_rows(pair)
        indices = (2 * pair, 2 * pair + 1)
        for side, index in enumerate(indices):
            tables = [
                jnp.zeros((cs, 256), low),
                table_s[pl.ds(index * cn, cn), :],
            ]
            if pad:
                tables.append(jnp.zeros((pad, 256), low))
            tables.append(below_s[...])
            entry = jnp.concatenate(
                [pick_s[chunk_rows(index), :], edge_cot_ref[chunk_rows(index), :]], axis=1
            )
            arrived = dot(entry, jnp.concatenate(tables, axis=0))
            yield
            gain_sum = jnp.zeros((8, 128), high)
            shift_sum = jnp.zeros((8, 128), high)
            for first, last in row_pieces(chunk, PIECE_NORM):
                rows = pl.ds(index * chunk + first, last - first)
                upstream, plain = sides(arrived[first:last])
                normed = normed_s[rows, :]
                cross = upstream * normed
                gain_sum = gain_sum + fold_rows(cross)
                live = live_rows(index, first, last - first)
                shift_sum = shift_sum + fold_rows(jnp.where(live, upstream, 0.0))
                cross = jnp.mean(cross * vec[3], axis=1, keepdims=True)
                d_three = inverse_s[rows, :] * (upstream * vec[3] - plain - normed * cross)
                message_s[
                    pl.ds(base + first, last - first), side * 128 : (side + 1) * 128
                ] = d_three.astype(low)
            sums_s[3] += gain_sum
            sums_s[4] += shift_sum
            yield
        for gradient_s, slope_s, weights in ((message_s, slope_two_s, 3), (slope_two_s, slope_one_s, 2)):
            back = dot(gradient_s[wide_rows, :], wide_s[weights])
            yield
            for first, last in row_pieces(chunk, PIECE):
                rows = pl.ds(base + first, last - first)
                slope_s[rows, :] = back[first:last].astype(low) * slope_s[rows, :]
            yield
        back = dot(slope_one_s[wide_rows, :], wide_s[4])
        yield
        for index, half in zip(indices, sides(back)):
            for first, last in row_pieces(chunk, PIECE):
                rows = pl.ds(index * chunk + first, last - first)
                edge_grad_ref[rows, :] = edge_cot_ref[rows, :].astype(high) + half[first:last]
        yield
        ones = jnp.ones((16, chunk), low)
        entry = [edge_in_ref[chunk_rows(index), :].T for index in indices]
        hots = [pick_t[index, : cs + cn, :] for index in indices]
        total = dot(jnp.concatenate(entry + hots, axis=0), slope_one_s[wide_rows, :])
        grads_ref[0:128, :] += total[:128, :128] + total[128:256, 128:]
        first = total[256 : 256 + cs + cn, :128]
        second = total[256 + cs + cn :, 128:]
        node_rows = pl.ds(pair * z.pair_nodes, z.pair_nodes)
        slot_rows = pl.ds(pair * z.pair_slots, z.pair_slots)
        slot_pre_s[slot_rows, :] = jnp.concatenate([first[:cs], second[:cs]], axis=0).astype(low)
        recv_sum = jnp.concatenate([first[cs:], second[cs:]], axis=0)
        sums_s[0] += fold_rows(recv_sum)
        node_pre_s[node_rows, :] = recv_sum.astype(low)
        yield
        for k, act_s, gradient_s in ((1, act_one_s, slope_two_s), (2, act_two_s, message_s)):
            total = dot(
                jnp.concatenate([act_s[wide_rows, :].T, ones], axis=0), gradient_s[wide_rows, :]
            )
            grads_ref[pl.ds(512 + 128 * k, 128), :] += total[:128, :128] + total[128:256, 128:]
            sums_s[k] += (total[256:264, :128] + total[256:264, 128:]) * 0.125
            yield

    def group_end(group):
        node_rows = pl.ds(group * z.group_nodes, z.group_nodes)
        slot_rows = pl.ds(group * z.group_slots, z.group_slots)
        slot_grad_ref[slot_rows, :] = dot_nt(slot_pre_s[slot_rows, :], w_slot).astype(low)
        node_grad_ref[node_rows, :] += dot_nt(node_pre_s[node_rows, :], w_recv)
        yield
        grads_ref[128:256, :] += dot_tn(slot_ref[slot_rows, :], slot_pre_s[slot_rows, :])
        grads_ref[256:384, :] += dot_tn(node_in_ref[node_rows, :], node_pre_s[node_rows, :])
        yield

    emit(z.pairs, z.per_group, edge_forward, node_phase, edge_backward, group_end)


def layer_scratch(z):
    return [
        pltpu.VMEM((10, 8, 128), high),
        pltpu.VMEM((5, 256, 256), low),
        pltpu.VMEM((128, 256), low),
        pltpu.VMEM((z.tile, 128), low),
        pltpu.VMEM((z.tile_chunks, z.chunk_slots + z.chunk_nodes, z.chunk), low),
        pltpu.VMEM((z.tile // 2, 256), low),
        pltpu.VMEM((z.tile // 2, 256), low),
        pltpu.VMEM((z.tile // 2, 256), low),
        pltpu.VMEM((z.tile // 2, 256), low),
        pltpu.VMEM((z.tile, 128), high),
        pltpu.VMEM((z.tile, 128), low),
        pltpu.VMEM((z.tile // 2, 256), low),
        pltpu.VMEM((2, z.tile_nodes, 128), low),
        pltpu.VMEM((2, z.tile_nodes, 128), low),
        pltpu.VMEM((z.tile_nodes, 128), low),
        pltpu.VMEM((z.tile_nodes, 128), low),
        pltpu.VMEM((z.tile_nodes, 256), low),
        pltpu.VMEM((z.tile_slots, 128), low),
        pltpu.VMEM((z.tile_nodes, 128), low),
    ]


def layer_outputs(z, nodes, edges, slots):
    return [
        jax.ShapeDtypeStruct((nodes, 128), low),
        jax.ShapeDtypeStruct((edges, 128), low),
        jax.ShapeDtypeStruct((nodes, 128), high),
        jax.ShapeDtypeStruct((edges, 128), high),
        jax.ShapeDtypeStruct((slots, 128), low),
    ]


def layer_kernel(z, block_ref, *refs):
    inputs, weights, refs = refs[:8], refs[8:12], refs[12:]
    grads_in_ref, own, refs = refs[0], refs[1:6], refs[6:]
    results, grads_ref, staged, refs = refs[:5], refs[5], refs[6:11], refs[11:]
    carried, (own_sem, store_sem, *scratch) = refs[:5], refs[5:]
    step = pl.program_id(0)
    block, steps = block_ref[0], z.tiles - 1
    slot = lax.rem(step, 2)
    counts = [result.shape[0] // z.tiles for result in results]

    def stores(at, tile):
        return [
            pltpu.make_async_copy(
                place.at[at], result.at[pl.ds(tile * count, count), :], store_sem.at[at, k]
            )
            for k, (place, result, count) in enumerate(zip(staged, results, counts))
        ]

    own_loads = [
        pltpu.make_async_copy(source, place, own_sem.at[0, k])
        for k, (source, place) in enumerate(zip(own, carried))
    ]
    own_stores = [
        pltpu.make_async_copy(
            place, result.at[pl.ds(block * count, count), :], own_sem.at[1, k]
        )
        for k, (place, result, count) in enumerate(zip(carried, results, counts))
    ]

    def pass_on():
        for load, store in zip(own_loads, own_stores):
            load.wait()
            store.start()

    @pl.when(step == 0)
    def _():
        for load in own_loads:
            load.start()
        grads_ref[...] = grads_in_ref[...]
        prepare(weights[0], weights[2], weights[3], *scratch[:3])

    @pl.when(step == 1)
    def _():
        pass_on()

    @pl.when(step >= 2)
    def _():
        for copy in stores(slot, 0):
            copy.wait()

    tile = lax.rem(block + 1 + step, z.tiles)
    places = [place.at[slot] for place in staged]
    layer_tile(z, tile, *inputs, *weights, *places, grads_ref, *scratch)
    for copy in stores(slot, tile):
        copy.start()

    @pl.when(step == steps - 1)
    def _():
        close_sums(grads_ref, scratch[0])
        if steps == 1:
            pass_on()
        for store in own_stores:
            store.wait()
        if steps > 1:
            for copy in stores(1 - slot, 0):
                copy.wait()
        for copy in stores(slot, 0):
            copy.wait()


def layer_call(z, block, inputs, weights, grads, own):
    steps = z.tiles - 1

    def rows_spec(rows):
        return pl.BlockSpec((rows, 128), lambda i, block: (lax.rem(block[0] + 1 + i, z.tiles), 0))

    def whole(array):
        return pl.BlockSpec(
            array.shape, lambda i, block: (0,) * array.ndim, pipeline_mode=pl.Buffered(1)
        )

    hbm = pl.BlockSpec(memory_space=pltpu.HBM)
    shapes = layer_outputs(z, z.nodes, z.edges, z.slots)
    tile_shapes = layer_outputs(z, z.tile_nodes, z.tile, z.tile_slots)
    return pl.pallas_call(
        functools.partial(layer_kernel, z),
        grid_spec=pltpu.PrefetchScalarGridSpec(
            num_scalar_prefetch=1,
            grid=(steps,),
            in_specs=[
                pl.BlockSpec(memory_space=pltpu.SMEM),
                rows_spec(z.tile // 128),
                rows_spec(z.tile // 128),
                rows_spec(z.tile),
                rows_spec(z.tile),
                rows_spec(z.tile_nodes),
                rows_spec(z.tile_nodes),
                rows_spec(z.tile_slots),
            ]
            + [whole(w) for w in weights]
            + [whole(grads)]
            + [hbm] * 5,
            out_specs=[hbm] * 5 + [pl.BlockSpec(grads.shape, lambda i, block: (0, 0))],
            scratch_shapes=[pltpu.VMEM((2,) + item.shape, item.dtype) for item in tile_shapes]
            + [pltpu.VMEM(item.shape, item.dtype) for item in tile_shapes]
            + [pltpu.SemaphoreType.DMA((2, 5)), pltpu.SemaphoreType.DMA((2, 5))]
            + layer_scratch(z),
        ),
        out_shape=[*shapes, jax.ShapeDtypeStruct(grads.shape, high)],
        compiler_params=pltpu.CompilerParams(
            dimension_semantics=("arbitrary",), vmem_limit_bytes=VMEM
        ),
        name="layer",
    )(block, *inputs, *weights, grads, *own)


def signal(semaphore, where):
    pl.semaphore_signal(semaphore, inc=1, device_id=where, device_id_type=pl.DeviceIdType.MESH)


def send(source, target, send_sem, recv_sem, where):
    copy = pltpu.make_async_remote_copy(
        src_ref=source,
        dst_ref=target,
        send_sem=send_sem,
        recv_sem=recv_sem,
        device_id=where,
        device_id_type=pl.DeviceIdType.MESH,
    )
    copy.start()
    return copy


def fetch_kernel(z, peers, unroll, count_ref, *refs):
    request_ref, sources, weight_refs, refs = refs[0], refs[1:7], refs[7:11], refs[11:]
    rows_ref, asked_ref, block_ref, results, refs = refs[0], refs[1], refs[2], refs[3:9], refs[9:]
    wanted_v, asked_v, node_v, node_s, picked_s, out_s, refs = *refs[:6], refs[6:]
    ask_send, ask_recv, row_send, row_recv, load_sem, store_sem, refs = *refs[:6], refs[6:]
    loaded, weights, slot_v, staged, scratch = refs[:6], refs[6:10], refs[10], refs[11:17], refs[17:]
    me = lax.axis_index("dom")
    slots = picked_s.shape[0]
    mates = z.tile_slots // slots
    blocks = peers // mates
    block, place = lax.div(me, mates), lax.rem(me, mates)

    def peer(across, along, sign):
        return (
            lax.rem(block + (blocks + sign * across), blocks) * mates
            + lax.rem(place + (mates + sign * along), mates)
        )

    order = sorted(range(1, blocks), key=lambda across: (abs(2 * across - blocks), across))
    shifts = [(across, along) for across in order for along in range(mates)]
    shifts[mates:mates] = [(0, along) for along in range(1, mates)]
    barrier = pltpu.get_barrier_semaphore()
    for across, along in shifts:
        signal(barrier, {"dom": peer(across, along, 1)})
    loads = [
        pltpu.make_async_copy(request_ref, wanted_v, load_sem.at[0]),
        pltpu.make_async_copy(sources[4], node_v, load_sem.at[1]),
    ]
    for k, (source, target) in enumerate(zip(sources, loaded)):
        rows = target.shape[0]
        loads.append(
            pltpu.make_async_copy(
                source.at[pl.ds(block * rows, rows), :], target, load_sem.at[2 + k]
            )
        )
    for k, (source, target) in enumerate(zip(weight_refs, weights)):
        loads.append(pltpu.make_async_copy(source, target, load_sem.at[8 + k]))
    for load in loads:
        load.start()
    loads[0].wait()
    for k in range(peers):
        asked_v[k] = wanted_v[pl.ds(k, 1), :]
    loads[1].wait()
    node_s[...] = node_v[...].astype(high)
    block_ref[0] = block
    pl.semaphore_wait(barrier, peers - 1)
    asks = []
    for across, along in shifts:
        other, k = peer(across, along, 1), across * mates + along
        asks.append(
            send(
                asked_v.at[other],
                asked_v.at[peers + me],
                ask_send.at[k],
                ask_recv.at[k],
                {"dom": other},
            )
        )
    asked_v[peers + me] = asked_v[me]
    grads_v = staged[5]
    grads_v[...] = jnp.zeros_like(grads_v)
    for load in loads[8:]:
        load.wait()
    prepare(weights[0], weights[2], weights[3], *scratch[:3])
    for ask in asks:
        ask.wait_recv()
    local = pltpu.make_async_copy(asked_v.at[pl.ds(peers, peers)], asked_ref, load_sem.at[0])
    local.start()
    local.wait()
    sends, arrivals = [], []
    for across, along in shifts + [(0, 0)]:
        other, k = peer(across, along, -1), across * mates + along

        @pl.loop(0, slots // unroll)
        def _(group):
            for place in range(unroll):
                row = group * unroll + place
                index = asked_ref[other, 0, row]
                picked_s[pl.ds(row, 1), :] = node_s[pl.ds(index, 1), :]

        if not k:
            slot_v[place] = picked_s[...].astype(low)
            continue
        out_s[other] = picked_s[...].astype(low)
        target = rows_ref.at[me] if across else slot_v.at[place]
        copy = send(out_s.at[other], target, row_send.at[k], row_recv.at[k], {"dom": other})
        (sends if across else arrivals).append(copy)
    for load in loads[2:8]:
        load.wait()
    for copy in arrivals:
        copy.wait()
    slot_rows = slot_v.reshape(mates * slots, 128)
    layer_tile(z, block, count_ref, *loaded, slot_rows, *weights, *staged, *scratch)
    close_sums(grads_v, scratch[0])
    stores = [
        pltpu.make_async_copy(place, result, store_sem.at[k])
        for k, (place, result) in enumerate(zip(staged, results))
    ]
    for store in stores:
        store.start()
    for copy in asks:
        copy.wait_send()
    for copy in sends:
        copy.wait()
    for store in stores:
        store.wait()


def fetch_call(z, peers, count, request, ids, edges, nodes, weights):
    slots = request.shape[2]
    mates = z.tile_slots // slots
    dma = pltpu.SemaphoreType.DMA
    hbm = pl.BlockSpec(memory_space=pltpu.HBM)
    smem = pl.BlockSpec(memory_space=pltpu.SMEM)
    tile_shapes = layer_outputs(z, z.tile_nodes, z.tile, z.tile_slots)
    tile_shapes.append(jax.ShapeDtypeStruct((z.grad_rows, 128), high))
    ids_rows = z.tile // 128
    return pl.pallas_call(
        functools.partial(fetch_kernel, z, peers, 32),
        in_specs=[smem] + [hbm] * 11,
        out_specs=[hbm, smem, smem] + [hbm] * 6,
        out_shape=[
            jax.ShapeDtypeStruct((peers, slots, 128), low),
            jax.ShapeDtypeStruct((peers, 1, slots), jnp.int32),
            jax.ShapeDtypeStruct((1,), jnp.int32),
            *tile_shapes,
        ],
        scratch_shapes=[
            pltpu.VMEM((peers, slots), jnp.int32),
            pltpu.VMEM((2 * peers, 1, slots), jnp.int32),
            pltpu.VMEM((z.nodes, 128), low),
            pltpu.VMEM((z.nodes, 128), high),
            pltpu.VMEM((slots, 128), high),
            pltpu.VMEM((peers, slots, 128), low),
            dma((peers,)),
            dma((peers,)),
            dma((peers,)),
            dma((peers,)),
            dma((12,)),
            dma((6,)),
            pltpu.VMEM((ids_rows, 128), jnp.int32),
            pltpu.VMEM((ids_rows, 128), jnp.int32),
            pltpu.VMEM((z.tile, 128), low),
            pltpu.VMEM((z.tile, 128), low),
            pltpu.VMEM((z.tile_nodes, 128), low),
            pltpu.VMEM((z.tile_nodes, 128), low),
            *[pltpu.VMEM(w.shape, w.dtype) for w in weights],
            pltpu.VMEM((mates, slots, 128), low),
            *[pltpu.VMEM(item.shape, item.dtype) for item in tile_shapes],
            *layer_scratch(z),
        ],
        compiler_params=pltpu.CompilerParams(
            collective_id=0, has_side_effects=True, vmem_limit_bytes=VMEM
        ),
        name="fetch",
    )(count, request.reshape(peers, slots), *ids, *edges, *nodes, *weights)


def reduce_kernel(
    groups,
    peers,
    grads_ref,
    slot_grad_ref,
    sum_ref,
    back_ref,
    grads_s,
    all_s,
    half_out,
    half_in,
    half_sum,
    quarter_out,
    quarter_in,
    quarter_sum,
    piece_out,
    piece_in,
    back_send,
    back_recv,
    half_send,
    half_recv,
    quarter_send,
    quarter_recv,
    piece_send,
    piece_recv,
    load_sem,
):
    grp, dom = lax.axis_index("grp"), lax.axis_index("dom")
    core, level = lax.rem(dom, 2), lax.div(dom, 2)
    levels = peers // 2
    half, quarter, piece = half_sum.shape[0], quarter_sum.shape[0], piece_out.shape[1]
    barrier = pltpu.get_barrier_semaphore()
    for k in range(1, peers):
        signal(barrier, {"dom": lax.rem(dom + k, peers)})
    for k in range(1, groups):
        signal(barrier, {"grp": lax.rem(grp + k, groups)})
    twin = {"dom": 2 * level + 1 - core}
    loads = [
        pltpu.make_async_copy(
            grads_ref.at[pl.ds(first, half), :], grads_s.at[pl.ds(first, half), :], load_sem.at[k]
        )
        for k, first in enumerate(((1 - core) * half, core * half))
    ]
    loads.append(
        pltpu.make_async_copy(slot_grad_ref.at[dom], back_ref.at[dom], load_sem.at[2])
    )
    for load in loads:
        load.start()
    loads[0].wait()
    half_out[...] = grads_s[pl.ds((1 - core) * half, half), :].astype(low)
    loads[1].wait()
    pl.semaphore_wait(barrier, peers - 1 + groups - 1)

    sends = [send(half_out, half_in, half_send.at[0], half_recv.at[0], twin)]

    def give_back(k):
        other = lax.rem(dom + k, peers)
        return send(
            slot_grad_ref.at[other],
            back_ref.at[dom],
            back_send.at[k],
            back_recv.at[k],
            {"dom": other},
        )

    early = [k for k in range(1, peers) if 2 * k == peers or (2 * k < peers and k % 2)]
    backs = [give_back(k) for k in early]
    sends[0].wait_recv()
    half_sum[...] = grads_s[pl.ds(core * half, half), :] + half_in[...].astype(high)

    copies = []
    for k in range(1, groups):
        other = lax.rem(grp + k, groups)
        quarter_out[k] = half_sum[pl.ds(other * quarter, quarter), :].astype(low)
        copies.append(
            send(
                quarter_out.at[k],
                quarter_in.at[k],
                quarter_send.at[k],
                quarter_recv.at[k],
                {"grp": other},
            )
        )
    total = half_sum[pl.ds(grp * quarter, quarter), :]
    for k in range(1, groups):
        copies[k - 1].wait_recv()
        total = total + quarter_in[k].astype(high)
    quarter_sum[...] = total
    sends += copies

    copies = []
    for k in range(1, levels):
        other = lax.rem(level + k, levels)
        piece_out[k] = quarter_sum[pl.ds(other * piece, piece), :].astype(low)
        copies.append(
            send(
                piece_out.at[k],
                piece_in.at[k],
                piece_send.at[k],
                piece_recv.at[k],
                {"dom": 2 * other + core},
            )
        )
    total = quarter_sum[pl.ds(level * piece, piece), :]
    for k in range(1, levels):
        copies[k - 1].wait_recv()
        total = total + piece_in[k].astype(high)
    sends += copies

    own_half = core * half
    own_quarter = own_half + grp * quarter
    own_piece = own_quarter + level * piece
    all_s[pl.ds(own_piece, piece), :] = total.astype(low)
    copies = []
    for k in range(1, levels):
        place = all_s.at[pl.ds(own_piece, piece), :]
        where = {"dom": 2 * lax.rem(level + k, levels) + core}
        copies.append(
            send(place, place, piece_send.at[levels + k], piece_recv.at[levels + k], where)
        )
    backs += [give_back(k) for k in range(1, peers) if k not in early]
    for copy in copies:
        copy.wait_recv()
    sends += copies
    copies = []
    for k in range(1, groups):
        place = all_s.at[pl.ds(own_quarter, quarter), :]
        where = {"grp": lax.rem(grp + k, groups)}
        copies.append(
            send(place, place, quarter_send.at[groups + k], quarter_recv.at[groups + k], where)
        )
    for copy in copies:
        copy.wait_recv()
    sends += copies
    place = all_s.at[pl.ds(own_half, half), :]
    copy = send(place, place, half_send.at[1], half_recv.at[1], twin)
    copy.wait_recv()
    sends.append(copy)
    loads[2].wait()
    for copy in backs:
        copy.wait()
    for copy in sends:
        copy.wait_send()
    sum_ref[...] = all_s[...]


def reduce_call(groups, peers, grads, slot_grad):
    rows = grads.shape[0]
    levels = peers // 2
    half, quarter, piece = rows // 2, rows // 2 // groups, rows // 2 // groups // levels
    dma = pltpu.SemaphoreType.DMA
    return pl.pallas_call(
        functools.partial(reduce_kernel, groups, peers),
        in_specs=[pl.BlockSpec(memory_space=pltpu.HBM)] * 2,
        out_specs=[
            pl.BlockSpec(memory_space=pltpu.VMEM),
            pl.BlockSpec(memory_space=pltpu.HBM),
        ],
        out_shape=[
            jax.ShapeDtypeStruct((rows, 128), low),
            jax.ShapeDtypeStruct(slot_grad.shape, low),
        ],
        scratch_shapes=[
            pltpu.VMEM((rows, 128), high),
            pltpu.VMEM((rows, 128), low),
            pltpu.VMEM((half, 128), low),
            pltpu.VMEM((half, 128), low),
            pltpu.VMEM((half, 128), high),
            pltpu.VMEM((groups, quarter, 128), low),
            pltpu.VMEM((groups, quarter, 128), low),
            pltpu.VMEM((quarter, 128), high),
            pltpu.VMEM((levels, piece, 128), low),
            pltpu.VMEM((levels, piece, 128), low),
            dma((peers,)),
            dma((peers,)),
            dma((2,)),
            dma((2,)),
            dma((2 * groups,)),
            dma((2 * groups,)),
            dma((2 * levels,)),
            dma((2 * levels,)),
            dma((3,)),
        ],
        compiler_params=pltpu.CompilerParams(
            collective_id=1, has_side_effects=True, vmem_limit_bytes=VMEM
        ),
        name="reduce",
    )(grads, slot_grad)


def adamw_step(master, moment_mean, moment_var, average, gradient, factor):
    clipped = gradient * factor
    mean_new = beta_one * moment_mean + (1.0 - beta_one) * clipped
    var_new = beta_two * moment_var + (1.0 - beta_two) * clipped * clipped
    mean_hat = mean_new / (1.0 - beta_one**STEP)
    var_hat = var_new / (1.0 - beta_two**STEP)
    updated = master - learn_rate * (
        mean_hat / (jnp.sqrt(var_hat) + adam_eps) + decay_rate * master
    )
    return (
        mean_new,
        var_new,
        updated,
        updated.astype(low),
        ema_keep * average + (1.0 - ema_keep) * updated,
    )


FIRST = (0, 384, 640, 1152, 1162)


def finish_kernel(unroll, asked_ref, *refs):
    sources, (norm_ref, *results), refs = refs[:19], refs[19:41], refs[41:]
    loaded, (rows_s, *staged, load_sem, store_sem) = refs[:19], refs[19:]
    summed_s, back_s, node_s = loaded[16:]
    loads = [
        pltpu.make_async_copy(source, place, load_sem.at[k])
        for k, (source, place) in enumerate(zip(sources, loaded))
    ]
    for load in [*loads[17:], loads[16], *loads[:16]]:
        load.start()
    loads[17].wait()
    rows_s[...] = back_s[...].astype(high)
    slots = asked_ref.shape[2]
    loads[18].wait()

    @pl.loop(0, rows_s.shape[0] // unroll)
    def _(group):
        base = group * unroll
        peer, first = lax.div(base, slots), lax.rem(base, slots)
        places = [pl.ds(asked_ref[peer, 0, first + k], 1) for k in range(unroll)]
        values = [
            node_s[place, :] + rows_s[pl.ds(base + k, 1), :] for k, place in enumerate(places)
        ]
        for place, value in zip(places, values):
            node_s[place, :] = value

    stores = [pltpu.make_async_copy(node_s, results[20], store_sem.at[20])]
    stores[0].start()
    for load in loads[:17]:
        load.wait()
    gradient = summed_s[...].astype(high)
    square = jnp.sum(gradient * gradient, axis=0, keepdims=True)
    grad_norm = jnp.sqrt(jnp.sum(square, axis=1, keepdims=True))
    norm_ref[0] = grad_norm[0, 0]
    factor = clip_level / jnp.maximum(grad_norm, clip_level)
    for k in range(4):
        values = [place[...] for place in loaded[4 * k : 4 * k + 4]]
        updates = adamw_step(*values, gradient[FIRST[k] : FIRST[k + 1]], factor)
        for place, value in enumerate(updates):
            place += 5 * k
            staged[place][...] = value
            store = pltpu.make_async_copy(staged[place], results[place], store_sem.at[place])
            store.start()
            stores.append(store)
    for store in stores:
        store.wait()


def finish_call(asked, part, back, summed, tensors):
    smem = pl.BlockSpec(memory_space=pltpu.SMEM)
    hbm = pl.BlockSpec(memory_space=pltpu.HBM)
    sources = [*tensors, summed, back, part]
    shapes = []
    for k in range(4):
        shape = tensors[4 * k].shape
        shapes += [jax.ShapeDtypeStruct(shape, kind) for kind in (high, high, high, low, high)]
    return pl.pallas_call(
        functools.partial(finish_kernel, 32),
        in_specs=[smem] + [hbm] * 19,
        out_specs=[smem] + [hbm] * 21,
        out_shape=[
            jax.ShapeDtypeStruct((1,), high),
            *shapes,
            jax.ShapeDtypeStruct(part.shape, high),
        ],
        scratch_shapes=[
            *[pltpu.VMEM(item.shape, item.dtype) for item in sources],
            pltpu.VMEM(back.shape, high),
            *[pltpu.VMEM(item.shape, item.dtype) for item in shapes],
            pltpu.SemaphoreType.DMA((19,)),
            pltpu.SemaphoreType.DMA((21,)),
        ],
        compiler_params=pltpu.CompilerParams(vmem_limit_bytes=VMEM),
        name="finish",
    )(asked, *sources)


def shards(
    node_in,
    edge_in,
    edge_slot,
    edge_receiver,
    edge_count,
    request,
    node_cot,
    edge_cot,
    *tensors,
):
    groups, peers = lax.axis_size("grp"), lax.axis_size("dom")
    slots = request.shape[2]
    z = Sizes(edge_in.shape[0], node_in.shape[0], peers * slots, groups * peers)
    weights = tensors[::4]
    ids = (edge_slot.reshape(-1, 128), edge_receiver.reshape(-1, 128))
    slot_rows, asked, block, *own, grads = fetch_call(
        z,
        peers,
        edge_count,
        request,
        ids,
        (edge_in, edge_cot),
        (node_in, node_cot),
        weights,
    )
    node_out, edge_out, node_part, edge_grad, slot_grad, grads = layer_call(
        z,
        block,
        (
            edge_count,
            *ids,
            edge_in,
            edge_cot,
            node_in,
            node_cot,
            slot_rows.reshape(peers * slots, 128),
        ),
        weights,
        grads,
        own,
    )
    summed, returned = reduce_call(groups, peers, grads, slot_grad.reshape(peers, slots, 128))
    flat = [tensor.reshape(-1, 128) for tensor in tensors]
    grad_norm, *results, node_grad = finish_call(
        asked, node_part, returned.reshape(peers * slots, 128), summed, flat
    )
    results = [value.reshape(tensors[k // 5 * 4].shape) for k, value in enumerate(results)]
    return (node_out, edge_out, node_grad, edge_grad, grad_norm.reshape(()), *results)


def solution(mesh):
    rows = P(("grp", "dom"), None)
    in_specs = (
        rows,
        rows,
        P(("grp", "dom")),
        P(("grp", "dom")),
        P(("grp", "dom")),
        P(("grp", "dom"), None, None),
        rows,
        rows,
    ) + (P(),) * 16
    out_specs = (rows,) * 4 + (P(),) * 21
    return jax.shard_map(shards, mesh=mesh, in_specs=in_specs, out_specs=out_specs, check_vma=False)
```

```python
import functools
import math

import jax
import jax.numpy as jnp
from jax import lax
from jax.experimental import pallas as pl
from jax.experimental.pallas import tpu as pltpu
from jax.sharding import PartitionSpec as P

STEP = 10

eps_norm = 1e-05
beta_one = 0.5
beta_two = 0.6
learn_rate = 0.08
decay_rate = 0.01
adam_eps = 1e-08
ema_keep = 0.9
clip_level = 1.0

gelu_in = math.sqrt(2.0 / math.pi)
gelu_cube = gelu_in * 0.044715

low = jnp.bfloat16
high = jnp.float32

GAP = 4
PIECE = 64
PIECE_NORM = 32
VMEM = 60 * 1024 * 1024
PAIRS = 8


def dot(operand, weights):
    return jnp.dot(operand, weights, preferred_element_type=high)


def dot_nt(operand, weights):
    return lax.dot_general(
        operand, weights, (((1,), (1,)), ((), ())), preferred_element_type=high
    )


def dot_tn(operand, weights):
    return lax.dot_general(
        operand, weights, (((0,), (0,)), ((), ())), preferred_element_type=high
    )


def gelu_pair(x):
    square = x * x
    t = jnp.tanh(x * (gelu_in + gelu_cube * square))
    above = 1.0 + t
    value = (0.5 * x) * above
    slope = 0.5 * above + (value * (1.0 - t)) * (gelu_in + (3.0 * gelu_cube) * square)
    return value.astype(low), slope.astype(low)


def fold_rows(values):
    return jnp.sum(values.reshape(values.shape[0] // 8, 8, values.shape[1]), axis=0)


def emit(pairs, per_group, forward, middle, backward, end):
    groups = pairs // per_group
    streams = {"forward": forward, "middle": middle, "backward": backward, "end": end}
    started = dict.fromkeys(streams, 0)
    last = dict.fromkeys(streams, -GAP)
    active, done, now = [], set(), 0

    def ready(name, k):
        if name == "middle":
            return all(("forward", k * per_group + j) in done for j in range(per_group))
        if name == "end":
            return all(("backward", k * per_group + j) in done for j in range(per_group))
        return name == "forward" or ("middle", k // per_group) in done

    while len(done) < 2 * pairs + 2 * groups:
        for name in streams:
            k = started[name]
            count = pairs if name in ("forward", "backward") else groups
            if k < count and now - last[name] >= GAP and ready(name, k):
                active.append(((name, k), streams[name](k)))
                started[name], last[name] = k + 1, now
        for item in list(active):
            try:
                next(item[1])
            except StopIteration:
                active.remove(item)
                done.add(item[0])
        now += 1


class Sizes:
    def __init__(self, edges, nodes, slots, devices):
        self.edges, self.nodes, self.slots = edges, nodes, slots
        blocks = edges // 128
        self.rwin = nodes // blocks
        self.swin = slots // blocks
        self.sub = 4
        while self.sub * (self.rwin + self.swin) > 128:
            self.sub //= 2
        self.chunk = self.sub * 128
        self.chunk_slots = self.sub * self.swin
        self.chunk_nodes = self.sub * self.rwin
        self.pair_nodes, self.pair_slots = 2 * self.chunk_nodes, 2 * self.chunk_slots
        self.per_group = 4
        self.pairs = PAIRS
        self.group_nodes = self.per_group * self.pair_nodes
        self.group_slots = self.per_group * self.pair_slots
        self.tile = self.pairs * 2 * self.chunk
        self.tile_chunks = 2 * self.pairs
        self.tile_nodes = self.pairs * self.pair_nodes
        self.tile_slots = self.pairs * self.pair_slots
        self.steps = edges // self.tile
        self.grad_rows = -(-1162 // (16 * devices)) * 16 * devices


def diagonal(first, second):
    zero_a = jnp.zeros((first.shape[0], second.shape[1]), first.dtype)
    zero_b = jnp.zeros((second.shape[0], first.shape[1]), first.dtype)
    return jnp.concatenate(
        [
            jnp.concatenate([first, zero_a], axis=1),
            jnp.concatenate([zero_b, second], axis=1),
        ],
        axis=0,
    )


def twice(row):
    return jnp.concatenate([row, row], axis=1)


def layer_kernel(
    z,
    count_ref,
    slot_ids_ref,
    recv_ids_ref,
    edge_in_ref,
    edge_cot_ref,
    node_in_ref,
    node_cot_ref,
    slot_ref,
    edge_entry_ref,
    node_entry_ref,
    inner_ref,
    vec_ref,
    node_out_ref,
    edge_out_ref,
    node_grad_ref,
    edge_grad_ref,
    slot_grad_ref,
    grads_ref,
    pick_s,
    pick_t,
    act_one_s,
    act_two_s,
    slope_one_s,
    slope_two_s,
    normed_s,
    inverse_s,
    message_s,
    node_act_s,
    node_slope_s,
    node_back_s,
    gathered_s,
    table_s,
    slot_pre_s,
    node_pre_s,
    slot_sum_s,
    recv_sum_s,
    sums_s,
    wide_s,
    below_s,
):
    step = pl.program_id(0)
    chunk, cn, cs = z.chunk, z.chunk_nodes, z.chunk_slots
    pad = 128 - cn - cs
    vec = [vec_ref[pl.ds(k, 1), :] for k in range(10)]

    @pl.when(step == 0)
    def _():
        grads_ref[...] = jnp.zeros_like(grads_ref)
        sums_s[...] = jnp.zeros_like(sums_s)
        first, second = inner_ref[0].astype(low), inner_ref[1].astype(low)
        wide_s[0] = diagonal(first, first)
        middle = second.astype(high)
        middle = (middle - jnp.mean(middle, axis=1, keepdims=True)).astype(low)
        wide_s[1] = diagonal(middle, middle)
        for k, weights in ((2, inner_ref[0]), (3, inner_ref[1]), (4, edge_entry_ref[0:128, :])):
            weights = weights.T.astype(low)
            wide_s[k] = diagonal(weights, weights)
        part = jnp.full((128, 128), 1.0 / 128.0, low)
        wide_s[5] = diagonal(part, part)
        row = lax.broadcasted_iota(jnp.int32, (128, 128), 0)
        column = lax.broadcasted_iota(jnp.int32, (128, 128), 1)
        gain = jnp.broadcast_to(vec[3] * (1.0 / 128.0), (128, 128)).T.astype(low)
        wide_s[6] = diagonal(gain, gain)
        below_s[:, :128] = jnp.where(row == column, 1.0, 0.0).astype(low)
        below_s[:, 128:] = gain

    edge_low = edge_entry_ref[...].astype(low)
    node_low = node_entry_ref[...].astype(low)
    inner_low = [None, None, inner_ref[2].astype(low), inner_ref[3].astype(low)]
    w_edge, w_slot, w_recv = edge_low[:128], edge_low[128:256], edge_low[256:]
    bias_three = vec[2] - jnp.mean(vec[2], axis=1, keepdims=True)
    gain_part = below_s[:, 128:]
    slot_pre_s[...] = dot(slot_ref[...], w_slot).astype(low)
    node_pre_s[...] = (dot(node_in_ref[...], w_recv) + vec[0]).astype(low)

    def live_rows(index, first, count):
        rows = lax.broadcasted_iota(jnp.int32, (count, 128), 0)
        return rows < count_ref[0] - (step * z.tile + index * chunk + first)

    def sides(wide):
        return wide[:, :128], wide[:, 128:]

    def chunk_rows(index):
        return pl.ds(index * chunk, chunk)

    def hot_block(block, k):
        pieces = []
        number = step * (z.tile // 128) + block
        for ref, width, count in ((slot_ids_ref, z.swin, cs), (recv_ids_ref, z.rwin, cn)):
            ids = ref[pl.ds(block, 1), :] - number * width
            band = lax.broadcasted_iota(jnp.int32, (width, 128), 0) == ids
            above, below = k * width, count - (k + 1) * width
            if above:
                pieces.append(jnp.zeros((above, 128), high))
            pieces.append(jnp.where(band, 1.0, 0.0))
            if below:
                pieces.append(jnp.zeros((below, 128), high))
        if pad:
            pieces.append(jnp.zeros((pad, 128), high))
        return jnp.concatenate(pieces, axis=0).astype(low)

    def row_pieces(count, rows):
        rows = min(count, rows)
        return [(first, first + rows) for first in range(0, count, rows)]

    def gelu_rows(pre, act_s, slope_s, base):
        for first, last in row_pieces(pre.shape[0], PIECE):
            act, slope = gelu_pair(pre[first:last].astype(low))
            act_s[pl.ds(base + first, last - first), :] = act
            slope_s[pl.ds(base + first, last - first), :] = slope

    def edge_forward(pair):
        base = pair * chunk
        wide_rows = chunk_rows(pair)
        indices = (2 * pair, 2 * pair + 1)
        for index in indices:
            for k in range(z.sub):
                block = index * z.sub + k
                hot_t = hot_block(block, k)
                pick_t[index, :, k * 128 : (k + 1) * 128] = hot_t[: cs + cn]
                pick_s[pl.ds(block * 128, 128), :] = hot_t.T
        yield
        pres = []
        for index in indices:
            tables = [
                w_edge,
                slot_pre_s[pl.ds(index * cs, cs), :],
                node_pre_s[pl.ds(index * cn, cn), :],
            ]
            if pad:
                tables.append(jnp.zeros((pad, 128), low))
            entry = jnp.concatenate(
                [edge_in_ref[chunk_rows(index), :], pick_s[chunk_rows(index), :]], axis=1
            )
            pres.append(dot(entry, jnp.concatenate(tables, axis=0)))
        yield
        gelu_rows(jnp.concatenate(pres, axis=1), act_one_s, slope_one_s, base)
        yield
        pre_two = dot(act_one_s[wide_rows, :], wide_s[0])
        yield
        bias = twice(vec[1])
        for first, last in row_pieces(chunk, PIECE):
            act, slope = gelu_pair((pre_two[first:last] + bias).astype(low))
            act_two_s[pl.ds(base + first, last - first), :] = act
            slope_two_s[pl.ds(base + first, last - first), :] = slope
        yield
        pre_three = dot(act_two_s[wide_rows, :], wide_s[1])
        yield
        for side, index in enumerate(indices):
            half = pre_three[:, side * 128 : (side + 1) * 128]
            for first, last in row_pieces(chunk, PIECE_NORM):
                rows = pl.ds(index * chunk + first, last - first)
                live = live_rows(index, first, last - first)
                center = half[first:last] + bias_three
                inverse = lax.rsqrt(jnp.mean(center * center, axis=1, keepdims=True) + eps_norm)
                inverse = jnp.where(live, inverse, 0.0)
                normed = center * inverse
                normed_s[rows, :] = normed
                inverse_s[rows, :] = inverse
                message = jnp.where(live, normed * vec[3] + vec[4], 0.0)
                edge_out_ref[rows, :] = (edge_in_ref[rows, :].astype(high) + message).astype(low)
                message_s[
                    pl.ds(base + first, last - first), side * 128 : (side + 1) * 128
                ] = message.astype(low)
            yield
        hots = [pick_t[index, cs : cs + cn, :] for index in indices]
        total = dot(jnp.concatenate(hots, axis=0), message_s[wide_rows, :]).astype(low)
        gathered_s[pl.ds(indices[0] * cn, cn), :] = total[:cn, :128]
        gathered_s[pl.ds(indices[1] * cn, cn), :] = total[cn:, 128:]
        yield

    def node_phase(group):
        base = group * z.group_nodes
        rows = pl.ds(base, z.group_nodes)
        parts = row_pieces(z.group_nodes, PIECE)

        def here(first, last):
            return pl.ds(base + first, last - first)

        entry = jnp.concatenate([node_in_ref[rows, :], gathered_s[rows, :]], axis=1)
        pre = dot(entry, node_low)
        yield
        for first, last in parts:
            act, slope = gelu_pair(pre[first:last] + vec[5])
            node_act_s[0, here(first, last), :] = act
            node_slope_s[0, here(first, last), :] = slope
        yield
        pre = dot(node_act_s[0, rows, :], inner_low[2])
        yield
        for first, last in parts:
            act, slope = gelu_pair(pre[first:last] + vec[6])
            node_act_s[1, here(first, last), :] = act
            node_slope_s[1, here(first, last), :] = slope
        yield
        pre = dot(node_act_s[1, rows, :], inner_low[3])
        yield
        for first, last in parts:
            piece = here(first, last)
            value = pre[first:last] + vec[7]
            center = value - jnp.mean(value, axis=1, keepdims=True)
            inverse = lax.rsqrt(jnp.mean(center * center, axis=1, keepdims=True) + eps_norm)
            normed = center * inverse
            node_out_ref[piece, :] = (
                node_in_ref[piece, :].astype(high) + normed * vec[8] + vec[9]
            ).astype(low)
            upstream = node_cot_ref[piece, :].astype(high)
            sums_s[8] += fold_rows(upstream * normed)
            sums_s[9] += fold_rows(upstream)
            upper = upstream * vec[8]
            mean_plain = jnp.mean(upper, axis=1, keepdims=True)
            mean_cross = jnp.mean(upper * normed, axis=1, keepdims=True)
            d_three = inverse * (upper - mean_plain - normed * mean_cross)
            sums_s[7] += fold_rows(d_three)
            node_back_s[2, piece, :] = d_three.astype(low)
        yield
        for k in (1, 0):
            back = dot_nt(node_back_s[k + 1, rows, :], inner_low[2 + k])
            yield
            for first, last in parts:
                piece = here(first, last)
                value = back[first:last] * node_slope_s[k, piece, :].astype(high)
                sums_s[5 + k] += fold_rows(value)
                node_back_s[k, piece, :] = value.astype(low)
            yield
        back = dot_nt(node_back_s[0, rows, :], node_low)
        for first, last in parts:
            piece = here(first, last)
            node_grad_ref[piece, :] = node_cot_ref[piece, :].astype(high) + back[first:last, :128]
            table_s[piece, :128] = back[first:last, 128:].astype(low)
        yield
        table_s[rows, 128:] = dot(table_s[rows, :128], gain_part).astype(low)
        yield
        grads_ref[384:640, :] += dot_tn(entry, node_back_s[0, rows, :])
        grads_ref[896:1024, :] += dot_tn(node_act_s[0, rows, :], node_back_s[1, rows, :])
        grads_ref[1024:1152, :] += dot_tn(node_act_s[1, rows, :], node_back_s[2, rows, :])
        yield

    def edge_backward(pair):
        base = pair * chunk
        wide_rows = chunk_rows(pair)
        indices = (2 * pair, 2 * pair + 1)
        for side, index in enumerate(indices):
            tables = [
                jnp.zeros((cs, 256), low),
                table_s[pl.ds(index * cn, cn), :],
            ]
            if pad:
                tables.append(jnp.zeros((pad, 256), low))
            tables.append(below_s[...])
            entry = jnp.concatenate(
                [pick_s[chunk_rows(index), :], edge_cot_ref[chunk_rows(index), :]], axis=1
            )
            arrived = dot(entry, jnp.concatenate(tables, axis=0))
            yield
            gain_sum = jnp.zeros((8, 128), high)
            shift_sum = jnp.zeros((8, 128), high)
            for first, last in row_pieces(chunk, PIECE_NORM):
                rows = pl.ds(index * chunk + first, last - first)
                upstream, plain = sides(arrived[first:last])
                normed = normed_s[rows, :]
                cross = upstream * normed
                gain_sum = gain_sum + fold_rows(cross)
                live = live_rows(index, first, last - first)
                shift_sum = shift_sum + fold_rows(jnp.where(live, upstream, 0.0))
                cross = jnp.mean(cross * vec[3], axis=1, keepdims=True)
                d_three = inverse_s[rows, :] * (upstream * vec[3] - plain - normed * cross)
                message_s[
                    pl.ds(base + first, last - first), side * 128 : (side + 1) * 128
                ] = d_three.astype(low)
            sums_s[3] += gain_sum
            sums_s[4] += shift_sum
            yield
        for gradient_s, slope_s, weights in ((message_s, slope_two_s, 3), (slope_two_s, slope_one_s, 2)):
            back = dot(gradient_s[wide_rows, :], wide_s[weights])
            yield
            for first, last in row_pieces(chunk, PIECE):
                rows = pl.ds(base + first, last - first)
                slope_s[rows, :] = back[first:last].astype(low) * slope_s[rows, :]
            yield
        back = dot(slope_one_s[wide_rows, :], wide_s[4])
        yield
        for index, half in zip(indices, sides(back)):
            for first, last in row_pieces(chunk, PIECE):
                rows = pl.ds(index * chunk + first, last - first)
                edge_grad_ref[rows, :] = edge_cot_ref[rows, :].astype(high) + half[first:last]
        yield
        ones = jnp.ones((16, chunk), low)
        entry = [edge_in_ref[chunk_rows(index), :].T for index in indices]
        hots = [pick_t[index, : cs + cn, :] for index in indices]
        total = dot(jnp.concatenate(entry + hots, axis=0), slope_one_s[wide_rows, :])
        grads_ref[0:128, :] += total[:128, :128] + total[128:256, 128:]
        first = total[256 : 256 + cs + cn, :128]
        second = total[256 + cs + cn :, 128:]
        node_rows = pl.ds(pair * z.pair_nodes, z.pair_nodes)
        slot_rows = pl.ds(pair * z.pair_slots, z.pair_slots)
        slot_sum_s[slot_rows, :] = jnp.concatenate([first[:cs], second[:cs]], axis=0).astype(low)
        recv_sum = jnp.concatenate([first[cs:], second[cs:]], axis=0)
        sums_s[0] += fold_rows(recv_sum)
        recv_sum_s[node_rows, :] = recv_sum.astype(low)
        yield
        for k, act_s, gradient_s in ((1, act_one_s, slope_two_s), (2, act_two_s, message_s)):
            total = dot(
                jnp.concatenate([act_s[wide_rows, :].T, ones], axis=0), gradient_s[wide_rows, :]
            )
            grads_ref[pl.ds(512 + 128 * k, 128), :] += total[:128, :128] + total[128:256, 128:]
            sums_s[k] += (total[256:264, :128] + total[256:264, 128:]) * 0.125
            yield

    def group_end(group):
        node_rows = pl.ds(group * z.group_nodes, z.group_nodes)
        slot_rows = pl.ds(group * z.group_slots, z.group_slots)
        slot_grad_ref[slot_rows, :] = dot_nt(slot_sum_s[slot_rows, :], w_slot).astype(low)
        node_grad_ref[node_rows, :] += dot_nt(recv_sum_s[node_rows, :], w_recv)
        yield
        grads_ref[128:256, :] += dot_tn(slot_ref[slot_rows, :], slot_sum_s[slot_rows, :])
        grads_ref[256:384, :] += dot_tn(node_in_ref[node_rows, :], recv_sum_s[node_rows, :])
        yield

    emit(z.pairs, z.per_group, edge_forward, node_phase, edge_backward, group_end)

    @pl.when(step == z.steps - 1)
    def _():
        grads_ref[1152:1162, :] = jnp.sum(sums_s[...], axis=1)


def layer_call(z, count, slot_ids, recv_ids, edge_in, edge_cot, node_in, node_cot, slot_rows, weights):
    def rows_spec(rows):
        return pl.BlockSpec((rows, 128), lambda i: (i, 0))

    def whole(array):
        return pl.BlockSpec(array.shape, lambda i: (0,) * array.ndim)

    return pl.pallas_call(
        functools.partial(layer_kernel, z),
        grid=(z.steps,),
        in_specs=[
            pl.BlockSpec(memory_space=pltpu.SMEM),
            rows_spec(z.tile // 128),
            rows_spec(z.tile // 128),
            rows_spec(z.tile),
            rows_spec(z.tile),
            rows_spec(z.tile_nodes),
            rows_spec(z.tile_nodes),
            rows_spec(z.tile_slots),
        ]
        + [whole(w) for w in weights],
        out_specs=[
            rows_spec(z.tile_nodes),
            rows_spec(z.tile),
            rows_spec(z.tile_nodes),
            rows_spec(z.tile),
            rows_spec(z.tile_slots),
            pl.BlockSpec((z.grad_rows, 128), lambda i: (0, 0)),
        ],
        out_shape=[
            jax.ShapeDtypeStruct((z.nodes, 128), low),
            jax.ShapeDtypeStruct((z.edges, 128), low),
            jax.ShapeDtypeStruct((z.nodes, 128), high),
            jax.ShapeDtypeStruct((z.edges, 128), high),
            jax.ShapeDtypeStruct((z.slots, 128), low),
            jax.ShapeDtypeStruct((z.grad_rows, 128), high),
        ],
        scratch_shapes=[
            pltpu.VMEM((z.tile, 128), low),
            pltpu.VMEM((z.tile_chunks, z.chunk_slots + z.chunk_nodes, z.chunk), low),
            pltpu.VMEM((z.tile // 2, 256), low),
            pltpu.VMEM((z.tile // 2, 256), low),
            pltpu.VMEM((z.tile // 2, 256), low),
            pltpu.VMEM((z.tile // 2, 256), low),
            pltpu.VMEM((z.tile, 128), high),
            pltpu.VMEM((z.tile, 128), high),
            pltpu.VMEM((z.tile // 2, 256), low),
            pltpu.VMEM((2, z.tile_nodes, 128), low),
            pltpu.VMEM((2, z.tile_nodes, 128), low),
            pltpu.VMEM((3, z.tile_nodes, 128), low),
            pltpu.VMEM((z.tile_nodes, 128), low),
            pltpu.VMEM((z.tile_nodes, 256), low),
            pltpu.VMEM((z.tile_slots, 128), low),
            pltpu.VMEM((z.tile_nodes, 128), low),
            pltpu.VMEM((z.tile_slots, 128), low),
            pltpu.VMEM((z.tile_nodes, 128), low),
            pltpu.VMEM((10, 8, 128), high),
            pltpu.VMEM((7, 256, 256), low),
            pltpu.VMEM((128, 256), low),
        ],
        compiler_params=pltpu.CompilerParams(
            dimension_semantics=("arbitrary",), vmem_limit_bytes=VMEM
        ),
        name="layer",
    )(count, slot_ids, recv_ids, edge_in, edge_cot, node_in, node_cot, slot_rows, *weights)


def signal(semaphore, where):
    pl.semaphore_signal(semaphore, inc=1, device_id=where, device_id_type=pl.DeviceIdType.MESH)


def send(source, target, send_sem, recv_sem, where):
    copy = pltpu.make_async_remote_copy(
        src_ref=source,
        dst_ref=target,
        send_sem=send_sem,
        recv_sem=recv_sem,
        device_id=where,
        device_id_type=pl.DeviceIdType.MESH,
    )
    copy.start()
    return copy


def fetch_kernel(
    peers,
    unroll,
    request_ref,
    node_ref,
    rows_ref,
    asked_ref,
    wanted_v,
    asked_v,
    node_v,
    node_s,
    picked_s,
    out_s,
    ask_send,
    ask_recv,
    row_send,
    row_recv,
    load_sem,
):
    me = lax.axis_index("dom")
    slots = picked_s.shape[0]
    barrier = pltpu.get_barrier_semaphore()
    for k in range(1, peers):
        signal(barrier, {"dom": lax.rem(me + k, peers)})
    loads = [
        pltpu.make_async_copy(request_ref, wanted_v, load_sem.at[0]),
        pltpu.make_async_copy(node_ref, node_v, load_sem.at[1]),
    ]
    for load in loads:
        load.start()
    loads[0].wait()
    for k in range(peers):
        asked_v[k] = wanted_v[pl.ds(k, 1), :]
    loads[1].wait()
    node_s[...] = node_v[...].astype(high)
    pl.semaphore_wait(barrier, peers - 1)
    shifts = [peers // 2 + (k // 2) * (1 - 2 * (k % 2)) for k in range(1, peers)]
    asks = [
        send(
            asked_v.at[lax.rem(me + k, peers)],
            asked_v.at[peers + me],
            ask_send.at[k],
            ask_recv.at[k],
            {"dom": lax.rem(me + k, peers)},
        )
        for k in shifts
    ]
    asked_v[peers + me] = asked_v[me]
    for ask in asks:
        ask.wait_recv()
    local = pltpu.make_async_copy(asked_v.at[pl.ds(peers, peers)], asked_ref, load_sem.at[0])
    local.start()
    local.wait()
    sends = []
    for k in shifts + [0]:
        other = lax.rem(me + (peers - k), peers)

        @pl.loop(0, slots // unroll)
        def _(group):
            for place in range(unroll):
                row = group * unroll + place
                index = asked_ref[other, 0, row]
                picked_s[pl.ds(row, 1), :] = node_s[pl.ds(index, 1), :]

        out_s[other] = picked_s[...].astype(low)
        if k:
            sends.append(
                send(
                    out_s.at[other],
                    rows_ref.at[me],
                    row_send.at[k],
                    row_recv.at[k],
                    {"dom": other},
                )
            )
    local = pltpu.make_async_copy(out_s.at[me], rows_ref.at[me], load_sem.at[0])
    local.start()
    for copy in asks:
        copy.wait_send()
    local.wait()
    for copy in sends:
        copy.wait()


def fetch_call(peers, request, node_in):
    slots = request.shape[2]
    dma = pltpu.SemaphoreType.DMA
    hbm = pl.BlockSpec(memory_space=pltpu.HBM)
    return pl.pallas_call(
        functools.partial(fetch_kernel, peers, 32),
        in_specs=[hbm, hbm],
        out_specs=[hbm, pl.BlockSpec(memory_space=pltpu.SMEM)],
        out_shape=[
            jax.ShapeDtypeStruct((peers, slots, 128), low),
            jax.ShapeDtypeStruct((peers, 1, slots), jnp.int32),
        ],
        scratch_shapes=[
            pltpu.VMEM((peers, slots), jnp.int32),
            pltpu.VMEM((2 * peers, 1, slots), jnp.int32),
            pltpu.VMEM(node_in.shape, low),
            pltpu.VMEM(node_in.shape, high),
            pltpu.VMEM((slots, 128), high),
            pltpu.VMEM((peers, slots, 128), low),
            dma((peers,)),
            dma((peers,)),
            dma((peers,)),
            dma((peers,)),
            dma((2,)),
        ],
        compiler_params=pltpu.CompilerParams(
            collective_id=0, has_side_effects=True, vmem_limit_bytes=VMEM
        ),
        name="fetch",
    )(request.reshape(peers, slots), node_in)


def reduce_kernel(
    groups,
    peers,
    grads_ref,
    slot_grad_ref,
    sum_ref,
    back_ref,
    grads_s,
    all_s,
    half_out,
    half_in,
    half_sum,
    quarter_out,
    quarter_in,
    quarter_sum,
    piece_out,
    piece_in,
    back_send,
    back_recv,
    half_send,
    half_recv,
    quarter_send,
    quarter_recv,
    piece_send,
    piece_recv,
    load_sem,
):
    grp, dom = lax.axis_index("grp"), lax.axis_index("dom")
    core, level = lax.rem(dom, 2), lax.div(dom, 2)
    levels = peers // 2
    half, quarter, piece = half_sum.shape[0], quarter_sum.shape[0], piece_out.shape[1]
    barrier = pltpu.get_barrier_semaphore()
    for k in range(1, peers):
        signal(barrier, {"dom": lax.rem(dom + k, peers)})
    for k in range(1, groups):
        signal(barrier, {"grp": lax.rem(grp + k, groups)})
    twin = {"dom": 2 * level + 1 - core}
    loads = [
        pltpu.make_async_copy(
            grads_ref.at[pl.ds(first, half), :], grads_s.at[pl.ds(first, half), :], load_sem.at[k]
        )
        for k, first in enumerate(((1 - core) * half, core * half))
    ]
    loads.append(
        pltpu.make_async_copy(slot_grad_ref.at[dom], back_ref.at[dom], load_sem.at[2])
    )
    for load in loads:
        load.start()
    loads[0].wait()
    half_out[...] = grads_s[pl.ds((1 - core) * half, half), :].astype(low)
    loads[1].wait()
    pl.semaphore_wait(barrier, peers - 1 + groups - 1)

    sends = [send(half_out, half_in, half_send.at[0], half_recv.at[0], twin)]

    def give_back(k):
        other = lax.rem(dom + k, peers)
        return send(
            slot_grad_ref.at[other],
            back_ref.at[dom],
            back_send.at[k],
            back_recv.at[k],
            {"dom": other},
        )

    early = [k for k in range(1, peers) if 2 * k == peers or (2 * k < peers and k % 2)]
    backs = [give_back(k) for k in early]
    sends[0].wait_recv()
    half_sum[...] = grads_s[pl.ds(core * half, half), :] + half_in[...].astype(high)

    copies = []
    for k in range(1, groups):
        other = lax.rem(grp + k, groups)
        quarter_out[k] = half_sum[pl.ds(other * quarter, quarter), :].astype(low)
        copies.append(
            send(
                quarter_out.at[k],
                quarter_in.at[k],
                quarter_send.at[k],
                quarter_recv.at[k],
                {"grp": other},
            )
        )
    total = half_sum[pl.ds(grp * quarter, quarter), :]
    for k in range(1, groups):
        copies[k - 1].wait_recv()
        total = total + quarter_in[k].astype(high)
    quarter_sum[...] = total
    sends += copies

    copies = []
    for k in range(1, levels):
        other = lax.rem(level + k, levels)
        piece_out[k] = quarter_sum[pl.ds(other * piece, piece), :].astype(low)
        copies.append(
            send(
                piece_out.at[k],
                piece_in.at[k],
                piece_send.at[k],
                piece_recv.at[k],
                {"dom": 2 * other + core},
            )
        )
    total = quarter_sum[pl.ds(level * piece, piece), :]
    for k in range(1, levels):
        copies[k - 1].wait_recv()
        total = total + piece_in[k].astype(high)
    sends += copies

    own_half = core * half
    own_quarter = own_half + grp * quarter
    own_piece = own_quarter + level * piece
    all_s[pl.ds(own_piece, piece), :] = total.astype(low)
    copies = []
    for k in range(1, levels):
        place = all_s.at[pl.ds(own_piece, piece), :]
        where = {"dom": 2 * lax.rem(level + k, levels) + core}
        copies.append(
            send(place, place, piece_send.at[levels + k], piece_recv.at[levels + k], where)
        )
    backs += [give_back(k) for k in range(1, peers) if k not in early]
    for copy in copies:
        copy.wait_recv()
    sends += copies
    copies = []
    for k in range(1, groups):
        place = all_s.at[pl.ds(own_quarter, quarter), :]
        where = {"grp": lax.rem(grp + k, groups)}
        copies.append(
            send(place, place, quarter_send.at[groups + k], quarter_recv.at[groups + k], where)
        )
    for copy in copies:
        copy.wait_recv()
    sends += copies
    place = all_s.at[pl.ds(own_half, half), :]
    copy = send(place, place, half_send.at[1], half_recv.at[1], twin)
    copy.wait_recv()
    sends.append(copy)
    loads[2].wait()
    for copy in backs:
        copy.wait()
    for copy in sends:
        copy.wait_send()
    sum_ref[...] = all_s[...]


def reduce_call(groups, peers, grads, slot_grad):
    rows = grads.shape[0]
    levels = peers // 2
    half, quarter, piece = rows // 2, rows // 2 // groups, rows // 2 // groups // levels
    dma = pltpu.SemaphoreType.DMA
    return pl.pallas_call(
        functools.partial(reduce_kernel, groups, peers),
        in_specs=[pl.BlockSpec(memory_space=pltpu.HBM)] * 2,
        out_specs=[
            pl.BlockSpec(memory_space=pltpu.VMEM),
            pl.BlockSpec(memory_space=pltpu.HBM),
        ],
        out_shape=[
            jax.ShapeDtypeStruct((rows, 128), low),
            jax.ShapeDtypeStruct(slot_grad.shape, low),
        ],
        scratch_shapes=[
            pltpu.VMEM((rows, 128), high),
            pltpu.VMEM((rows, 128), low),
            pltpu.VMEM((half, 128), low),
            pltpu.VMEM((half, 128), low),
            pltpu.VMEM((half, 128), high),
            pltpu.VMEM((groups, quarter, 128), low),
            pltpu.VMEM((groups, quarter, 128), low),
            pltpu.VMEM((quarter, 128), high),
            pltpu.VMEM((levels, piece, 128), low),
            pltpu.VMEM((levels, piece, 128), low),
            dma((peers,)),
            dma((peers,)),
            dma((2,)),
            dma((2,)),
            dma((2 * groups,)),
            dma((2 * groups,)),
            dma((2 * levels,)),
            dma((2 * levels,)),
            dma((3,)),
        ],
        compiler_params=pltpu.CompilerParams(
            collective_id=1, has_side_effects=True, vmem_limit_bytes=VMEM
        ),
        name="reduce",
    )(grads, slot_grad)


def adamw_step(master, moment_mean, moment_var, average, gradient, factor):
    clipped = gradient * factor
    mean_new = beta_one * moment_mean + (1.0 - beta_one) * clipped
    var_new = beta_two * moment_var + (1.0 - beta_two) * clipped * clipped
    mean_hat = mean_new / (1.0 - beta_one**STEP)
    var_hat = var_new / (1.0 - beta_two**STEP)
    updated = master - learn_rate * (
        mean_hat / (jnp.sqrt(var_hat) + adam_eps) + decay_rate * master
    )
    return (
        mean_new,
        var_new,
        updated,
        updated.astype(low),
        ema_keep * average + (1.0 - ema_keep) * updated,
    )


FIRST = (0, 384, 640, 1152, 1162)


def finish_kernel(unroll, asked_ref, *refs):
    sources, (norm_ref, *results), refs = refs[:19], refs[19:41], refs[41:]
    loaded, (rows_s, *staged, load_sem, store_sem) = refs[:19], refs[19:]
    summed_s, back_s, node_s = loaded[16:]
    loads = [
        pltpu.make_async_copy(source, place, load_sem.at[k])
        for k, (source, place) in enumerate(zip(sources, loaded))
    ]
    for load in [*loads[17:], loads[16], *loads[:16]]:
        load.start()
    loads[17].wait()
    rows_s[...] = back_s[...].astype(high)
    slots = asked_ref.shape[2]
    loads[18].wait()

    @pl.loop(0, rows_s.shape[0] // unroll)
    def _(group):
        base = group * unroll
        peer, first = lax.div(base, slots), lax.rem(base, slots)
        places = [pl.ds(asked_ref[peer, 0, first + k], 1) for k in range(unroll)]
        values = [
            node_s[place, :] + rows_s[pl.ds(base + k, 1), :] for k, place in enumerate(places)
        ]
        for place, value in zip(places, values):
            node_s[place, :] = value

    stores = [pltpu.make_async_copy(node_s, results[20], store_sem.at[20])]
    stores[0].start()
    for load in loads[:17]:
        load.wait()
    gradient = summed_s[...].astype(high)
    square = jnp.sum(gradient * gradient, axis=0, keepdims=True)
    grad_norm = jnp.sqrt(jnp.sum(square, axis=1, keepdims=True))
    norm_ref[0] = grad_norm[0, 0]
    factor = clip_level / jnp.maximum(grad_norm, clip_level)
    for k in range(4):
        values = [place[...] for place in loaded[4 * k : 4 * k + 4]]
        updates = adamw_step(*values, gradient[FIRST[k] : FIRST[k + 1]], factor)
        for place, value in enumerate(updates):
            place += 5 * k
            staged[place][...] = value
            store = pltpu.make_async_copy(staged[place], results[place], store_sem.at[place])
            store.start()
            stores.append(store)
    for store in stores:
        store.wait()


def finish_call(asked, part, back, summed, tensors):
    smem = pl.BlockSpec(memory_space=pltpu.SMEM)
    hbm = pl.BlockSpec(memory_space=pltpu.HBM)
    sources = [*tensors, summed, back, part]
    shapes = []
    for k in range(4):
        shape = tensors[4 * k].shape
        shapes += [jax.ShapeDtypeStruct(shape, kind) for kind in (high, high, high, low, high)]
    return pl.pallas_call(
        functools.partial(finish_kernel, 32),
        in_specs=[smem] + [hbm] * 19,
        out_specs=[smem] + [hbm] * 21,
        out_shape=[
            jax.ShapeDtypeStruct((1,), high),
            *shapes,
            jax.ShapeDtypeStruct(part.shape, high),
        ],
        scratch_shapes=[
            *[pltpu.VMEM(item.shape, item.dtype) for item in sources],
            pltpu.VMEM(back.shape, high),
            *[pltpu.VMEM(item.shape, item.dtype) for item in shapes],
            pltpu.SemaphoreType.DMA((19,)),
            pltpu.SemaphoreType.DMA((21,)),
        ],
        compiler_params=pltpu.CompilerParams(vmem_limit_bytes=VMEM),
        name="finish",
    )(asked, *sources)


def shards(
    node_in,
    edge_in,
    edge_slot,
    edge_receiver,
    edge_count,
    request,
    node_cot,
    edge_cot,
    *tensors,
):
    groups, peers = lax.axis_size("grp"), lax.axis_size("dom")
    slots = request.shape[2]
    z = Sizes(edge_in.shape[0], node_in.shape[0], peers * slots, groups * peers)
    slot_rows, asked = fetch_call(peers, request, node_in)
    node_out, edge_out, node_part, edge_grad, slot_grad, grads = layer_call(
        z,
        edge_count,
        edge_slot.reshape(-1, 128),
        edge_receiver.reshape(-1, 128),
        edge_in,
        edge_cot,
        node_in,
        node_cot,
        slot_rows.reshape(peers * slots, 128),
        tensors[::4],
    )
    summed, returned = reduce_call(groups, peers, grads, slot_grad.reshape(peers, slots, 128))
    flat = [tensor.reshape(-1, 128) for tensor in tensors]
    grad_norm, *results, node_grad = finish_call(
        asked, node_part, returned.reshape(peers * slots, 128), summed, flat
    )
    results = [value.reshape(tensors[k // 5 * 4].shape) for k, value in enumerate(results)]
    return (node_out, edge_out, node_grad, edge_grad, grad_norm.reshape(()), *results)


def solution(mesh):
    rows = P(("grp", "dom"), None)
    in_specs = (
        rows,
        rows,
        P(("grp", "dom")),
        P(("grp", "dom")),
        P(("grp", "dom")),
        P(("grp", "dom"), None, None),
        rows,
        rows,
    ) + (P(),) * 16
    out_specs = (rows,) * 4 + (P(),) * 21
    return jax.shard_map(shards, mesh=mesh, in_specs=in_specs, out_specs=out_specs, check_vma=False)
```
